32 devices in a mesh: dp: 4 (over y, core), point: 8 (over z, x).
Axes of the slice: x: 2, y: 2, z: 4, core: 2. Of those that a mesh axis runs over, the one named last changes fastest.
Arguments:
- inputs: float32 [4, 4096, 256], P('dp', 'point'), may hold values from -6 to 6
- cotangent: float32 [4, 4096, 256], P('dp', 'point'), may hold values from -6 to 6
- gain_one: float32 [256], replicated, may hold values from 0.5 to 1.5
- fx_weight: float32 [256, 256], replicated, may hold values from -0.375 to 0.375
- x_weight: float32 [256, 256], replicated, may hold values from -0.375 to 0.375
- slice_logit_weight: float32 [32, 64], replicated, may hold values from -2 to 2
- temper: float32 [8], replicated, may hold values from 0.5 to 2
- slice_query_matrix: float32 [32, 32], replicated, may hold values from -1.5 to 1.5
- slice_key_matrix: float32 [32, 32], replicated, may hold values from -1.5 to 1.5
- slice_value_matrix: float32 [32, 32], replicated, may hold values from -1 to 1
- out_weight: float32 [256, 256], replicated, may hold values from -0.375 to 0.375
- gain_two: float32 [256], replicated, may hold values from 0.5 to 1.5
- expand_weight: float32 [256, 256], replicated, may hold values from -0.375 to 0.375
- down_weight: float32 [256, 256], replicated, may hold values from -0.375 to 0.375
Outputs:
- input_grad: float32 [4, 4096, 256], P('dp', 'point')
- matrix_grads: float32 [5, 256, 256], replicated
- attention_gradient_set: float32 [3, 32, 32], replicated
- slice_grad: float32 [32, 64], replicated
- gain_grads: float32 [2, 256], replicated
The draws below stay inside these ranges and needn't reach their ends.
All inputs are finite; a program needn't handle non-finite values.
Results may differ from the reference program's by a relative error of at most 0.00016.
Values sent between devices are 32-bit elements; how exact they have to be, the bound alone decides.
No kernel may reach another device: no remote copies, remote signals or barrier semaphores. Data moves between devices by JAX's collectives and lax.ppermute only.
A program may use at most 64 MiB of HBM per device.

```python
import math
import jax
import jax.numpy as jnp
from jax import lax

C = 256
HEADS = 8
SLICES = 64
DH = 32
SAMPLES = 4
POINTS = 4096


def level_of(stream_key, extent, cuts, low, top_value):
    loudness = 1.0
    for position, blocks in cuts:
        heights = jax.random.uniform(jax.random.fold_in(jax.random.fold_in(stream_key, 6), position), (blocks,), jnp.float32, low / len(cuts), top_value / len(cuts))
        loudness = loudness * jnp.repeat(jnp.exp(heights), extent[position] // blocks).reshape((-1,) + (1,) * (len(extent) - 1 - position))
    return loudness


def scatter_about(own_key, extent, width, reach, pieces=(), dtype=jnp.bfloat16):
    values = width * jax.random.normal(own_key, extent, jnp.float32)
    if pieces:
        values = values * level_of(own_key, extent, pieces, -0.22, 0.18)
    return jnp.clip(values, -reach, reach).astype(dtype)


def setup_inputs(seed: int = 0) -> dict:
    splits = jax.random.split(jax.random.key(seed), 15)
    return {
        "inputs": scatter_about(splits[0], (SAMPLES, POINTS, C), 1.0, 6.0, ((0, 4), (1, 8)), jnp.float32),
        "cotangent": scatter_about(splits[1], (SAMPLES, POINTS, C), 1.0, 6.0, ((0, 4), (1, 8)), jnp.float32),
        "gain_one": jnp.clip(1.0 + 0.1 * jax.random.normal(splits[2], (C,), jnp.float32), 0.5, 1.5),
        "fx_weight": scatter_about(splits[3], (C, C), C ** -0.5, 0.375, (), jnp.float32),
        "x_weight": scatter_about(splits[4], (C, C), C ** -0.5, 0.375, (), jnp.float32),
        "slice_logit_weight": scatter_about(splits[5], (DH, SLICES), (DH // 4) ** -0.5, 2.0, (), jnp.float32),
        "temper": jnp.clip(jnp.exp(jax.random.uniform(splits[6], (HEADS,), jnp.float32, math.log(0.5), math.log(2.0))), 0.5, 2.0),
        "slice_query_matrix": scatter_about(splits[7], (DH, DH), (DH // 2) ** -0.5, 1.5, (), jnp.float32),
        "slice_key_matrix": scatter_about(splits[8], (DH, DH), (DH // 2) ** -0.5, 1.5, (), jnp.float32),
        "slice_value_matrix": scatter_about(splits[9], (DH, DH), DH ** -0.5, 1.0, (), jnp.float32),
        "out_weight": scatter_about(splits[10], (C, C), C ** -0.5, 0.375, (), jnp.float32),
        "gain_two": jnp.clip(1.0 + 0.1 * jax.random.normal(splits[11], (C,), jnp.float32), 0.5, 1.5),
        "expand_weight": scatter_about(splits[12], (C, C), C ** -0.5, 0.375, (), jnp.float32),
        "down_weight": scatter_about(splits[13], (C, C), C ** -0.5, 0.375, (), jnp.float32),
    }


def matmul(left, right):
    return jnp.dot(left, right, precision=lax.Precision.HIGHEST)

def normed(value_rows, gain):
    centre = value_rows - lax.optimization_barrier(jnp.mean(value_rows, axis=-1, keepdims=True))
    spread_back = lax.optimization_barrier(jnp.mean(centre * centre, axis=-1, keepdims=True))
    return centre * lax.rsqrt(spread_back + 1e-05) * gain

def front(rows, gain_one, fx_weight, x_weight, slice_logit_weight, temper):
    count = rows.shape[0]
    heads = temper.shape[0]
    normal = normed(rows, gain_one)
    feature_rows = matmul(normal, fx_weight).reshape(count, heads, -1)
    assign = matmul(normal, x_weight).reshape(count, heads, -1)
    slice_logit_rows = jnp.einsum('phd,dm->phm', assign, slice_logit_weight, precision=lax.Precision.HIGHEST)
    slice_membership_weights = jax.nn.softmax(slice_logit_rows / temper[None, :, None], axis=-1)
    total = lax.optimization_barrier(jnp.sum(slice_membership_weights, axis=0))
    summed_tokens = jnp.einsum('fkc,fkv->kcv', slice_membership_weights, feature_rows, precision=lax.Precision.HIGHEST)
    return (slice_membership_weights, summed_tokens, total)

def middle(summed_tokens, total, slice_query_matrix, slice_key_matrix, slice_value_matrix):
    slice_tokens = summed_tokens / (total[:, :, None] + 1e-05)
    query_rows = jnp.einsum('plq,qz->plz', slice_tokens, slice_query_matrix, precision=lax.Precision.HIGHEST)
    key_rows = jnp.einsum('plq,qz->plz', slice_tokens, slice_key_matrix, precision=lax.Precision.HIGHEST)
    value_rows = jnp.einsum('plq,qz->plz', slice_tokens, slice_value_matrix, precision=lax.Precision.HIGHEST)
    score_logits = jnp.einsum('aot,azt->aoz', query_rows, key_rows, precision=lax.Precision.HIGHEST)
    score_logits = score_logits * query_rows.shape[-1] ** (-0.5)
    attention_probs = jax.nn.softmax(score_logits, axis=-1)
    return jnp.einsum('ecg,ego->eco', attention_probs, value_rows, precision=lax.Precision.HIGHEST)

def back(rows, slice_membership_weights, slice_result_rows, out_weight, gain_two, expand_weight, down_weight):
    spread_back = jnp.einsum('lua,uaf->luf', slice_membership_weights, slice_result_rows, precision=lax.Precision.HIGHEST)
    spread_back = spread_back.reshape(rows.shape[0], -1)
    mixed = rows + matmul(spread_back, out_weight)
    hidden = jax.nn.gelu(matmul(normed(mixed, gain_two), expand_weight))
    return mixed + matmul(hidden, down_weight)

def reference(inputs, cotangent, gain_one, fx_weight, x_weight, slice_logit_weight, temper, slice_query_matrix, slice_key_matrix, slice_value_matrix, out_weight, gain_two, expand_weight, down_weight):

    def layer(rows, g_one, w_fx, w_x, w_slice, w_query, w_key, w_value, w_out, g_two, w_up, w_down):
        slice_membership_weights, summed_tokens, total = front(rows, g_one, w_fx, w_x, w_slice, temper)
        slice_result_rows = middle(summed_tokens, total, w_query, w_key, w_value)
        return back(rows, slice_membership_weights, slice_result_rows, w_out, g_two, w_up, w_down)
    params = (gain_one, fx_weight, x_weight, slice_logit_weight, slice_query_matrix, slice_key_matrix, slice_value_matrix, out_weight, gain_two, expand_weight, down_weight)
    grads_in = []
    sums = None
    for sample in range(SAMPLES):
        output, pullback = jax.vjp(layer, inputs[sample], *params)
        parts = pullback(cotangent[sample])
        grads_in.append(parts[0])
        if sums is None:
            sums = list(parts[1:])
        else:
            sums = [old + new for old, new in zip(sums, parts[1:])]
    factor = 1.0 / jnp.sqrt(jnp.float32(SAMPLES * POINTS))
    g_one, w_fx, w_x, w_slice, w_query, w_key, w_value, w_out, g_two, w_up, w_down = [item * factor for item in sums]
    matrix_grads = jnp.stack([w_fx, w_x, w_out, w_up, w_down])
    attention_gradient_set = jnp.stack([w_query, w_key, w_value])
    gain_grads = jnp.stack([g_one, g_two])
    return (jnp.stack(grads_in), matrix_grads, attention_gradient_set, w_slice, gain_grads)
```

```python
import functools
import math

import jax
import jax.numpy as jnp
from jax import lax
from jax.experimental import pallas as pl
from jax.experimental.pallas import tpu as pltpu
from jax.sharding import PartitionSpec as P

F32 = jnp.float32
BF16 = jnp.bfloat16
GROUP = 4
EPS = 1e-05
GELU_A = math.sqrt(2.0 / math.pi)
GELU_B = 0.044715
VMEM_LIMIT = 50 * 1024 * 1024


def split(value):
    high = value.astype(BF16)
    return high, (value - high.astype(F32)).astype(BF16)


def product(left, right, left_dim, right_dim):
    def one(a, b):
        return lax.dot_general(
            a, b, (((left_dim,), (right_dim,)), ((), ())), preferred_element_type=F32
        )

    return one(left[0], right[0]) + (one(left[0], right[1]) + one(left[1], right[0]))


def rows_of(pair, start, size):
    return pair[0][start : start + size], pair[1][start : start + size]


def stacked(first, second, axis=0):
    return tuple(jnp.concatenate([a, b], axis=axis) for a, b in zip(first, second))


def column(row):
    wide = jnp.broadcast_to(row, (8, row.shape[1]))
    return wide.T[:, 0:1]


def head_mask(head_size, slices):
    shape = (GROUP * head_size, GROUP * slices)
    row = lax.broadcasted_iota(jnp.int32, shape, 0) // head_size
    lane = lax.broadcasted_iota(jnp.int32, shape, 1) // slices
    return row == lane


def spread_blocks(value, mask):
    return jnp.where(mask, jnp.concatenate([value] * GROUP, axis=0), 0.0)


def fold_blocks(value, mask, head_size):
    kept = jnp.where(mask, value, 0.0)
    total = kept[:head_size]
    for i in range(1, GROUP):
        total = total + kept[i * head_size : (i + 1) * head_size]
    return total


def standardise(columns):
    centre = columns - jnp.mean(columns, axis=0, keepdims=True)
    rstd = lax.rsqrt(jnp.mean(centre * centre, axis=0, keepdims=True) + EPS)
    return centre * rstd, rstd


def standardise_pull(grad, hat, rstd):
    first = jnp.mean(grad, axis=0, keepdims=True)
    second = jnp.mean(grad * hat, axis=0, keepdims=True)
    return rstd * (grad - first - hat * second)


def front_kernel(
    x, gain, fx_weight, x_weight, logit_weight, temper,
    weight_h, weight_l, fx_h, fx_l, assign_h, assign_l, normal_h, normal_l, x_t, sums,
):
    head_size, slices = logit_weight.shape
    heads = temper.shape[0]
    points = x.shape[1]
    width = x.shape[2]
    columns = x[0].T
    x_t[...] = columns
    hat, _ = standardise(columns)
    normal = split(hat * column(gain[...]))
    normal_h[...], normal_l[...] = normal
    both = split(jnp.concatenate([fx_weight[...], x_weight[...]], axis=1))
    projected = split(product(both, normal, 0, 0))
    fx = rows_of(projected, 0, width)
    assign = rows_of(projected, width, width)
    fx_h[...], fx_l[...] = fx
    assign_h[...], assign_l[...] = assign
    mask = head_mask(head_size, slices)
    wide = jnp.concatenate([logit_weight[...]] * GROUP, axis=1)
    logit_blocks = split(spread_blocks(wide, mask))
    ones = jnp.ones((16, points), BF16)
    nums, dens = [], []
    for g in range(heads // GROUP):
        rows = GROUP * head_size
        logits = product(logit_blocks, rows_of(assign, g * rows, rows), 0, 0)
        parts = []
        for i in range(GROUP):
            scale = jnp.full((1, points), temper[g * GROUP + i], F32)
            scaled = logits[i * slices : (i + 1) * slices] / scale
            scaled = scaled - jnp.max(scaled, axis=0, keepdims=True)
            grown = jnp.exp(scaled)
            parts.append(grown / jnp.sum(grown, axis=0, keepdims=True))
        weights = split(jnp.concatenate(parts, axis=0))
        span = slice(g * GROUP * slices, (g + 1) * GROUP * slices)
        weight_h[span], weight_l[span] = weights
        num = product(rows_of(fx, g * rows, rows), weights, 1, 1)
        nums.append(fold_blocks(num, mask, head_size))
        nt = (((1,), (1,)), ((), ()))
        den = lax.dot_general(ones, weights[0], nt, preferred_element_type=F32)
        den = den + lax.dot_general(ones, weights[1], nt, preferred_element_type=F32)
        dens.append(den[:8])
    sums[0:head_size] = jnp.concatenate(nums, axis=1)
    sums[head_size : head_size + 8] = jnp.concatenate(dens, axis=1)


def back_kernel(
    factor,
    sums, x_t, weight_h, weight_l, cotangent, query, key, value, out_weight, gain,
    expand_weight, down_weight,
    out_sum, mixed_grad, spread_grad_h, spread_grad_l, middle, attn, early,
):
    head_size = query.shape[0]
    slices = attn.shape[0] // 2
    heads = weight_h.shape[0] // slices
    rows, lanes = GROUP * head_size, GROUP * slices
    denom = sums[head_size : head_size + 1] + EPS
    tokens = sums[0:head_size] / denom
    token_pair = split(tokens)
    maps = split(jnp.concatenate([query[...], key[...], value[...]], axis=1).T)
    qkv = product(maps, token_pair, 1, 0)
    qkv_pair = split(qkv)
    wide = 2 * slices
    same = (lax.broadcasted_iota(jnp.int32, (wide, wide), 0) // slices) == (
        lax.broadcasted_iota(jnp.int32, (wide, wide), 1) // slices
    )
    results = []
    for pair in range(heads // 2):
        span = slice(pair * wide, (pair + 1) * wide)
        q = tuple(a[0:head_size, span] for a in qkv_pair)
        k = tuple(a[head_size : 2 * head_size, span] for a in qkv_pair)
        v = tuple(a[2 * head_size :, span] for a in qkv_pair)
        scores = product(k, q, 0, 0) * head_size ** (-0.5)
        scores = jnp.where(same, scores, -1e30)
        scores = scores - jnp.max(scores, axis=0, keepdims=True)
        grown = jnp.where(same, jnp.exp(scores), 0.0)
        probs = grown / jnp.sum(grown, axis=0, keepdims=True)
        attn[:, span] = probs
        results.append(product(v, split(probs), 1, 0))
    result = jnp.concatenate(results, axis=1)
    middle[0:head_size] = tokens
    middle[head_size : 4 * head_size] = qkv
    middle[4 * head_size : 5 * head_size] = result
    mask = head_mask(head_size, slices)
    spread = []
    for g in range(heads // GROUP):
        span = slice(g * lanes, (g + 1) * lanes)
        blocks = split(spread_blocks(result[:, span], mask))
        spread.append(product(blocks, (weight_h[span], weight_l[span]), 1, 0))
    spread = split(jnp.concatenate(spread, axis=0))
    out_pair = split(out_weight[...])
    mixed = x_t[...] + product(out_pair, spread, 0, 0)
    hat, rstd = standardise(mixed)
    gain_column = column(gain[...])
    normal = split(hat * gain_column)
    expand = split(expand_weight[...])
    before = product(expand, normal, 0, 0)
    square = before * before
    bent = jnp.tanh(GELU_A * (before + GELU_B * before * square))
    half = 0.5 * (1.0 + bent)
    hidden = split(before * half)
    slope = half + 0.5 * before * (1.0 - bent * bent) * (GELU_A * (1.0 + 3.0 * GELU_B * square))
    cot = cotangent[0]
    cot_t = cot.T
    hidden_grad = product(split(down_weight[...]), split(cot_t), 1, 0)
    before_grad = split(hidden_grad * slope)
    normal_grad = product(expand, before_grad, 1, 0)
    grad = cot_t + standardise_pull(normal_grad * gain_column, hat, rstd)
    mixed_grad[...] = grad
    grad_pair = split(grad)
    spread_grad = split(product(out_pair, grad_pair, 1, 0))
    spread_grad_h[...], spread_grad_l[...] = spread_grad
    sums_out = []
    for g in range(heads // GROUP):
        span = slice(g * lanes, (g + 1) * lanes)
        full = product(
            rows_of(spread_grad, g * rows, rows), (weight_h[span], weight_l[span]), 1, 1
        )
        sums_out.append(fold_blocks(full, mask, head_size))
    out_sum[...] = jnp.concatenate(sums_out, axis=1)
    width = out_weight.shape[0]
    early[0:width] = product(spread, grad_pair, 1, 1) * factor
    early[width : 2 * width] = product(normal, before_grad, 1, 1) * factor
    early[2 * width : 3 * width] = product(hidden, split(cot), 1, 0) * factor
    ones = jnp.ones((16, hat.shape[1]), BF16)
    nt = (((1,), (1,)), ((), ()))
    gains = split(normal_grad * hat)
    gain_row = lax.dot_general(ones, gains[0], nt, preferred_element_type=F32)
    gain_row = gain_row + lax.dot_general(ones, gains[1], nt, preferred_element_type=F32)
    early[3 * width :] = jnp.zeros((early.shape[0] - 3 * width, width), F32)
    early[3 * width : 3 * width + 8] = gain_row[:8] * factor


def end_kernel(
    factor, middle_factor,
    out_sum, sums, middle, attn, weight_h, weight_l, fx_h, fx_l, assign_h, assign_l, normal_h,
    normal_l, x_t, mixed_grad, spread_grad_h, spread_grad_l, query, key, value, fx_weight,
    x_weight, logit_weight, temper, gain,
    x_grad, late,
):
    head_size, slices = logit_weight.shape
    heads = temper.shape[0]
    rows, lanes = GROUP * head_size, GROUP * slices
    points = x_t.shape[1]
    width = x_t.shape[0]
    tokens = middle[0:head_size]
    qkv_pair = split(middle[head_size : 4 * head_size])
    result = middle[4 * head_size : 5 * head_size]
    result_grad = split(out_sum[...])
    wide = 2 * slices
    parts = []
    for pair in range(heads // 2):
        span = slice(pair * wide, (pair + 1) * wide)
        q = tuple(a[0:head_size, span] for a in qkv_pair)
        k = tuple(a[head_size : 2 * head_size, span] for a in qkv_pair)
        v = tuple(a[2 * head_size :, span] for a in qkv_pair)
        probs = attn[:, span]
        grad = tuple(a[:, span] for a in result_grad)
        value_grad = product(grad, split(probs), 1, 1)
        probs_grad = product(v, grad, 0, 0)
        weighted = probs * probs_grad
        total = jnp.sum(weighted, axis=0, keepdims=True)
        score_grad = split((weighted - probs * total) * head_size ** (-0.5))
        query_grad = product(k, score_grad, 1, 0)
        key_grad = product(q, score_grad, 1, 1)
        parts.append(jnp.concatenate([query_grad, key_grad, value_grad], axis=0))
    qkv_grad = split(jnp.concatenate(parts, axis=1))
    maps = split(jnp.concatenate([query[...], key[...], value[...]], axis=1))
    map_grad = product(split(tokens), qkv_grad, 1, 1)
    denom = sums[head_size : head_size + 1] + EPS
    num_grad = product(maps, qkv_grad, 1, 0) / denom
    den_grad = column(-jnp.sum(num_grad * tokens, axis=0, keepdims=True))
    mask = head_mask(head_size, slices)
    logit_wide = jnp.concatenate([logit_weight[...]] * GROUP, axis=1)
    logit_blocks = split(spread_blocks(logit_wide, mask))
    fx_grads, assign_grads = [], []
    logit_grad = jnp.zeros((head_size, lanes), F32)
    for g in range(heads // GROUP):
        span = slice(g * lanes, (g + 1) * lanes)
        piece = slice(g * rows, (g + 1) * rows)
        num_blocks = split(spread_blocks(num_grad[:, span], mask))
        result_blocks = split(spread_blocks(result[:, span], mask))
        weights = (weight_h[span], weight_l[span])
        fx_grads.append(product(num_blocks, weights, 1, 0))
        weight_grad = product(
            stacked(num_blocks, result_blocks),
            stacked(
                (fx_h[piece], fx_l[piece]), (spread_grad_h[piece], spread_grad_l[piece])
            ),
            0,
            0,
        )
        weight_grad = weight_grad + den_grad[span]
        grads = []
        for i in range(GROUP):
            block = slice(i * slices, (i + 1) * slices)
            scale = jnp.full((1, points), temper[g * GROUP + i], F32)
            w = weights[0][block].astype(F32) + weights[1][block].astype(F32)
            weighted = w * weight_grad[block]
            total = jnp.sum(weighted, axis=0, keepdims=True)
            grads.append((weighted - w * total) / scale)
        grads = split(jnp.concatenate(grads, axis=0))
        assign_grads.append(product(logit_blocks, grads, 1, 0))
        full = product((assign_h[piece], assign_l[piece]), grads, 1, 1)
        logit_grad = logit_grad + fold_blocks(full, mask, head_size)
    both_grad = split(jnp.concatenate(fx_grads + assign_grads, axis=0))
    both = split(jnp.concatenate([fx_weight[...], x_weight[...]], axis=1))
    normal_grad = product(both, both_grad, 1, 0)
    hat, rstd = standardise(x_t[...])
    columns = mixed_grad[...] + standardise_pull(normal_grad * column(gain[...]), hat, rstd)
    x_grad[0] = columns.T
    normal = (normal_h[...], normal_l[...])
    matrix = product(normal, both_grad, 1, 1) * factor
    late[0:width] = matrix[:, :width]
    late[width : 2 * width] = matrix[:, width:]
    logit_grad = logit_grad[:, : 2 * slices] + logit_grad[:, 2 * slices :]
    logit_grad = logit_grad[:, :slices] + logit_grad[:, slices:]
    base = 2 * width
    late[base:] = jnp.zeros((late.shape[0] - base, width), F32)
    late[base : base + head_size, 0 : 3 * head_size] = map_grad * middle_factor
    late[base : base + head_size, 128 : 128 + slices] = logit_grad * factor
    ones = jnp.ones((16, points), BF16)
    nt = (((1,), (1,)), ((), ()))
    gains = split(normal_grad * hat)
    gain_row = lax.dot_general(ones, gains[0], nt, preferred_element_type=F32)
    gain_row = gain_row + lax.dot_general(ones, gains[1], nt, preferred_element_type=F32)
    late[base + head_size : base + head_size + 8] = gain_row[:8] * factor


VMEM = pl.BlockSpec(memory_space=pltpu.VMEM)
SMEM = pl.BlockSpec(memory_space=pltpu.SMEM)


def call(body, name, in_specs, out_shape, args, flops):
    return pl.pallas_call(
        body,
        name=name,
        in_specs=in_specs,
        out_specs=[VMEM] * len(out_shape),
        out_shape=out_shape,
        compiler_params=pltpu.CompilerParams(vmem_limit_bytes=VMEM_LIMIT),
        cost_estimate=pl.CostEstimate(flops=flops, bytes_accessed=4 << 20, transcendentals=0),
    )(*args)


def swap(value, moves, sizes):
    dp, point = sizes
    pairs = []
    for d in range(dp):
        for p in range(point):
            other_d, other_p = moves(d, p)
            pairs.append((d * point + p, other_d * point + other_p))
    return lax.ppermute(value, ("dp", "point"), pairs)


def flip(axis, bit):
    if axis == 0:
        return lambda d, p: (d ^ bit, p)
    return lambda d, p: (d, p ^ bit)


def bits(count):
    return [1 << i for i in range(count.bit_length() - 1)]


def power(count):
    return count & (count - 1) == 0


def sum_points(value, sizes):
    if not power(sizes[1]):
        return lax.psum(value, "point")
    for bit in bits(sizes[1]):
        value = value + swap(value, flip(1, bit), sizes)
    return value


def halve(value, upper):
    half = value.shape[0] // 2
    mine = lax.dynamic_slice_in_dim(value, upper * half, half, 0)
    other = lax.dynamic_slice_in_dim(value, (1 - upper) * half, half, 0)
    return mine, other


def join(mine, other, upper):
    low = jnp.where(upper == 0, mine, other)
    high = jnp.where(upper == 0, other, mine)
    return jnp.concatenate([low, high], axis=0)


def sum_all(value, sizes):
    dp, point = sizes
    if not (power(dp) and power(point)) or dp < 2 or point < 2:
        return lax.psum(value, ("dp", "point"))
    d, p = lax.axis_index("dp"), lax.axis_index("point")
    steps = [(1, 1)] + [(0, b) for b in bits(dp)[1:]] + [(1, b) for b in bits(point)[1:]]
    turn = len(steps) // 2
    orders = [steps, steps[turn:] + steps[:turn]]

    def move(i):
        choices = [flip(*order[i]) for order in orders]
        return lambda d, p: choices[d & 1](d, p)

    core = d & 1
    mine, other = halve(value, core)
    value = mine + swap(other, flip(0, 1), sizes)
    axis_bits = [order[0] for order in orders]
    places = [((d if a == 0 else p) // b) & 1 for a, b in axis_bits]
    upper = jnp.where(core == 0, places[0], places[1])
    mine, other = halve(value, upper)
    value = mine + swap(other, move(0), sizes)
    for i in range(1, len(steps)):
        value = value + swap(value, move(i), sizes)
    value = join(value, swap(value, move(0), sizes), upper)
    return join(value, swap(value, flip(0, 1), sizes), core)


def shards(
    sizes,
    inputs, cotangent, gain_one, fx_weight, x_weight, slice_logit_weight, temper,
    slice_query_matrix, slice_key_matrix, slice_value_matrix, out_weight, gain_two,
    expand_weight, down_weight,
):
    points, width = inputs.shape[1:]
    head_size, slices = slice_logit_weight.shape
    heads = temper.shape[0]
    total = heads * slices
    gain_one, gain_two = gain_one[None], gain_two[None]
    factor = 1.0 / math.sqrt(points * sizes[0] * sizes[1])

    def shape(*dims, dtype=F32):
        return jax.ShapeDtypeStruct(dims, dtype)

    half = functools.partial(shape, dtype=BF16)
    pair = [half(width, points)] * 2
    dense = 6 * points * width * width
    (w_h, w_l, fx_h, fx_l, as_h, as_l, n_h, n_l, x_t, sums) = call(
        front_kernel, "front", [VMEM] * 5 + [SMEM],
        [half(total, points)] * 2 + pair * 3 + [shape(width, points), shape(head_size + 8, total)],
        (inputs, gain_one, fx_weight, x_weight, slice_logit_weight, temper),
        4 * dense,
    )
    sums = sum_points(sums, sizes)
    out_sum, mixed_grad, sg_h, sg_l, middle, attn, early = call(
        functools.partial(back_kernel, factor), "back", [VMEM] * 12,
        [shape(head_size, total), shape(width, points)] + pair
        + [shape(5 * head_size, total), shape(2 * slices, total), shape(3 * width + 32, width)],
        (sums, x_t, w_h, w_l, cotangent, slice_query_matrix, slice_key_matrix,
         slice_value_matrix, out_weight, gain_two, expand_weight, down_weight),
        10 * dense,
    )
    out_sum = sum_points(out_sum, sizes)
    input_grad, late = call(
        functools.partial(end_kernel, factor, factor / sizes[1]), "end",
        [VMEM] * 22 + [SMEM] + [VMEM],
        [shape(1, points, width), shape(2 * width + head_size + 32, width)],
        (out_sum, sums, middle, attn, w_h, w_l, fx_h, fx_l, as_h, as_l, n_h, n_l, x_t,
         mixed_grad, sg_h, sg_l, slice_query_matrix, slice_key_matrix, slice_value_matrix,
         fx_weight, x_weight, slice_logit_weight, temper, gain_one),
        10 * dense,
    )
    early = sum_all(early, sizes)
    late = sum_all(late, sizes)
    matrix_grads = jnp.concatenate([late[: 2 * width], early[: 3 * width]], axis=0)
    small = late[2 * width : 2 * width + head_size]
    maps = jnp.stack([small[:, i * head_size : (i + 1) * head_size] for i in range(3)])
    gains = jnp.stack([late[2 * width + head_size], early[3 * width]])
    return (
        input_grad,
        matrix_grads.reshape(5, width, width),
        maps,
        small[:, 128 : 128 + slices],
        gains,
    )


def solution(mesh):
    sizes = (mesh.shape["dp"], mesh.shape["point"])
    placed = (P("dp", "point", None),) * 2 + (P(),) * 12
    return jax.shard_map(
        functools.partial(shards, sizes),
        mesh=mesh,
        in_specs=placed,
        out_specs=(P("dp", "point", None), P(), P(), P(), P()),
        check_vma=False,
    )
```

```python
import functools
import math

import jax
import jax.numpy as jnp
from jax import lax
from jax.experimental import pallas as pl
from jax.experimental.pallas import tpu as pltpu
from jax.sharding import PartitionSpec as P

F32 = jnp.float32
BF16 = jnp.bfloat16
GROUP = 4
EPS = 1e-05
GELU_A = math.sqrt(2.0 / math.pi)
GELU_B = 0.044715
VMEM_LIMIT = 16 * 1024 * 1024


def split(value):
    high = value.astype(BF16)
    return high, (value - high.astype(F32)).astype(BF16)


def product(left, right, left_dim, right_dim):
    def one(a, b):
        return lax.dot_general(
            a, b, (((left_dim,), (right_dim,)), ((), ())), preferred_element_type=F32
        )

    return one(left[0], right[0]) + (one(left[0], right[1]) + one(left[1], right[0]))


def rows_of(pair, start, size):
    return pair[0][start : start + size], pair[1][start : start + size]


def stacked(first, second, axis=0):
    return tuple(jnp.concatenate([a, b], axis=axis) for a, b in zip(first, second))


def column(row):
    wide = jnp.broadcast_to(row, (8, row.shape[1]))
    return wide.T[:, 0:1]


def head_mask(head_size, slices):
    shape = (GROUP * head_size, GROUP * slices)
    row = lax.broadcasted_iota(jnp.int32, shape, 0) // head_size
    lane = lax.broadcasted_iota(jnp.int32, shape, 1) // slices
    return row == lane


def spread_blocks(value, mask):
    return jnp.where(mask, jnp.concatenate([value] * GROUP, axis=0), 0.0)


def fold_blocks(value, mask, head_size):
    kept = jnp.where(mask, value, 0.0)
    total = kept[:head_size]
    for i in range(1, GROUP):
        total = total + kept[i * head_size : (i + 1) * head_size]
    return total


def standardise(columns):
    centre = columns - jnp.mean(columns, axis=0, keepdims=True)
    rstd = lax.rsqrt(jnp.mean(centre * centre, axis=0, keepdims=True) + EPS)
    return centre * rstd, rstd


def standardise_pull(grad, hat, rstd):
    first = jnp.mean(grad, axis=0, keepdims=True)
    second = jnp.mean(grad * hat, axis=0, keepdims=True)
    return rstd * (grad - first - hat * second)


def row_total(left, right):
    value = split(left * right)
    ones = jnp.ones((16, left.shape[1]), BF16)
    nt = (((1,), (1,)), ((), ()))
    total = lax.dot_general(ones, value[0], nt, preferred_element_type=F32)
    total = total + lax.dot_general(ones, value[1], nt, preferred_element_type=F32)
    return total[0:1]


def fetch(sources, targets, sems):
    copies = [
        pltpu.make_async_copy(source, target, sems.at[i])
        for i, (source, target) in enumerate(zip(sources, targets))
    ]
    for copy in copies:
        copy.start()
    return copies


def front_kernel(
    x_hbm, gain_hbm, fx_hbm, xw_hbm, logit_hbm, temper_hbm,
    weight_h, weight_l, fx_h, fx_l, assign_h, assign_l, hat_h, hat_l, x_t, both_h, both_l, sums,
    x, gain, fx_weight, x_weight, logit_weight, temper, sems,
):
    sources = (x_hbm, gain_hbm, fx_hbm, xw_hbm, logit_hbm, temper_hbm)
    targets = (x, gain, fx_weight, x_weight, logit_weight, temper)
    copies = fetch(sources, targets, sems)
    head_size, slices = logit_weight.shape
    heads = temper.shape[0]
    points = x.shape[1]
    width = x.shape[2]
    copies[0].wait()
    columns = x[0].T
    x_t[...] = columns
    hat, _ = standardise(columns)
    hat = split(hat)
    hat_h[...], hat_l[...] = hat
    for copy in copies[1:]:
        copy.wait()
    both = jnp.concatenate([fx_weight[...], x_weight[...]], axis=1)
    both = split(both * column(gain[...]))
    both_h[...], both_l[...] = both
    projected = split(product(both, hat, 0, 0))
    fx = rows_of(projected, 0, width)
    assign = rows_of(projected, width, width)
    fx_h[...], fx_l[...] = fx
    assign_h[...], assign_l[...] = assign
    mask = head_mask(head_size, slices)
    wide = jnp.concatenate([logit_weight[...]] * GROUP, axis=1)
    logit_blocks = split(spread_blocks(wide, mask))
    ones = jnp.ones((16, points), BF16)
    nums, dens = [], []
    for g in range(heads // GROUP):
        rows = GROUP * head_size
        logits = product(logit_blocks, rows_of(assign, g * rows, rows), 0, 0)
        parts = []
        for i in range(GROUP):
            scale = jnp.full((1, points), temper[g * GROUP + i], F32)
            scaled = logits[i * slices : (i + 1) * slices] / scale
            scaled = scaled - jnp.max(scaled, axis=0, keepdims=True)
            grown = jnp.exp(scaled)
            parts.append(grown / jnp.sum(grown, axis=0, keepdims=True))
        weights = split(jnp.concatenate(parts, axis=0))
        span = slice(g * GROUP * slices, (g + 1) * GROUP * slices)
        weight_h[span], weight_l[span] = weights
        num = product(rows_of(fx, g * rows, rows), weights, 1, 1)
        nums.append(fold_blocks(num, mask, head_size))
        nt = (((1,), (1,)), ((), ()))
        den = lax.dot_general(ones, weights[0], nt, preferred_element_type=F32)
        den = den + lax.dot_general(ones, weights[1], nt, preferred_element_type=F32)
        dens.append(den[:8])
    sums[0:head_size] = jnp.concatenate(nums, axis=1)
    sums[head_size : head_size + 8] = jnp.concatenate(dens, axis=1)


def ready_kernel(
    cotangent, out_weight, gain, expand_weight, down_weight, query, key, value,
    cot_t, hidden_grad, out_t_h, out_t_l, expand_h, expand_l, expand_t_h, expand_t_l, maps_h,
    maps_l,
):
    columns = cotangent[0].T
    cot_t[...] = columns
    hidden_grad[...] = product(split(down_weight[...]), split(columns), 1, 0)
    out_t_h[...], out_t_l[...] = split(out_weight[...].T)
    expand = expand_weight[...] * column(gain[...])
    expand_h[...], expand_l[...] = split(expand)
    expand_t_h[...], expand_t_l[...] = split(expand.T)
    maps = jnp.concatenate([query[...], key[...], value[...]], axis=1)
    maps_h[...], maps_l[...] = split(maps.T)


def back_kernel(
    sums, x_t, weight_h, weight_l, cot_t, hidden_grad, out_weight, out_t_h, out_t_l, expand_h,
    expand_l, expand_t_h, expand_t_l, maps_h, maps_l,
    out_sum, mixed_grad, spread_grad_h, spread_grad_l, middle, attn, spread_h, spread_l, hat_h,
    hat_l, before_grad_h, before_grad_l, hidden_h, hidden_l,
):
    head_size = maps_h.shape[1]
    slices = attn.shape[0] // 2
    heads = weight_h.shape[0] // slices
    rows, lanes = GROUP * head_size, GROUP * slices
    denom = sums[head_size : head_size + 1] + EPS
    tokens = sums[0:head_size] / denom
    qkv = product((maps_h[...], maps_l[...]), split(tokens), 1, 0)
    qkv_pair = split(qkv)
    wide = 2 * slices
    same = (lax.broadcasted_iota(jnp.int32, (wide, wide), 0) // slices) == (
        lax.broadcasted_iota(jnp.int32, (wide, wide), 1) // slices
    )
    results = []
    for pair in range(heads // 2):
        span = slice(pair * wide, (pair + 1) * wide)
        q = tuple(a[0:head_size, span] for a in qkv_pair)
        k = tuple(a[head_size : 2 * head_size, span] for a in qkv_pair)
        v = tuple(a[2 * head_size :, span] for a in qkv_pair)
        scores = product(k, q, 0, 0) * head_size ** (-0.5)
        scores = jnp.where(same, scores, -1e30)
        scores = scores - jnp.max(scores, axis=0, keepdims=True)
        grown = jnp.where(same, jnp.exp(scores), 0.0)
        probs = grown / jnp.sum(grown, axis=0, keepdims=True)
        attn[:, span] = probs
        results.append(product(v, split(probs), 1, 0))
    result = jnp.concatenate(results, axis=1)
    middle[0:head_size] = tokens
    middle[head_size : 4 * head_size] = qkv
    middle[4 * head_size : 5 * head_size] = result
    mask = head_mask(head_size, slices)
    spread = []
    for g in range(heads // GROUP):
        span = slice(g * lanes, (g + 1) * lanes)
        blocks = split(spread_blocks(result[:, span], mask))
        spread.append(product(blocks, (weight_h[span], weight_l[span]), 1, 0))
    spread = split(jnp.concatenate(spread, axis=0))
    spread_h[...], spread_l[...] = spread
    mixed = x_t[...] + product((out_t_h[...], out_t_l[...]), spread, 1, 0)
    hat, rstd = standardise(mixed)
    hat_pair = split(hat)
    hat_h[...], hat_l[...] = hat_pair
    before = product((expand_t_h[...], expand_t_l[...]), hat_pair, 1, 0)
    square = before * before
    bent = jnp.tanh(GELU_A * (before + GELU_B * before * square))
    half = 0.5 * (1.0 + bent)
    hidden_h[...], hidden_l[...] = split(before * half)
    slope = half + 0.5 * before * (1.0 - bent * bent) * (GELU_A * (1.0 + 3.0 * GELU_B * square))
    before_grad = split(hidden_grad[...] * slope)
    before_grad_h[...], before_grad_l[...] = before_grad
    hat_grad = product((expand_h[...], expand_l[...]), before_grad, 1, 0)
    grad = cot_t[...] + standardise_pull(hat_grad, hat, rstd)
    mixed_grad[...] = grad
    spread_grad = split(product(split(out_weight[...]), split(grad), 1, 0))
    spread_grad_h[...], spread_grad_l[...] = spread_grad
    sums_out = []
    for g in range(heads // GROUP):
        span = slice(g * lanes, (g + 1) * lanes)
        full = product(
            rows_of(spread_grad, g * rows, rows), (weight_h[span], weight_l[span]), 1, 1
        )
        sums_out.append(fold_blocks(full, mask, head_size))
    out_sum[...] = jnp.concatenate(sums_out, axis=1)


def early_kernel(
    factor,
    spread_h, spread_l, mixed_grad, hat_h, hat_l, before_grad_h, before_grad_l, hidden_h,
    hidden_l, cotangent,
    early,
):
    width = mixed_grad.shape[0]
    spread = (spread_h[...], spread_l[...])
    early[0:width] = product(spread, split(mixed_grad[...]), 1, 1) * factor
    hat = (hat_h[...], hat_l[...])
    before_grad = (before_grad_h[...], before_grad_l[...])
    early[width : 2 * width] = product(hat, before_grad, 1, 1) * factor
    hidden = (hidden_h[...], hidden_l[...])
    early[2 * width :] = product(hidden, split(cotangent[0]), 1, 0) * factor


def end_kernel(
    factor, middle_factor,
    out_sum, sums, middle, attn, weight_h, weight_l, fx_h, fx_l, assign_h, assign_l, hat_h,
    hat_l, spread_grad_h, spread_grad_l, query, key, value, logit_weight, temper,
    late, both_grad_h, both_grad_l,
):
    head_size, slices = logit_weight.shape
    heads = temper.shape[0]
    rows, lanes = GROUP * head_size, GROUP * slices
    width, points = hat_h.shape
    tokens = middle[0:head_size]
    qkv_pair = split(middle[head_size : 4 * head_size])
    result = middle[4 * head_size : 5 * head_size]
    result_grad = split(out_sum[...])
    wide = 2 * slices
    parts = []
    for pair in range(heads // 2):
        span = slice(pair * wide, (pair + 1) * wide)
        q = tuple(a[0:head_size, span] for a in qkv_pair)
        k = tuple(a[head_size : 2 * head_size, span] for a in qkv_pair)
        v = tuple(a[2 * head_size :, span] for a in qkv_pair)
        probs = attn[:, span]
        grad = tuple(a[:, span] for a in result_grad)
        value_grad = product(grad, split(probs), 1, 1)
        probs_grad = product(v, grad, 0, 0)
        weighted = probs * probs_grad
        total = jnp.sum(weighted, axis=0, keepdims=True)
        score_grad = split((weighted - probs * total) * head_size ** (-0.5))
        query_grad = product(k, score_grad, 1, 0)
        key_grad = product(q, score_grad, 1, 1)
        parts.append(jnp.concatenate([query_grad, key_grad, value_grad], axis=0))
    qkv_grad = split(jnp.concatenate(parts, axis=1))
    maps = split(jnp.concatenate([query[...], key[...], value[...]], axis=1))
    map_grad = product(split(tokens), qkv_grad, 1, 1)
    denom = sums[head_size : head_size + 1] + EPS
    num_grad = product(maps, qkv_grad, 1, 0) / denom
    den_grad = column(-jnp.sum(num_grad * tokens, axis=0, keepdims=True))
    mask = head_mask(head_size, slices)
    logit_wide = jnp.concatenate([logit_weight[...]] * GROUP, axis=1)
    logit_blocks = split(spread_blocks(logit_wide, mask))
    fx_grads, assign_grads = [], []
    logit_grad = jnp.zeros((head_size, lanes), F32)
    for g in range(heads // GROUP):
        span = slice(g * lanes, (g + 1) * lanes)
        piece = slice(g * rows, (g + 1) * rows)
        num_blocks = split(spread_blocks(num_grad[:, span], mask))
        result_blocks = split(spread_blocks(result[:, span], mask))
        weights = (weight_h[span], weight_l[span])
        fx_grads.append(product(num_blocks, weights, 1, 0))
        weight_grad = product(
            stacked(num_blocks, result_blocks),
            stacked(
                (fx_h[piece], fx_l[piece]), (spread_grad_h[piece], spread_grad_l[piece])
            ),
            0,
            0,
        )
        weight_grad = weight_grad + den_grad[span]
        grads = []
        for i in range(GROUP):
            block = slice(i * slices, (i + 1) * slices)
            scale = jnp.full((1, points), temper[g * GROUP + i], F32)
            w = weights[0][block].astype(F32) + weights[1][block].astype(F32)
            weighted = w * weight_grad[block]
            total = jnp.sum(weighted, axis=0, keepdims=True)
            grads.append((weighted - w * total) / scale)
        grads = split(jnp.concatenate(grads, axis=0))
        assign_grads.append(product(logit_blocks, grads, 1, 0))
        full = product((assign_h[piece], assign_l[piece]), grads, 1, 1)
        logit_grad = logit_grad + fold_blocks(full, mask, head_size)
    both_grad = split(jnp.concatenate(fx_grads + assign_grads, axis=0))
    both_grad_h[...], both_grad_l[...] = both_grad
    matrix = product((hat_h[...], hat_l[...]), both_grad, 1, 1) * factor
    late[0:width] = matrix[:, :width]
    late[width : 2 * width] = matrix[:, width:]
    logit_grad = logit_grad[:, : 2 * slices] + logit_grad[:, 2 * slices :]
    logit_grad = logit_grad[:, :slices] + logit_grad[:, slices:]
    base = 2 * width
    late[base:] = jnp.zeros((late.shape[0] - base, width), F32)
    late[base : base + head_size, 0 : 3 * head_size] = map_grad * middle_factor
    late[base : base + head_size, 128 : 128 + slices] = logit_grad * factor


def rows_kernel(both_h, both_l, both_grad_h, both_grad_l, x_t, mixed_grad, x_grad):
    both = (both_h[...], both_l[...])
    hat_grad = product(both, (both_grad_h[...], both_grad_l[...]), 1, 0)
    hat, rstd = standardise(x_t[...])
    x_grad[0] = (mixed_grad[...] + standardise_pull(hat_grad, hat, rstd)).T


def early_out_kernel(
    early, gain, expand_weight,
    matrices, gain_row, scaled, sems,
):
    width = gain.shape[1]
    copies = [
        pltpu.make_async_copy(early.at[0:width], matrices.at[2], sems.at[0]),
        pltpu.make_async_copy(early.at[2 * width : 3 * width], matrices.at[4], sems.at[1]),
        pltpu.make_async_copy(scaled, matrices.at[3], sems.at[2]),
    ]
    copies[0].start()
    copies[1].start()
    grad = early[width : 2 * width]
    scaled[...] = grad * column(gain[...])
    copies[2].start()
    gain_row[...] = row_total(grad, expand_weight[...])
    for copy in copies:
        copy.wait()


def late_out_kernel(
    late, gain, fx_weight, x_weight, gain_row, given,
    matrices, maps, logit, gains, scaled, sems,
):
    width = gain.shape[1]
    head_size, slices = logit.shape
    gain_column = column(gain[...])
    copies = []
    total = jnp.zeros((1, width), F32)
    for i, weight in enumerate((fx_weight, x_weight)):
        grad = late[i * width : (i + 1) * width]
        scaled[i] = grad * gain_column
        copies.append(pltpu.make_async_copy(scaled.at[i], matrices.at[i], sems.at[i]))
        copies[i].start()
        total = total + row_total(grad, weight[...])
    base = 2 * width
    for i in range(3):
        maps[i] = late[base : base + head_size, i * head_size : (i + 1) * head_size]
    logit[...] = late[base : base + head_size, 128 : 128 + slices]
    gains[...] = jnp.concatenate([total, gain_row[...]], axis=0)
    for copy in copies:
        copy.wait()


VMEM = pl.BlockSpec(memory_space=pltpu.VMEM)
SMEM = pl.BlockSpec(memory_space=pltpu.SMEM)


HBM = pl.BlockSpec(memory_space=pltpu.HBM)


def call(body, name, in_specs, out_specs, out_shape, args, flops, scratch=(), aliases=None):
    return pl.pallas_call(
        body,
        name=name,
        in_specs=in_specs,
        out_specs=out_specs,
        out_shape=out_shape,
        scratch_shapes=scratch,
        input_output_aliases=aliases or {},
        compiler_params=pltpu.CompilerParams(vmem_limit_bytes=VMEM_LIMIT),
        cost_estimate=pl.CostEstimate(flops=flops, bytes_accessed=1 << 20, transcendentals=0),
    )(*args)


def swap(value, moves, sizes):
    dp, point = sizes
    pairs = []
    for d in range(dp):
        for p in range(point):
            other_d, other_p = moves(d, p)
            pairs.append((d * point + p, other_d * point + other_p))
    return lax.ppermute(value, ("dp", "point"), pairs)


def flip(axis, bit):
    if axis == 0:
        return lambda d, p: (d ^ bit, p)
    return lambda d, p: (d, p ^ bit)


def bits(count):
    return [1 << i for i in range(count.bit_length() - 1)]


def power(count):
    return count & (count - 1) == 0


def tie(*values):
    return lax.optimization_barrier(values)


def halve(value, upper):
    half = value.shape[0] // 2
    mine = lax.dynamic_slice_in_dim(value, upper * half, half, 0)
    other = lax.dynamic_slice_in_dim(value, (1 - upper) * half, half, 0)
    return mine, other


def join(mine, other, upper):
    low = jnp.where(upper == 0, mine, other)
    high = jnp.where(upper == 0, other, mine)
    return jnp.concatenate([low, high], axis=0)


def point_steps(sizes):
    if not power(sizes[1]):
        return [lambda value: lax.psum(value, "point")]

    def step(bit):
        return lambda value: value + swap(value, flip(1, bit), sizes)

    return [step(bit) for bit in bits(sizes[1])]


def all_steps(sizes):
    dp, point = sizes
    if not (power(dp) and power(point)) or dp < 2 or point < 2:
        return [lambda value: lax.psum(value, ("dp", "point"))]
    d, p = lax.axis_index("dp"), lax.axis_index("point")
    axes = [(1, 1)] + [(0, b) for b in bits(dp)[1:]] + [(1, b) for b in bits(point)[1:]]
    turned = list(axes)
    for i in range(0, len(axes) - 1, 2):
        turned[i], turned[i + 1] = axes[i + 1], axes[i]

    def move(i):
        choices = [flip(*order[i]) for order in (axes, turned)]
        return lambda d, p: choices[d & 1](d, p)

    core = d & 1
    places = [((d if order[0][0] == 0 else p) & order[0][1]) // order[0][1]
              for order in (axes, turned)]
    upper = jnp.where(core == 0, places[0], places[1])

    def scatter(upper, moves):
        def step(value):
            mine, other = halve(value, upper)
            return mine + swap(other, moves, sizes)
        return step

    def add(moves):
        return lambda value: value + swap(value, moves, sizes)

    def gather(upper, moves):
        return lambda value: join(value, swap(value, moves, sizes), upper)

    cores = flip(0, 1)
    steps = [scatter(core, cores), scatter(upper, move(0))]
    steps += [add(move(i)) for i in range(1, len(axes))]
    return steps + [gather(upper, move(0)), gather(core, cores)]


def shards(
    sizes,
    inputs, cotangent, gain_one, fx_weight, x_weight, slice_logit_weight, temper,
    slice_query_matrix, slice_key_matrix, slice_value_matrix, out_weight, gain_two,
    expand_weight, down_weight,
):
    points, width = inputs.shape[1:]
    head_size, slices = slice_logit_weight.shape
    heads = temper.shape[0]
    total = heads * slices
    gain_one, gain_two = gain_one[None], gain_two[None]
    factor = 1.0 / math.sqrt(points * sizes[0] * sizes[1])

    def shape(*dims, dtype=F32):
        return jax.ShapeDtypeStruct(dims, dtype)

    def pair(*dims):
        return [shape(*dims, dtype=BF16)] * 2

    tall = pair(width, points)
    dense = 6 * points * width * width
    (w_h, w_l, fx_h, fx_l, as_h, as_l, h1_h, h1_l, x_t, both_h, both_l, sums) = call(
        front_kernel, "front", [HBM] * 6, [VMEM] * 12,
        pair(total, points) + tall * 3
        + [shape(width, points)] + pair(width, 2 * width) + [shape(head_size + 8, total)],
        (inputs, gain_one, fx_weight, x_weight, slice_logit_weight, temper),
        4 * dense,
        [
            pltpu.VMEM(inputs.shape, F32), pltpu.VMEM((1, width), F32),
            pltpu.VMEM((width, width), F32), pltpu.VMEM((width, width), F32),
            pltpu.VMEM((head_size, slices), F32), pltpu.SMEM((heads,), F32),
            pltpu.SemaphoreType.DMA((6,)),
        ],
    )
    ready = call(
        ready_kernel, "ready", [VMEM] * 8, [VMEM] * 10,
        [shape(width, points)] * 2 + pair(width, width) * 3 + pair(3 * head_size, head_size),
        (cotangent, out_weight, gain_two, expand_weight, down_weight, slice_query_matrix,
         slice_key_matrix, slice_value_matrix),
        2 * dense,
    )
    for step in point_steps(sizes):
        sums = step(sums)
    cot_t, hidden_grad, out_t_h, out_t_l, ex_h, ex_l, ext_h, ext_l, maps_h, maps_l = ready
    (out_sum, mixed_grad, sg_h, sg_l, middle, attn, sp_h, sp_l, h2_h, h2_l, bg_h, bg_l, hd_h,
     hd_l) = call(
        back_kernel, "back", [VMEM] * 15, [VMEM] * 14,
        [shape(head_size, total), shape(width, points)] + tall
        + [shape(5 * head_size, total), shape(2 * slices, total)] + tall * 4,
        (sums, x_t, w_h, w_l, cot_t, hidden_grad, out_weight, out_t_h, out_t_l, ex_h, ex_l,
         ext_h, ext_l, maps_h, maps_l),
        6 * dense,
    )
    early_value = call(
        functools.partial(early_kernel, factor), "early", [VMEM] * 10, VMEM,
        shape(3 * width, width),
        (sp_h, sp_l, mixed_grad, h2_h, h2_l, bg_h, bg_l, hd_h, hd_l, cotangent),
        3 * dense,
    )
    early_steps = all_steps(sizes)
    early_at = 0
    for i, step in enumerate(point_steps(sizes)):
        before = out_sum
        if early_at < len(early_steps) and i > 0:
            early_new = early_steps[early_at](early_value)
            early_at += 1
        else:
            early_new = early_value
        out_sum = step(before)
        out_sum, early_value = tie(out_sum, early_new)
    if early_at < len(early_steps):
        early_value = early_steps[early_at](early_value)
        early_at += 1
    late, bgr_h, bgr_l = call(
        functools.partial(end_kernel, factor, factor / sizes[1]), "end",
        [VMEM] * 18 + [SMEM], [VMEM] * 3,
        [shape(2 * width + head_size, width)] + pair(2 * width, points),
        (out_sum, sums, middle, attn, w_h, w_l, fx_h, fx_l, as_h, as_l, h1_h, h1_l, sg_h, sg_l,
         slice_query_matrix, slice_key_matrix, slice_value_matrix, slice_logit_weight, temper),
        8 * dense,
    )
    input_grad = call(
        rows_kernel, "rows", [VMEM] * 6, VMEM, shape(1, points, width),
        (both_h, both_l, bgr_h, bgr_l, x_t, mixed_grad),
        2 * dense,
    )
    for i, step in enumerate(all_steps(sizes)):
        if i > 0 and early_at < len(early_steps):
            early_new = early_steps[early_at](early_value)
            early_at += 1
            late = step(late)
            late, early_value = tie(late, early_new)
        else:
            late = step(late)
            late, early_value = tie(late, early_value)
    any_space = pl.BlockSpec(memory_space=pltpu.HBM)
    matrices, gain_row = call(
        early_out_kernel, "early_out", [VMEM] * 3, [any_space, VMEM],
        [shape(5, width, width), shape(1, width)],
        (early_value, gain_two, expand_weight),
        dense // 8,
        [pltpu.VMEM((width, width), F32), pltpu.SemaphoreType.DMA((3,))],
    )
    matrices, maps, logit, gains = call(
        late_out_kernel, "late_out", [VMEM] * 5 + [any_space], [any_space] + [VMEM] * 3,
        [shape(5, width, width), shape(3, head_size, head_size), shape(head_size, slices),
         shape(2, width)],
        (late, gain_one, fx_weight, x_weight, gain_row, matrices),
        dense // 8,
        [pltpu.VMEM((2, width, width), F32), pltpu.SemaphoreType.DMA((2,))],
        {5: 0},
    )
    return input_grad, matrices, maps, logit, gains


def solution(mesh):
    sizes = (mesh.shape["dp"], mesh.shape["point"])
    placed = (P("dp", "point", None),) * 2 + (P(),) * 12
    return jax.shard_map(
        functools.partial(shards, sizes),
        mesh=mesh,
        in_specs=placed,
        out_specs=(P("dp", "point", None), P(), P(), P(), P()),
        check_vma=False,
    )
```

```python
import functools
import math

import jax
import jax.numpy as jnp
from jax import lax
from jax.experimental import pallas as pl
from jax.experimental.pallas import tpu as pltpu
from jax.sharding import PartitionSpec as P

F32 = jnp.float32
BF16 = jnp.bfloat16
GROUP = 4
EPS = 1e-05
EARLY = 2
LATE = 1
GELU_A = math.sqrt(2.0 / math.pi)
GELU_B = 0.044715
SMALL = 16 * 1024 * 1024
FRONT_LIMIT = 16 * 1024 * 1024


def split(value):
    high = value.astype(BF16)
    return high, (value - high.astype(F32)).astype(BF16)


def product(left, right, left_dim, right_dim):
    def one(a, b):
        return lax.dot_general(
            a, b, (((left_dim,), (right_dim,)), ((), ())), preferred_element_type=F32
        )

    return one(left[0], right[0]) + (one(left[0], right[1]) + one(left[1], right[0]))


def rows_of(pair, start, size):
    return pair[0][start : start + size], pair[1][start : start + size]


def stacked(first, second, axis=0):
    return tuple(jnp.concatenate([a, b], axis=axis) for a, b in zip(first, second))


def column(row):
    wide = jnp.broadcast_to(row, (8, row.shape[1]))
    return wide.T[:, 0:1]


def head_mask(head_size, slices):
    shape = (GROUP * head_size, GROUP * slices)
    row = lax.broadcasted_iota(jnp.int32, shape, 0) // head_size
    lane = lax.broadcasted_iota(jnp.int32, shape, 1) // slices
    return row == lane


def spread_blocks(value, mask):
    return jnp.where(mask, jnp.concatenate([value] * GROUP, axis=0), 0.0)


def fold_blocks(value, mask, head_size):
    kept = jnp.where(mask, value, 0.0)
    total = kept[:head_size]
    for i in range(1, GROUP):
        total = total + kept[i * head_size : (i + 1) * head_size]
    return total


def standardise(columns):
    centre = columns - jnp.mean(columns, axis=0, keepdims=True)
    rstd = lax.rsqrt(jnp.mean(centre * centre, axis=0, keepdims=True) + EPS)
    return centre * rstd, rstd


def standardise_pull(grad, hat, rstd):
    first = jnp.mean(grad, axis=0, keepdims=True)
    second = jnp.mean(grad * hat, axis=0, keepdims=True)
    return rstd * (grad - first - hat * second)


def row_total(left, right):
    value = split(left * right)
    ones = jnp.ones((16, left.shape[1]), BF16)
    nt = (((1,), (1,)), ((), ()))
    total = lax.dot_general(ones, value[0], nt, preferred_element_type=F32)
    total = total + lax.dot_general(ones, value[1], nt, preferred_element_type=F32)
    return total[0:1]


def fetch(sources, targets, sems):
    copies = [
        pltpu.make_async_copy(source, target, sems.at[i])
        for i, (source, target) in enumerate(zip(sources, targets))
    ]
    for copy in copies:
        copy.start()
    return copies


def views(ref, *sizes):
    result, start = [], 0
    for size in sizes:
        result.append(ref.at[start : start + size])
        start += size
    return result


def front_kernel(
    x_hbm, gain_hbm, fx_hbm, xw_hbm, logit_hbm, temper_hbm,
    packed, wide_packed, sums,
    x, gain, fx_weight, x_weight, logit_weight, temper, sems,
):
    sources = (x_hbm, gain_hbm, fx_hbm, xw_hbm, logit_hbm, temper_hbm)
    targets = (x, gain, fx_weight, x_weight, logit_weight, temper)
    width, total = x.shape[2], packed.shape[1]
    weight_h, weight_l, fx_h, fx_l, assign_h, assign_l, hat_h, hat_l, both_h, both_l = views(
        packed, *[total] * 2, *[width] * 8
    )
    x_t, rstd_rows, temper_rows = views(wide_packed, width, 8, temper.shape[0])
    copies = fetch(sources, targets, sems)
    head_size, slices = logit_weight.shape
    heads = temper.shape[0]
    points = x.shape[1]
    width = x.shape[2]
    copies[0].wait()
    columns = x[0].T
    x_t[...] = columns
    hat, rstd = standardise(columns)
    rstd_rows[...] = jnp.broadcast_to(rstd, (8, points))
    hat = split(hat)
    hat_h[...], hat_l[...] = hat
    for copy in copies[1:]:
        copy.wait()
    both = jnp.concatenate([fx_weight[...], x_weight[...]], axis=1)
    both = split(both * column(gain[...]))
    both_h[...], both_l[...] = both
    projected = split(product(both, hat, 0, 0))
    fx = rows_of(projected, 0, width)
    assign = rows_of(projected, width, width)
    fx_h[...], fx_l[...] = fx
    assign_h[...], assign_l[...] = assign
    mask = head_mask(head_size, slices)
    wide = jnp.concatenate([logit_weight[...]] * GROUP, axis=1)
    logit_blocks = split(spread_blocks(wide, mask))
    ones = jnp.ones((16, points), BF16)
    nums, dens = [], []
    for g in range(heads // GROUP):
        rows = GROUP * head_size
        logits = product(logit_blocks, rows_of(assign, g * rows, rows), 0, 0)
        parts = []
        for i in range(GROUP):
            head = g * GROUP + i
            scale = jnp.full((1, points), temper[head], F32)
            temper_rows[head : head + 1] = scale
            scaled = logits[i * slices : (i + 1) * slices] / scale
            scaled = scaled - jnp.max(scaled, axis=0, keepdims=True)
            grown = jnp.exp(scaled)
            parts.append(grown / jnp.sum(grown, axis=0, keepdims=True))
        weights = split(jnp.concatenate(parts, axis=0))
        span = slice(g * GROUP * slices, (g + 1) * GROUP * slices)
        weight_h[span], weight_l[span] = weights
        num = product(rows_of(fx, g * rows, rows), weights, 1, 1)
        nums.append(fold_blocks(num, mask, head_size))
        nt = (((1,), (1,)), ((), ()))
        den = lax.dot_general(ones, weights[0], nt, preferred_element_type=F32)
        den = den + lax.dot_general(ones, weights[1], nt, preferred_element_type=F32)
        dens.append(den[:8])
    sums[0:head_size] = jnp.concatenate(nums, axis=1)
    sums[head_size : head_size + 8] = jnp.concatenate(dens, axis=1)


def map_views(packed, width, head_size, slices):
    views_of = views(
        packed, *[width] * 8, *[GROUP * head_size] * 2, *[3 * head_size] * 2, *[head_size] * 2
    )
    maps_t = [ref.at[:, 0:head_size] for ref in views_of[10:12]]
    maps = [ref.at[:, 0 : 3 * head_size] for ref in views_of[12:14]]
    logits = [ref.at[:, 0 : GROUP * slices] for ref in views_of[8:10]]
    return views_of[:8], logits, maps_t, maps


def ready_kernel(
    cotangent, out_weight, gain, expand_weight, down_weight, query, key, value, logit_weight,
    columns_packed, packed,
):
    width = cotangent.shape[2]
    head_size, slices = logit_weight.shape
    cot_t, hidden_grad = views(columns_packed, width, width)
    (out_h, out_l, out_t_h, out_t_l, expand_h, expand_l, expand_t_h, expand_t_l), logits, maps_t, maps = (
        map_views(packed, width, head_size, slices)
    )
    columns = cotangent[0].T
    cot_t[...] = columns
    hidden_grad[...] = product(split(down_weight[...]), split(columns), 1, 0)
    out_h[...], out_l[...] = split(out_weight[...])
    out_t_h[...], out_t_l[...] = split(out_weight[...].T)
    expand = expand_weight[...] * column(gain[...])
    expand_h[...], expand_l[...] = split(expand)
    expand_t_h[...], expand_t_l[...] = split(expand.T)
    both = jnp.concatenate([query[...], key[...], value[...]], axis=1)
    maps_t[0][...], maps_t[1][...] = split(both.T)
    maps[0][...], maps[1][...] = split(both)
    wide = jnp.concatenate([logit_weight[...]] * GROUP, axis=1)
    logits[0][...], logits[1][...] = split(spread_blocks(wide, head_mask(head_size, slices)))


def back_views(packed, wide_packed, width, head_size, slices):
    return views(packed, *[width] * 12) + views(
        wide_packed, width, 5 * head_size, 2 * slices, 8
    )


def back_kernel(
    head_size, slices,
    sums, front, front_wide, columns_packed, map_packed,
    out_sum, packed, wide_packed,
):
    total = front.shape[1]
    heads = total // slices
    width = (wide_packed.shape[0] - 8) - 5 * head_size - 2 * slices
    weight_h, weight_l = views(front, total, total)
    x_t = front_wide.at[0:width]
    cot_t, hidden_grad = views(columns_packed, width, width)
    (out_h, out_l, out_t_h, out_t_l, expand_h, expand_l, expand_t_h, expand_t_l), _, maps_t, _ = (
        map_views(map_packed, width, head_size, slices)
    )
    maps_h, maps_l = maps_t
    (spread_grad_h, spread_grad_l, spread_h, spread_l, hat_h, hat_l, before_grad_h, before_grad_l,
     hidden_h, hidden_l, grad_h, grad_l, mixed_grad, middle, attn, denom_rows) = back_views(
        packed, wide_packed, width, head_size, slices
    )
    rows, lanes = GROUP * head_size, GROUP * slices
    denom = sums[head_size : head_size + 1] + EPS
    denom_rows[...] = jnp.broadcast_to(denom, (8, total))
    tokens = sums[0:head_size] / denom
    qkv = product((maps_h[...], maps_l[...]), split(tokens), 1, 0)
    qkv_pair = split(qkv)
    wide = 2 * slices
    same = (lax.broadcasted_iota(jnp.int32, (wide, wide), 0) // slices) == (
        lax.broadcasted_iota(jnp.int32, (wide, wide), 1) // slices
    )
    results = []
    for pair in range(heads // 2):
        span = slice(pair * wide, (pair + 1) * wide)
        q = tuple(a[0:head_size, span] for a in qkv_pair)
        k = tuple(a[head_size : 2 * head_size, span] for a in qkv_pair)
        v = tuple(a[2 * head_size :, span] for a in qkv_pair)
        scores = product(k, q, 0, 0) * head_size ** (-0.5)
        scores = jnp.where(same, scores, -1e30)
        scores = scores - jnp.max(scores, axis=0, keepdims=True)
        grown = jnp.where(same, jnp.exp(scores), 0.0)
        probs = grown / jnp.sum(grown, axis=0, keepdims=True)
        attn[:, span] = probs
        results.append(product(v, split(probs), 1, 0))
    result = jnp.concatenate(results, axis=1)
    middle[0:head_size] = tokens
    middle[head_size : 4 * head_size] = qkv
    middle[4 * head_size : 5 * head_size] = result
    mask = head_mask(head_size, slices)
    spread = []
    for g in range(heads // GROUP):
        span = slice(g * lanes, (g + 1) * lanes)
        blocks = split(spread_blocks(result[:, span], mask))
        spread.append(product(blocks, (weight_h[span], weight_l[span]), 1, 0))
    spread = split(jnp.concatenate(spread, axis=0))
    spread_h[...], spread_l[...] = spread
    mixed = x_t[...] + product((out_t_h[...], out_t_l[...]), spread, 1, 0)
    hat, rstd = standardise(mixed)
    hat_pair = split(hat)
    hat_h[...], hat_l[...] = hat_pair
    before = product((expand_t_h[...], expand_t_l[...]), hat_pair, 1, 0)
    square = before * before
    bent = jnp.tanh(GELU_A * (before + GELU_B * before * square))
    half = 0.5 * (1.0 + bent)
    hidden_h[...], hidden_l[...] = split(before * half)
    slope = half + 0.5 * before * (1.0 - bent * bent) * (GELU_A * (1.0 + 3.0 * GELU_B * square))
    before_grad = split(hidden_grad[...] * slope)
    before_grad_h[...], before_grad_l[...] = before_grad
    hat_grad = product((expand_h[...], expand_l[...]), before_grad, 1, 0)
    grad = cot_t[...] + standardise_pull(hat_grad, hat, rstd)
    mixed_grad[...] = grad
    grad_pair = split(grad)
    grad_h[...], grad_l[...] = grad_pair
    spread_grad = split(product((out_h[...], out_l[...]), grad_pair, 1, 0))
    spread_grad_h[...], spread_grad_l[...] = spread_grad
    sums_out = []
    for g in range(heads // GROUP):
        span = slice(g * lanes, (g + 1) * lanes)
        full = product(
            rows_of(spread_grad, g * rows, rows), (weight_h[span], weight_l[span]), 1, 1
        )
        sums_out.append(fold_blocks(full, mask, head_size))
    out_sum[...] = jnp.concatenate(sums_out, axis=1)


def place(axes):
    d, p = lax.axis_index("dp"), lax.axis_index("point")
    halves = [lax.rem((p if axis else d) // bit, 2) for axis, bit in axes]
    first = lax.rem(d, 2) == 0
    return jnp.where(first, *halves), jnp.where(first, *halves[::-1])


def block(ref, index, size):
    return ref.at[pl.ds(pl.multiple_of(index * size, 8), size)]


def store_halves(value, mine, other):
    half = mine.shape[0]
    core = lax.rem(lax.axis_index("dp"), 2)
    mine[...] = block(value, core, half)[...]
    other[...] = block(value, 1 - core, half)[...]


def add_halve_kernel(axes, mine, received, kept, sent):
    half = kept.shape[0]
    upper, _ = place(axes)
    kept[...] = block(mine, upper, half)[...] + block(received, upper, half)[...]
    sent[...] = block(mine, 1 - upper, half)[...] + block(received, 1 - upper, half)[...]


def arrange(levels, own, partner, result):
    core = lax.rem(lax.axis_index("dp"), 2)
    count = 1 << len(levels)
    size = own.shape[0] // count
    for side, ref in enumerate((own, partner)):
        uppers = [place(axes)[side] for axes in levels]
        for i in range(count):
            index = core if side == 0 else 1 - core
            for level, upper in enumerate(uppers):
                same = (i >> (len(levels) - 1 - level)) & 1 == 0
                index = 2 * index + (upper if same else 1 - upper)
            block(result, index, size)[...] = ref[i * size : (i + 1) * size]


def early_kernel(factor, columns_packed, packed, mine, other, early):
    width = early.shape[1]
    pieces = [ref[...] for ref in views(packed, *[width] * 12)[2:]]
    spread, hat, before_grad, hidden, grad = (pieces[i : i + 2] for i in range(0, 10, 2))
    early[0:width] = product(spread, grad, 1, 1) * factor
    early[width : 2 * width] = product(hat, before_grad, 1, 1) * factor
    early[2 * width :] = product(hidden, split(columns_packed[0:width]), 1, 1) * factor
    store_halves(early, mine, other)


def end_kernel(
    factor, middle_factor, head_size, slices,
    out_sum, front, front_wide, map_packed, back, back_wide,
    late_mine, late_other, packed,
    late,
):
    width = late.shape[1]
    points = front.shape[1]
    total = out_sum.shape[1]
    heads = total // slices
    weight_h, weight_l, fx_h, fx_l, assign_h, assign_l, hat_h, hat_l = views(
        front, *[total] * 2, *[width] * 6
    )
    temper_rows = front_wide.at[width + 8 : width + 8 + heads]
    both_grad_h, both_grad_l = views(packed, 2 * width, 2 * width)
    _, logit_maps, _, maps = map_views(map_packed, width, head_size, slices)
    spread_grad_h, spread_grad_l, *_, middle, attn, denom_rows = back_views(
        back, back_wide, width, head_size, slices
    )
    rows, lanes = GROUP * head_size, GROUP * slices
    tokens = middle[0:head_size]
    qkv_pair = split(middle[head_size : 4 * head_size])
    result = middle[4 * head_size : 5 * head_size]
    result_grad = split(out_sum[...])
    wide = 2 * slices
    parts = []
    for pair in range(heads // 2):
        span = slice(pair * wide, (pair + 1) * wide)
        q = tuple(a[0:head_size, span] for a in qkv_pair)
        k = tuple(a[head_size : 2 * head_size, span] for a in qkv_pair)
        v = tuple(a[2 * head_size :, span] for a in qkv_pair)
        probs = attn[:, span]
        grad = tuple(a[:, span] for a in result_grad)
        value_grad = product(grad, split(probs), 1, 1)
        probs_grad = product(v, grad, 0, 0)
        weighted = probs * probs_grad
        total = jnp.sum(weighted, axis=0, keepdims=True)
        score_grad = split((weighted - probs * total) * head_size ** (-0.5))
        query_grad = product(k, score_grad, 1, 0)
        key_grad = product(q, score_grad, 1, 1)
        parts.append(jnp.concatenate([query_grad, key_grad, value_grad], axis=0))
    qkv_grad = split(jnp.concatenate(parts, axis=1))
    maps = (maps[0][...], maps[1][...])
    map_grad = product(split(tokens), qkv_grad, 1, 1)
    denom = denom_rows[0:1]
    num_grad = product(maps, qkv_grad, 1, 0) / denom
    den_grad = column(-jnp.sum(num_grad * tokens, axis=0, keepdims=True))
    mask = head_mask(head_size, slices)
    logit_blocks = (logit_maps[0][...], logit_maps[1][...])
    fx_grads, assign_grads = [], []
    logit_grad = jnp.zeros((head_size, lanes), F32)
    for g in range(heads // GROUP):
        span = slice(g * lanes, (g + 1) * lanes)
        piece = slice(g * rows, (g + 1) * rows)
        num_blocks = split(spread_blocks(num_grad[:, span], mask))
        result_blocks = split(spread_blocks(result[:, span], mask))
        weights = (weight_h[span], weight_l[span])
        fx_grads.append(product(num_blocks, weights, 1, 0))
        weight_grad = product(
            stacked(num_blocks, result_blocks),
            stacked(
                (fx_h[piece], fx_l[piece]), (spread_grad_h[piece], spread_grad_l[piece])
            ),
            0,
            0,
        )
        weight_grad = weight_grad + den_grad[span]
        grads = []
        for i in range(GROUP):
            block = slice(i * slices, (i + 1) * slices)
            head = g * GROUP + i
            scale = temper_rows[head : head + 1]
            w = weights[0][block].astype(F32) + weights[1][block].astype(F32)
            weighted = w * weight_grad[block]
            total = jnp.sum(weighted, axis=0, keepdims=True)
            grads.append((weighted - w * total) / scale)
        grads = split(jnp.concatenate(grads, axis=0))
        assign_grads.append(product(logit_blocks, grads, 1, 0))
        full = product((assign_h[piece], assign_l[piece]), grads, 1, 1)
        logit_grad = logit_grad + fold_blocks(full, mask, head_size)
    both_grad = split(jnp.concatenate(fx_grads + assign_grads, axis=0))
    both_grad_h[...], both_grad_l[...] = both_grad
    matrix = product((hat_h[...], hat_l[...]), both_grad, 1, 1) * factor
    late[0:width] = matrix[:, :width]
    late[width : 2 * width] = matrix[:, width:]
    logit_grad = logit_grad[:, : 2 * slices] + logit_grad[:, 2 * slices :]
    logit_grad = logit_grad[:, :slices] + logit_grad[:, slices:]
    base = 2 * width
    late[base:] = jnp.zeros((late.shape[0] - base, width), F32)
    late[base : base + head_size, 0 : 3 * head_size] = map_grad * middle_factor
    late[base : base + head_size, 128 : 128 + slices] = logit_grad * factor
    store_halves(late, late_mine, late_other)


def rows_kernel(front, front_wide, back_wide, end, x_grad):
    width = x_grad.shape[2]
    total = front.shape[1]
    _, hat_h, hat_l, both_h, both_l = views(front, 2 * total + 4 * width, *[width] * 4)
    rstd = front_wide[width : width + 1]
    grads = [ref[...] for ref in views(end, 2 * width, 2 * width)]
    hat_grad = product((both_h[...], both_l[...]), grads, 1, 0)
    hat = hat_h[...].astype(F32) + hat_l[...].astype(F32)
    x_grad[0] = (back_wide[0:width] + standardise_pull(hat_grad, hat, rstd)).T


def early_out_kernel(
    levels,
    own, partner, gain, expand_weight,
    matrices, gain_row,
    early, scaled, sems,
):
    arrange(levels, own, partner, early)
    width = gain.shape[1]
    copies = [
        pltpu.make_async_copy(early.at[0:width], matrices.at[2], sems.at[0]),
        pltpu.make_async_copy(early.at[2 * width : 3 * width], matrices.at[4], sems.at[1]),
        pltpu.make_async_copy(scaled, matrices.at[3], sems.at[2]),
    ]
    copies[0].start()
    copies[1].start()
    grad = early[width : 2 * width]
    scaled[...] = grad * column(gain[...])
    copies[2].start()
    gain_row[...] = row_total(grad, expand_weight[...])
    for copy in copies:
        copy.wait()


def late_out_kernel(
    levels,
    own, partner, gain, fx_weight, x_weight, gain_row, given,
    matrices, maps, logit, gains,
    late, scaled, sems,
):
    arrange(levels, own, partner, late)
    width = gain.shape[1]
    head_size, slices = logit.shape
    gain_column = column(gain[...])
    copies = []
    total = jnp.zeros((1, width), F32)
    for i, weight in enumerate((fx_weight, x_weight)):
        grad = late[i * width : (i + 1) * width]
        scaled[i] = grad * gain_column
        copies.append(pltpu.make_async_copy(scaled.at[i], matrices.at[i], sems.at[i]))
        copies[i].start()
        total = total + row_total(grad, weight[...])
    base = 2 * width
    for i in range(3):
        maps[i] = late[base : base + head_size, i * head_size : (i + 1) * head_size]
    logit[...] = late[base : base + head_size, 128 : 128 + slices]
    gains[...] = jnp.concatenate([total, gain_row[...]], axis=0)
    for copy in copies:
        copy.wait()


VMEM = pl.BlockSpec(memory_space=pltpu.VMEM)
SMEM = pl.BlockSpec(memory_space=pltpu.SMEM)


HBM = pl.BlockSpec(memory_space=pltpu.HBM)


def call(body, name, in_specs, out_specs, out_shape, args, flops, limit=SMALL, scratch=(),
         aliases=None):
    return pl.pallas_call(
        body,
        name=name,
        in_specs=in_specs,
        out_specs=out_specs,
        out_shape=out_shape,
        scratch_shapes=scratch,
        input_output_aliases=aliases or {},
        compiler_params=pltpu.CompilerParams(vmem_limit_bytes=limit),
        cost_estimate=pl.CostEstimate(flops=flops, bytes_accessed=1 << 20, transcendentals=0),
    )(*args)


def swap(value, moves, sizes):
    dp, point = sizes
    pairs = []
    for d in range(dp):
        for p in range(point):
            other_d, other_p = moves(d, p)
            pairs.append((d * point + p, other_d * point + other_p))
    return lax.ppermute(value, ("dp", "point"), pairs)


def bits(count):
    return [1 << i for i in range(count.bit_length() - 1)]


def tie(*values):
    return lax.optimization_barrier(values)


def flips(axes):
    def moves(d, p):
        axis, bit = axes[d & 1]
        return (d, p ^ bit) if axis else (d ^ bit, p)

    return moves


CORES = ((0, 1), (0, 1))


def paired(axes):
    turned = list(axes)
    for i in range(0, len(axes) - 1, 2):
        turned[i], turned[i + 1] = axes[i + 1], axes[i]
    return list(zip(axes, turned))


def point_steps(sizes):
    masks = bits(sizes[1])
    groups = [[bit] for bit in masks[:-2]]
    groups.append([masks[-2], masks[-1], masks[-2] | masks[-1]] if len(masks) > 1 else masks)

    def step(group):
        def run(value):
            parts = [swap(value, flips(((1, mask),) * 2), sizes) for mask in group]
            if len(parts) == 1:
                return value + parts[0]
            return (value + parts[0]) + (parts[1] + parts[2])
        return run

    return [step(group) for group in groups]


def all_axes(sizes):
    return paired(
        [(1, 1)] + [(0, b) for b in bits(sizes[0])[1:]] + [(1, b) for b in bits(sizes[1])[1:]]
    )


def all_steps(sizes, scatters):
    steps_axes = all_axes(sizes)

    def add_halve(i, mine, received):
        half = (mine.shape[0] // 2, mine.shape[1])
        return call(
            functools.partial(add_halve_kernel, steps_axes[i]), "add_halve", [VMEM] * 2,
            [VMEM] * 2, [jax.ShapeDtypeStruct(half, F32)] * 2, (mine, received), mine.size,
        )

    def cores(value):
        return add_halve(0, value[0], swap(value[1], flips(CORES), sizes))

    def scatter(i):
        def step(value):
            received = swap(value[1], flips(steps_axes[i]), sizes)
            if i + 1 < scatters:
                return add_halve(i + 1, value[0], received)
            return value[0] + received
        return step

    def add(i):
        return lambda value: value + swap(value, flips(steps_axes[i]), sizes)

    def gather(i):
        return lambda value: jnp.concatenate(
            [value, swap(value, flips(steps_axes[i]), sizes)], axis=0
        )

    def last(value):
        return value, swap(value, flips(CORES), sizes)

    return (
        [cores] + [scatter(i) for i in range(scatters)]
        + [add(i) for i in range(scatters, len(steps_axes))]
        + [gather(i) for i in reversed(range(scatters))] + [last]
    )


def shards(
    sizes,
    inputs, cotangent, gain_one, fx_weight, x_weight, slice_logit_weight, temper,
    slice_query_matrix, slice_key_matrix, slice_value_matrix, out_weight, gain_two,
    expand_weight, down_weight,
):
    points, width = inputs.shape[1:]
    head_size, slices = slice_logit_weight.shape
    heads = temper.shape[0]
    total = heads * slices
    gain_one, gain_two = gain_one[None], gain_two[None]
    factor = 1.0 / math.sqrt(points * sizes[0] * sizes[1])
    axes = all_axes(sizes)

    def shape(*dims, dtype=F32):
        return jax.ShapeDtypeStruct(dims, dtype)

    def pair(*dims):
        return [shape(*dims, dtype=BF16)] * 2

    dense = 6 * points * width * width
    pinned = [
        pltpu.with_memory_space_constraint(array, pltpu.HBM)
        for array in (inputs, gain_one, fx_weight, x_weight, slice_logit_weight, temper)
    ]
    front, front_wide, sums = call(
        front_kernel, "front", [HBM] * 6, [VMEM] * 3,
        [shape(2 * total + 8 * width, points, dtype=BF16), shape(width + 8 + heads, points),
         shape(head_size + 8, total)],
        pinned,
        4 * dense,
        FRONT_LIMIT,
        [
            pltpu.VMEM(inputs.shape, F32), pltpu.VMEM((1, width), F32),
            pltpu.VMEM((width, width), F32), pltpu.VMEM((width, width), F32),
            pltpu.VMEM((head_size, slices), F32), pltpu.SMEM((heads,), F32),
            pltpu.SemaphoreType.DMA((6,)),
        ],
    )
    sums, cotangent, out_weight, gain_two, expand_weight, down_weight = tie(
        sums, cotangent, out_weight, gain_two, expand_weight, down_weight
    )
    columns, maps = call(
        ready_kernel, "ready", [VMEM] * 9, [VMEM] * 2,
        [shape(2 * width, points),
         shape(8 * width + (2 * GROUP + 8) * head_size, width, dtype=BF16)],
        (cotangent, out_weight, gain_two, expand_weight, down_weight, slice_query_matrix,
         slice_key_matrix, slice_value_matrix, slice_logit_weight),
        2 * dense,
    )
    for step in point_steps(sizes):
        sums = step(sums)
    out_sum, back, back_wide = call(
        functools.partial(back_kernel, head_size, slices), "back", [VMEM] * 5, [VMEM] * 3,
        [shape(head_size, total), shape(12 * width, points, dtype=BF16),
         shape(width + 5 * head_size + 2 * slices + 8, points)],
        (sums, front, front_wide, columns, maps),
        6 * dense,
    )
    early_value = call(
        functools.partial(early_kernel, factor), "early", [VMEM] * 2, [VMEM] * 2,
        [shape(3 * width // 2, width)] * 2, (columns, back), 3 * dense,
        scratch=[pltpu.VMEM((3 * width, width), F32)],
    )
    early_steps = all_steps(sizes, EARLY)
    taken = 0
    for i, step in enumerate(point_steps(sizes)):
        if taken < len(early_steps):
            early_new = early_steps[taken](early_value)
            taken += 1
        else:
            early_new = early_value
        out_sum, early_value = tie(step(out_sum), early_new)
    if taken < len(early_steps):
        early_value = early_steps[taken](early_value)
        taken += 1
    rows = 2 * width + head_size
    mine, other, end = call(
        functools.partial(end_kernel, factor, factor / sizes[1], head_size, slices), "end",
        [VMEM] * 6, [VMEM] * 3,
        [shape(rows // 2, width)] * 2 + [shape(4 * width, points, dtype=BF16)],
        (out_sum, front, front_wide, maps, back, back_wide),
        8 * dense,
        scratch=[pltpu.VMEM((rows, width), F32)],
    )
    late, early_value = tie((mine, other), early_value)
    input_grad = call(
        rows_kernel, "rows", [VMEM] * 4, VMEM, shape(1, points, width),
        (front, front_wide, back_wide, end), 2 * dense,
    )
    steps = all_steps(sizes, LATE)
    for i, step in enumerate(steps):
        late = step(late)
        if i > 0 and taken < len(early_steps):
            late, early_value = tie(late, early_steps[taken](early_value))
            taken += 1
        if i == 0:
            late, input_grad = tie(late, input_grad)
    matrices, gain_row = call(
        functools.partial(early_out_kernel, tuple(axes[:EARLY])), "early_out", [VMEM] * 4, [HBM, VMEM],
        [shape(5, width, width), shape(1, width)],
        (*early_value, gain_two, expand_weight),
        dense // 8,
        scratch=[pltpu.VMEM((3 * width, width), F32), pltpu.VMEM((width, width), F32),
                 pltpu.SemaphoreType.DMA((3,))],
    )
    matrices, map_grads, logit_grad, gains = call(
        functools.partial(late_out_kernel, tuple(axes[:LATE])), "late_out", [VMEM] * 6 + [HBM],
        [HBM] + [VMEM] * 3,
        [shape(5, width, width), shape(3, head_size, head_size), shape(head_size, slices),
         shape(2, width)],
        (*late, gain_one, fx_weight, x_weight, gain_row, matrices),
        dense // 8,
        scratch=[pltpu.VMEM((rows, width), F32), pltpu.VMEM((2, width, width), F32),
                 pltpu.SemaphoreType.DMA((2,))],
        aliases={6: 0},
    )
    return input_grad, matrices, map_grads, logit_grad, gains


def solution(mesh):
    sizes = (mesh.shape["dp"], mesh.shape["point"])
    placed = (P("dp", "point", None),) * 2 + (P(),) * 12
    return jax.shard_map(
        functools.partial(shards, sizes),
        mesh=mesh,
        in_specs=placed,
        out_specs=(P("dp", "point", None), P(), P(), P(), P()),
        check_vma=False,
    )
```

```python
import functools
import math

import jax
import jax.numpy as jnp
from jax import lax
from jax.experimental import pallas as pl
from jax.experimental.pallas import tpu as pltpu
from jax.sharding import PartitionSpec as P

F32 = jnp.float32
BF16 = jnp.bfloat16
GROUP = 4
EPS = 1e-05
EARLY = 0
LATE = 0
GELU_A = math.sqrt(2.0 / math.pi)
GELU_B = 0.044715
SMALL = 16 * 1024 * 1024
FRONT_LIMIT = 16 * 1024 * 1024


def split(value):
    high = value.astype(BF16)
    return high, (value - high.astype(F32)).astype(BF16)


def product(left, right, left_dim, right_dim):
    def one(a, b):
        return lax.dot_general(
            a, b, (((left_dim,), (right_dim,)), ((), ())), preferred_element_type=F32
        )

    if left[0].shape[left_dim] % 128 == 0:
        return one(
            jnp.concatenate([left[0], left[0], left[1]], axis=left_dim),
            jnp.concatenate([right[0], right[1], right[0]], axis=right_dim),
        )
    return one(left[0], right[0]) + (one(left[0], right[1]) + one(left[1], right[0]))


def rows_of(pair, start, size):
    return pair[0][start : start + size], pair[1][start : start + size]


def stacked(first, second, axis=0):
    return tuple(jnp.concatenate([a, b], axis=axis) for a, b in zip(first, second))


def column(row):
    wide = jnp.broadcast_to(row, (8, row.shape[1]))
    return wide.T[:, 0:1]


def head_mask(head_size, slices):
    shape = (GROUP * head_size, GROUP * slices)
    row = lax.broadcasted_iota(jnp.int32, shape, 0) // head_size
    lane = lax.broadcasted_iota(jnp.int32, shape, 1) // slices
    return row == lane


def spread_blocks(value, mask):
    return jnp.where(mask, jnp.concatenate([value] * GROUP, axis=0), 0.0)


def fold_blocks(value, mask, head_size):
    kept = jnp.where(mask, value, 0.0)
    total = kept[:head_size]
    for i in range(1, GROUP):
        total = total + kept[i * head_size : (i + 1) * head_size]
    return total


def standardise(columns):
    centre = columns - jnp.mean(columns, axis=0, keepdims=True)
    rstd = lax.rsqrt(jnp.mean(centre * centre, axis=0, keepdims=True) + EPS)
    return centre * rstd, rstd


def standardise_pull(grad, hat, rstd):
    first = jnp.mean(grad, axis=0, keepdims=True)
    second = jnp.mean(grad * hat, axis=0, keepdims=True)
    return rstd * (grad - first - hat * second)


def row_total(left, right):
    value = split(left * right)
    ones = jnp.ones((16, left.shape[1]), BF16)
    nt = (((1,), (1,)), ((), ()))
    total = lax.dot_general(ones, value[0], nt, preferred_element_type=F32)
    total = total + lax.dot_general(ones, value[1], nt, preferred_element_type=F32)
    return total[0:1]


def fetch(sources, targets, sems):
    copies = [
        pltpu.make_async_copy(source, target, sems.at[i])
        for i, (source, target) in enumerate(zip(sources, targets))
    ]
    for copy in copies:
        copy.start()
    return copies


def views(ref, *sizes):
    result, start = [], 0
    for size in sizes:
        result.append(ref.at[start : start + size])
        start += size
    return result


def front_kernel(
    x_hbm, gain_hbm, fx_hbm, xw_hbm, logit_hbm, temper_hbm,
    packed, wide_packed, sums,
    x, gain, fx_weight, x_weight, logit_weight, temper, sems,
):
    sources = (x_hbm, gain_hbm, fx_hbm, xw_hbm, logit_hbm, temper_hbm)
    targets = (x, gain, fx_weight, x_weight, logit_weight, temper)
    width, total = x.shape[2], packed.shape[1]
    weight_h, weight_l, fx_h, fx_l, assign_h, assign_l, hat_h, hat_l, both_h, both_l = views(
        packed, *[total] * 2, *[width] * 8
    )
    x_t, rstd_rows, temper_rows = views(wide_packed, width, 8, temper.shape[0])
    copies = fetch(sources, targets, sems)
    head_size, slices = logit_weight.shape
    heads = temper.shape[0]
    points = x.shape[1]
    width = x.shape[2]
    copies[0].wait()
    columns = x[0].T
    x_t[...] = columns
    hat, rstd = standardise(columns)
    rstd_rows[...] = jnp.broadcast_to(rstd, (8, points))
    hat = split(hat)
    hat_h[...], hat_l[...] = hat
    for copy in copies[1:]:
        copy.wait()
    both = jnp.concatenate([fx_weight[...], x_weight[...]], axis=1)
    both = split(both * column(gain[...]))
    both_h[...], both_l[...] = both
    projected = split(product(both, hat, 0, 0))
    fx = rows_of(projected, 0, width)
    assign = rows_of(projected, width, width)
    fx_h[...], fx_l[...] = fx
    assign_h[...], assign_l[...] = assign
    mask = head_mask(head_size, slices)
    wide = jnp.concatenate([logit_weight[...]] * GROUP, axis=1)
    logit_blocks = split(spread_blocks(wide, mask))
    ones = jnp.ones((16, points), BF16)
    nums, dens = [], []
    for g in range(heads // GROUP):
        rows = GROUP * head_size
        logits = product(logit_blocks, rows_of(assign, g * rows, rows), 0, 0)
        parts = []
        for i in range(GROUP):
            head = g * GROUP + i
            scale = jnp.full((1, points), temper[head], F32)
            temper_rows[head : head + 1] = scale
            scaled = logits[i * slices : (i + 1) * slices] / scale
            scaled = scaled - jnp.max(scaled, axis=0, keepdims=True)
            grown = jnp.exp(scaled)
            parts.append(grown / jnp.sum(grown, axis=0, keepdims=True))
        weights = split(jnp.concatenate(parts, axis=0))
        span = slice(g * GROUP * slices, (g + 1) * GROUP * slices)
        weight_h[span], weight_l[span] = weights
        num = product(rows_of(fx, g * rows, rows), weights, 1, 1)
        nums.append(fold_blocks(num, mask, head_size))
        nt = (((1,), (1,)), ((), ()))
        den = lax.dot_general(ones, weights[0], nt, preferred_element_type=F32)
        den = den + lax.dot_general(ones, weights[1], nt, preferred_element_type=F32)
        dens.append(den[:8])
    sums[0:head_size] = jnp.concatenate(nums, axis=1)
    sums[head_size : head_size + 8] = jnp.concatenate(dens, axis=1)


def map_views(packed, width, head_size, slices):
    views_of = views(
        packed, *[width] * 8, *[GROUP * head_size] * 2, *[3 * head_size] * 2, *[head_size] * 2
    )
    maps_t = [ref.at[:, 0:head_size] for ref in views_of[10:12]]
    maps = [ref.at[:, 0 : 3 * head_size] for ref in views_of[12:14]]
    logits = [ref.at[:, 0 : GROUP * slices] for ref in views_of[8:10]]
    return views_of[:8], logits, maps_t, maps


def ready_kernel(
    cotangent, out_weight, gain, expand_weight, down_weight, query, key, value, logit_weight,
    columns_packed, packed,
):
    width = cotangent.shape[2]
    head_size, slices = logit_weight.shape
    cot_t, hidden_grad = views(columns_packed, width, width)
    (out_h, out_l, out_t_h, out_t_l, expand_h, expand_l, expand_t_h, expand_t_l), logits, maps_t, maps = (
        map_views(packed, width, head_size, slices)
    )
    columns = cotangent[0].T
    cot_t[...] = columns
    hidden_grad[...] = product(split(down_weight[...]), split(columns), 1, 0)
    out_h[...], out_l[...] = split(out_weight[...])
    out_t_h[...], out_t_l[...] = split(out_weight[...].T)
    expand = expand_weight[...] * column(gain[...])
    expand_h[...], expand_l[...] = split(expand)
    expand_t_h[...], expand_t_l[...] = split(expand.T)
    both = jnp.concatenate([query[...], key[...], value[...]], axis=1)
    maps_t[0][...], maps_t[1][...] = split(both.T)
    maps[0][...], maps[1][...] = split(both)
    wide = jnp.concatenate([logit_weight[...]] * GROUP, axis=1)
    logits[0][...], logits[1][...] = split(spread_blocks(wide, head_mask(head_size, slices)))


def back_views(packed, wide_packed, width, head_size, slices):
    return views(packed, *[width] * 12) + views(
        wide_packed, width, 5 * head_size, 2 * slices, 8
    )


def back_kernel(
    head_size, slices,
    sums, front, front_wide, columns_packed, map_packed,
    out_sum, packed, wide_packed,
):
    total = front.shape[1]
    heads = total // slices
    width = (wide_packed.shape[0] - 8) - 5 * head_size - 2 * slices
    weight_h, weight_l = views(front, total, total)
    x_t = front_wide.at[0:width]
    cot_t, hidden_grad = views(columns_packed, width, width)
    (out_h, out_l, out_t_h, out_t_l, expand_h, expand_l, expand_t_h, expand_t_l), _, maps_t, _ = (
        map_views(map_packed, width, head_size, slices)
    )
    maps_h, maps_l = maps_t
    (spread_grad_h, spread_grad_l, spread_h, spread_l, hat_h, hat_l, before_grad_h, before_grad_l,
     hidden_h, hidden_l, grad_h, grad_l, mixed_grad, middle, attn, denom_rows) = back_views(
        packed, wide_packed, width, head_size, slices
    )
    rows, lanes = GROUP * head_size, GROUP * slices
    denom = sums[head_size : head_size + 1] + EPS
    denom_rows[...] = jnp.broadcast_to(denom, (8, total))
    tokens = sums[0:head_size] / denom
    qkv = product((maps_h[...], maps_l[...]), split(tokens), 1, 0)
    qkv_pair = split(qkv)
    wide = 2 * slices
    same = (lax.broadcasted_iota(jnp.int32, (wide, wide), 0) // slices) == (
        lax.broadcasted_iota(jnp.int32, (wide, wide), 1) // slices
    )
    results = []
    for pair in range(heads // 2):
        span = slice(pair * wide, (pair + 1) * wide)
        q = tuple(a[0:head_size, span] for a in qkv_pair)
        k = tuple(a[head_size : 2 * head_size, span] for a in qkv_pair)
        v = tuple(a[2 * head_size :, span] for a in qkv_pair)
        scores = product(k, q, 0, 0) * head_size ** (-0.5)
        scores = jnp.where(same, scores, -1e30)
        scores = scores - jnp.max(scores, axis=0, keepdims=True)
        grown = jnp.where(same, jnp.exp(scores), 0.0)
        probs = grown / jnp.sum(grown, axis=0, keepdims=True)
        attn[:, span] = probs
        results.append(product(v, split(probs), 1, 0))
    result = jnp.concatenate(results, axis=1)
    middle[0:head_size] = tokens
    middle[head_size : 4 * head_size] = qkv
    middle[4 * head_size : 5 * head_size] = result
    mask = head_mask(head_size, slices)
    spread = []
    for g in range(heads // GROUP):
        span = slice(g * lanes, (g + 1) * lanes)
        blocks = split(spread_blocks(result[:, span], mask))
        spread.append(product(blocks, (weight_h[span], weight_l[span]), 1, 0))
    spread = split(jnp.concatenate(spread, axis=0))
    spread_h[...], spread_l[...] = spread
    mixed = x_t[...] + product((out_t_h[...], out_t_l[...]), spread, 1, 0)
    hat, rstd = standardise(mixed)
    hat_pair = split(hat)
    hat_h[...], hat_l[...] = hat_pair
    before = product((expand_t_h[...], expand_t_l[...]), hat_pair, 1, 0)
    square = before * before
    bent = jnp.tanh(GELU_A * (before + GELU_B * before * square))
    half = 0.5 * (1.0 + bent)
    hidden_h[...], hidden_l[...] = split(before * half)
    slope = half + 0.5 * before * (1.0 - bent * bent) * (GELU_A * (1.0 + 3.0 * GELU_B * square))
    before_grad = split(hidden_grad[...] * slope)
    before_grad_h[...], before_grad_l[...] = before_grad
    hat_grad = product((expand_h[...], expand_l[...]), before_grad, 1, 0)
    grad = cot_t[...] + standardise_pull(hat_grad, hat, rstd)
    mixed_grad[...] = grad
    grad_pair = split(grad)
    grad_h[...], grad_l[...] = grad_pair
    spread_grad = split(product((out_h[...], out_l[...]), grad_pair, 1, 0))
    spread_grad_h[...], spread_grad_l[...] = spread_grad
    sums_out = []
    for g in range(heads // GROUP):
        span = slice(g * lanes, (g + 1) * lanes)
        full = product(
            rows_of(spread_grad, g * rows, rows), (weight_h[span], weight_l[span]), 1, 1
        )
        sums_out.append(fold_blocks(full, mask, head_size))
    out_sum[...] = jnp.concatenate(sums_out, axis=1)


def place(axes):
    d, p = lax.axis_index("dp"), lax.axis_index("point")
    halves = [lax.rem((p if axis else d) // bit, 2) for axis, bit in axes]
    first = lax.rem(d, 2) == 0
    return jnp.where(first, *halves), jnp.where(first, *halves[::-1])


def block(ref, index, size):
    return ref.at[pl.ds(pl.multiple_of(index * size, 8), size)]


def store_halves(value, mine, other):
    half = mine.shape[0]
    core = lax.rem(lax.axis_index("dp"), 2)
    mine[...] = block(value, core, half)[...]
    other[...] = block(value, 1 - core, half)[...]


def quarter():
    return 2 * lax.rem(lax.axis_index("point"), 2) + lax.rem(lax.axis_index("dp") // 2, 2)


def add_quarter_kernel(mine, received, *parts):
    size = parts[0].shape[0]
    for i, part in enumerate(parts):
        index = quarter() ^ i
        part[...] = block(mine, index, size)[...] + block(received, index, size)[...]


def arrange_quarters(own, partner, result):
    core = lax.rem(lax.axis_index("dp"), 2)
    size = own.shape[0] // 4
    for side, ref in ((core, own), (1 - core, partner)):
        for i in range(4):
            block(result, 4 * side + (quarter() ^ i), size)[...] = ref[i * size : (i + 1) * size]


def add_halve_kernel(axes, mine, received, kept, sent):
    half = kept.shape[0]
    upper, _ = place(axes)
    kept[...] = block(mine, upper, half)[...] + block(received, upper, half)[...]
    sent[...] = block(mine, 1 - upper, half)[...] + block(received, 1 - upper, half)[...]


def arrange(levels, own, partner, result):
    if not levels:
        return arrange_quarters(own, partner, result)
    core = lax.rem(lax.axis_index("dp"), 2)
    count = 1 << len(levels)
    size = own.shape[0] // count
    for side, ref in enumerate((own, partner)):
        uppers = [place(axes)[side] for axes in levels]
        for i in range(count):
            index = core if side == 0 else 1 - core
            for level, upper in enumerate(uppers):
                same = (i >> (len(levels) - 1 - level)) & 1 == 0
                index = 2 * index + (upper if same else 1 - upper)
            block(result, index, size)[...] = ref[i * size : (i + 1) * size]


def early_kernel(factor, columns_packed, packed, mine, other, early):
    width = early.shape[1]
    pieces = [ref[...] for ref in views(packed, *[width] * 12)[2:]]
    spread, hat, before_grad, hidden, grad = (pieces[i : i + 2] for i in range(0, 10, 2))
    early[0:width] = product(spread, grad, 1, 1) * factor
    early[width : 2 * width] = product(hat, before_grad, 1, 1) * factor
    early[2 * width :] = product(hidden, split(columns_packed[0:width]), 1, 1) * factor
    store_halves(early, mine, other)


def end_kernel(
    factor, middle_factor, head_size, slices,
    out_sum, front, front_wide, map_packed, back, back_wide,
    late_mine, late_other, packed,
    late,
):
    width = late.shape[1]
    points = front.shape[1]
    total = out_sum.shape[1]
    heads = total // slices
    weight_h, weight_l, fx_h, fx_l, assign_h, assign_l, hat_h, hat_l = views(
        front, *[total] * 2, *[width] * 6
    )
    temper_rows = front_wide.at[width + 8 : width + 8 + heads]
    both_grad_h, both_grad_l = views(packed, 2 * width, 2 * width)
    _, logit_maps, _, maps = map_views(map_packed, width, head_size, slices)
    spread_grad_h, spread_grad_l, *_, middle, attn, denom_rows = back_views(
        back, back_wide, width, head_size, slices
    )
    rows, lanes = GROUP * head_size, GROUP * slices
    tokens = middle[0:head_size]
    qkv_pair = split(middle[head_size : 4 * head_size])
    result = middle[4 * head_size : 5 * head_size]
    result_grad = split(out_sum[...])
    wide = 2 * slices
    parts = []
    for pair in range(heads // 2):
        span = slice(pair * wide, (pair + 1) * wide)
        q = tuple(a[0:head_size, span] for a in qkv_pair)
        k = tuple(a[head_size : 2 * head_size, span] for a in qkv_pair)
        v = tuple(a[2 * head_size :, span] for a in qkv_pair)
        probs = attn[:, span]
        grad = tuple(a[:, span] for a in result_grad)
        value_grad = product(grad, split(probs), 1, 1)
        probs_grad = product(v, grad, 0, 0)
        weighted = probs * probs_grad
        total = jnp.sum(weighted, axis=0, keepdims=True)
        score_grad = split((weighted - probs * total) * head_size ** (-0.5))
        query_grad = product(k, score_grad, 1, 0)
        key_grad = product(q, score_grad, 1, 1)
        parts.append(jnp.concatenate([query_grad, key_grad, value_grad], axis=0))
    qkv_grad = split(jnp.concatenate(parts, axis=1))
    maps = (maps[0][...], maps[1][...])
    map_grad = product(split(tokens), qkv_grad, 1, 1)
    denom = denom_rows[0:1]
    num_grad = product(maps, qkv_grad, 1, 0) / denom
    den_grad = column(-jnp.sum(num_grad * tokens, axis=0, keepdims=True))
    mask = head_mask(head_size, slices)
    logit_blocks = (logit_maps[0][...], logit_maps[1][...])
    fx_grads, assign_grads = [], []
    logit_grad = jnp.zeros((head_size, lanes), F32)
    for g in range(heads // GROUP):
        span = slice(g * lanes, (g + 1) * lanes)
        piece = slice(g * rows, (g + 1) * rows)
        num_blocks = split(spread_blocks(num_grad[:, span], mask))
        result_blocks = split(spread_blocks(result[:, span], mask))
        weights = (weight_h[span], weight_l[span])
        fx_grads.append(product(num_blocks, weights, 1, 0))
        weight_grad = product(
            stacked(num_blocks, result_blocks),
            stacked(
                (fx_h[piece], fx_l[piece]), (spread_grad_h[piece], spread_grad_l[piece])
            ),
            0,
            0,
        )
        weight_grad = weight_grad + den_grad[span]
        grads = []
        for i in range(GROUP):
            block = slice(i * slices, (i + 1) * slices)
            head = g * GROUP + i
            scale = temper_rows[head : head + 1]
            w = weights[0][block].astype(F32) + weights[1][block].astype(F32)
            weighted = w * weight_grad[block]
            total = jnp.sum(weighted, axis=0, keepdims=True)
            grads.append((weighted - w * total) / scale)
        grads = split(jnp.concatenate(grads, axis=0))
        assign_grads.append(product(logit_blocks, grads, 1, 0))
        full = product((assign_h[piece], assign_l[piece]), grads, 1, 1)
        logit_grad = logit_grad + fold_blocks(full, mask, head_size)
    both_grad = split(jnp.concatenate(fx_grads + assign_grads, axis=0))
    both_grad_h[...], both_grad_l[...] = both_grad
    matrix = product((hat_h[...], hat_l[...]), both_grad, 1, 1) * factor
    late[0:width] = matrix[:, :width]
    late[width : 2 * width] = matrix[:, width:]
    logit_grad = logit_grad[:, : 2 * slices] + logit_grad[:, 2 * slices :]
    logit_grad = logit_grad[:, :slices] + logit_grad[:, slices:]
    base = 2 * width
    late[base:] = jnp.zeros((late.shape[0] - base, width), F32)
    late[base : base + head_size, 0 : 3 * head_size] = map_grad * middle_factor
    late[base : base + head_size, 128 : 128 + slices] = logit_grad * factor
    store_halves(late, late_mine, late_other)


def rows_kernel(front, front_wide, back_wide, end, x_grad):
    width = x_grad.shape[2]
    total = front.shape[1]
    _, hat_h, hat_l, both_h, both_l = views(front, 2 * total + 4 * width, *[width] * 4)
    rstd = front_wide[width : width + 1]
    grads = [ref[...] for ref in views(end, 2 * width, 2 * width)]
    hat_grad = product((both_h[...], both_l[...]), grads, 1, 0)
    hat = hat_h[...].astype(F32) + hat_l[...].astype(F32)
    x_grad[0] = (back_wide[0:width] + standardise_pull(hat_grad, hat, rstd)).T


def early_out_kernel(
    levels,
    own, partner, gain, expand_weight,
    matrices, gain_row,
    early, scaled, sems,
):
    arrange(levels, own, partner, early)
    width = gain.shape[1]
    copies = [
        pltpu.make_async_copy(early.at[0:width], matrices.at[2], sems.at[0]),
        pltpu.make_async_copy(early.at[2 * width : 3 * width], matrices.at[4], sems.at[1]),
        pltpu.make_async_copy(scaled, matrices.at[3], sems.at[2]),
    ]
    copies[0].start()
    copies[1].start()
    grad = early[width : 2 * width]
    scaled[...] = grad * column(gain[...])
    copies[2].start()
    gain_row[...] = row_total(grad, expand_weight[...])
    for copy in copies:
        copy.wait()


def late_out_kernel(
    levels,
    own, partner, gain, fx_weight, x_weight, gain_row, given,
    matrices, maps, logit, gains,
    late, scaled, sems,
):
    arrange(levels, own, partner, late)
    width = gain.shape[1]
    head_size, slices = logit.shape
    gain_column = column(gain[...])
    copies = []
    total = jnp.zeros((1, width), F32)
    for i, weight in enumerate((fx_weight, x_weight)):
        grad = late[i * width : (i + 1) * width]
        scaled[i] = grad * gain_column
        copies.append(pltpu.make_async_copy(scaled.at[i], matrices.at[i], sems.at[i]))
        copies[i].start()
        total = total + row_total(grad, weight[...])
    base = 2 * width
    for i in range(3):
        maps[i] = late[base : base + head_size, i * head_size : (i + 1) * head_size]
    logit[...] = late[base : base + head_size, 128 : 128 + slices]
    gains[...] = jnp.concatenate([total, gain_row[...]], axis=0)
    for copy in copies:
        copy.wait()


VMEM = pl.BlockSpec(memory_space=pltpu.VMEM)
SMEM = pl.BlockSpec(memory_space=pltpu.SMEM)


HBM = pl.BlockSpec(memory_space=pltpu.HBM)


def call(body, name, in_specs, out_specs, out_shape, args, flops, limit=SMALL, scratch=(),
         aliases=None):
    return pl.pallas_call(
        body,
        name=name,
        in_specs=in_specs,
        out_specs=out_specs,
        out_shape=out_shape,
        scratch_shapes=scratch,
        input_output_aliases=aliases or {},
        compiler_params=pltpu.CompilerParams(vmem_limit_bytes=limit),
        cost_estimate=pl.CostEstimate(flops=flops, bytes_accessed=1 << 20, transcendentals=0),
    )(*args)


def swap(value, moves, sizes):
    dp, point = sizes
    pairs = []
    for d in range(dp):
        for p in range(point):
            other_d, other_p = moves(d, p)
            pairs.append((d * point + p, other_d * point + other_p))
    return lax.ppermute(value, ("dp", "point"), pairs)


def bits(count):
    return [1 << i for i in range(count.bit_length() - 1)]


def tie(*values):
    return lax.optimization_barrier(values)


def flips(axes):
    def moves(d, p):
        axis, bit = axes[d & 1]
        return (d, p ^ bit) if axis else (d ^ bit, p)

    return moves


CORES = ((0, 1), (0, 1))


def paired(axes):
    turned = list(axes)
    for i in range(0, len(axes) - 1, 2):
        turned[i], turned[i + 1] = axes[i + 1], axes[i]
    return list(zip(axes, turned))


def point_steps(sizes):
    masks = bits(sizes[1])
    groups = [[bit] for bit in masks[:-2]]
    groups.append([masks[-2], masks[-1], masks[-2] | masks[-1]] if len(masks) > 1 else masks)

    def step(group):
        def run(value):
            parts = [swap(value, flips(((1, mask),) * 2), sizes) for mask in group]
            if len(parts) == 1:
                return value + parts[0]
            return (value + parts[0]) + (parts[1] + parts[2])
        return run

    return [step(group) for group in groups]


def all_axes(sizes):
    return paired(
        [(1, 1)] + [(0, b) for b in bits(sizes[0])[1:]] + [(1, b) for b in bits(sizes[1])[1:]]
    )


def quarter_steps(sizes):
    group = [lambda d, p: (d ^ 2, p), lambda d, p: (d, p ^ 1), lambda d, p: (d ^ 2, p ^ 1)]
    others = paired([(0, b) for b in bits(sizes[0])[2:]] + [(1, b) for b in bits(sizes[1])[1:]])

    def cores(value):
        received = swap(value[1], flips(CORES), sizes)
        part = (value[0].shape[0] // 4, value[0].shape[1])
        return call(
            add_quarter_kernel, "add_quarter", [VMEM] * 2, [VMEM] * 4,
            [jax.ShapeDtypeStruct(part, F32)] * 4, (value[0], received), received.size,
        )

    def scatter(value):
        parts = [swap(part, moves, sizes) for part, moves in zip(value[1:], group)]
        return (value[0] + parts[0]) + (parts[1] + parts[2])

    def add(axes):
        return lambda value: value + swap(value, flips(axes), sizes)

    def gather(value):
        return jnp.concatenate([value] + [swap(value, moves, sizes) for moves in group], axis=0)

    def last(value):
        return value, swap(value, flips(CORES), sizes)

    return [cores, scatter] + [add(axes) for axes in others] + [gather, last]


def all_steps(sizes, scatters):
    if scatters == 0:
        return quarter_steps(sizes)
    steps_axes = all_axes(sizes)

    def add_halve(i, mine, received):
        half = (mine.shape[0] // 2, mine.shape[1])
        return call(
            functools.partial(add_halve_kernel, steps_axes[i]), "add_halve", [VMEM] * 2,
            [VMEM] * 2, [jax.ShapeDtypeStruct(half, F32)] * 2, (mine, received), mine.size,
        )

    def cores(value):
        return add_halve(0, value[0], swap(value[1], flips(CORES), sizes))

    def scatter(i):
        def step(value):
            received = swap(value[1], flips(steps_axes[i]), sizes)
            if i + 1 < scatters:
                return add_halve(i + 1, value[0], received)
            return value[0] + received
        return step

    def add(i):
        return lambda value: value + swap(value, flips(steps_axes[i]), sizes)

    def gather(i):
        return lambda value: jnp.concatenate(
            [value, swap(value, flips(steps_axes[i]), sizes)], axis=0
        )

    def last(value):
        return value, swap(value, flips(CORES), sizes)

    return (
        [cores] + [scatter(i) for i in range(scatters)]
        + [add(i) for i in range(scatters, len(steps_axes))]
        + [gather(i) for i in reversed(range(scatters))] + [last]
    )


def shards(
    sizes,
    inputs, cotangent, gain_one, fx_weight, x_weight, slice_logit_weight, temper,
    slice_query_matrix, slice_key_matrix, slice_value_matrix, out_weight, gain_two,
    expand_weight, down_weight,
):
    points, width = inputs.shape[1:]
    head_size, slices = slice_logit_weight.shape
    heads = temper.shape[0]
    total = heads * slices
    gain_one, gain_two = gain_one[None], gain_two[None]
    factor = 1.0 / math.sqrt(points * sizes[0] * sizes[1])
    axes = all_axes(sizes)

    def shape(*dims, dtype=F32):
        return jax.ShapeDtypeStruct(dims, dtype)

    def pair(*dims):
        return [shape(*dims, dtype=BF16)] * 2

    dense = 6 * points * width * width
    pinned = [
        pltpu.with_memory_space_constraint(array, pltpu.HBM)
        for array in (inputs, gain_one, fx_weight, x_weight, slice_logit_weight, temper)
    ]
    front, front_wide, sums = call(
        front_kernel, "front", [HBM] * 6, [VMEM] * 3,
        [shape(2 * total + 8 * width, points, dtype=BF16), shape(width + 8 + heads, points),
         shape(head_size + 8, total)],
        pinned,
        4 * dense,
        FRONT_LIMIT,
        [
            pltpu.VMEM(inputs.shape, F32), pltpu.VMEM((1, width), F32),
            pltpu.VMEM((width, width), F32), pltpu.VMEM((width, width), F32),
            pltpu.VMEM((head_size, slices), F32), pltpu.SMEM((heads,), F32),
            pltpu.SemaphoreType.DMA((6,)),
        ],
    )
    sums, cotangent, out_weight, gain_two, expand_weight, down_weight = tie(
        sums, cotangent, out_weight, gain_two, expand_weight, down_weight
    )
    columns, maps = call(
        ready_kernel, "ready", [VMEM] * 9, [VMEM] * 2,
        [shape(2 * width, points),
         shape(8 * width + (2 * GROUP + 8) * head_size, width, dtype=BF16)],
        (cotangent, out_weight, gain_two, expand_weight, down_weight, slice_query_matrix,
         slice_key_matrix, slice_value_matrix, slice_logit_weight),
        2 * dense,
    )
    for step in point_steps(sizes):
        sums = step(sums)
    out_sum, back, back_wide = call(
        functools.partial(back_kernel, head_size, slices), "back", [VMEM] * 5, [VMEM] * 3,
        [shape(head_size, total), shape(12 * width, points, dtype=BF16),
         shape(width + 5 * head_size + 2 * slices + 8, points)],
        (sums, front, front_wide, columns, maps),
        6 * dense,
    )
    early_value = call(
        functools.partial(early_kernel, factor), "early", [VMEM] * 2, [VMEM] * 2,
        [shape(3 * width // 2, width)] * 2, (columns, back), 3 * dense,
        scratch=[pltpu.VMEM((3 * width, width), F32)],
    )
    behind = [early_value]
    for step in all_steps(sizes, EARLY):
        behind.append(step(behind[-1]))
    order = [0, 1]
    for i, step in enumerate(point_steps(sizes)):
        out_sum = step(out_sum)
        if i < len(order) and order[i] is not None:
            out_sum, _ = tie(out_sum, behind[order[i]])
    rows = -(-(2 * width + head_size) // 64) * 64
    mine, other, end = call(
        functools.partial(end_kernel, factor, factor / sizes[1], head_size, slices), "end",
        [VMEM] * 6, [VMEM] * 3,
        [shape(rows // 2, width)] * 2 + [shape(4 * width, points, dtype=BF16)],
        (out_sum, front, front_wide, maps, back, back_wide),
        8 * dense,
        scratch=[pltpu.VMEM((rows, width), F32)],
    )
    late, _ = tie((mine, other), behind[1])
    input_grad = call(
        rows_kernel, "rows", [VMEM] * 4, VMEM, shape(1, points, width),
        (front, front_wide, back_wide, end), 2 * dense,
    )
    steps = all_steps(sizes, LATE)
    for i, step in enumerate(steps):
        late = step(late)
        if i == 0:
            late, input_grad = tie(late, input_grad)
    matrices, gain_row = call(
        functools.partial(early_out_kernel, tuple(axes[:EARLY])), "early_out", [VMEM] * 4, [HBM, VMEM],
        [shape(5, width, width), shape(1, width)],
        (*behind[-1], gain_two, expand_weight),
        dense // 8,
        scratch=[pltpu.VMEM((3 * width, width), F32), pltpu.VMEM((width, width), F32),
                 pltpu.SemaphoreType.DMA((3,))],
    )
    matrices, map_grads, logit_grad, gains = call(
        functools.partial(late_out_kernel, tuple(axes[:LATE])), "late_out", [VMEM] * 6 + [HBM],
        [HBM] + [VMEM] * 3,
        [shape(5, width, width), shape(3, head_size, head_size), shape(head_size, slices),
         shape(2, width)],
        (*late, gain_one, fx_weight, x_weight, gain_row, matrices),
        dense // 8,
        scratch=[pltpu.VMEM((rows, width), F32), pltpu.VMEM((2, width, width), F32),
                 pltpu.SemaphoreType.DMA((2,))],
        aliases={6: 0},
    )
    return input_grad, matrices, map_grads, logit_grad, gains


def solution(mesh):
    sizes = (mesh.shape["dp"], mesh.shape["point"])
    placed = (P("dp", "point", None),) * 2 + (P(),) * 12
    return jax.shard_map(
        functools.partial(shards, sizes),
        mesh=mesh,
        in_specs=placed,
        out_specs=(P("dp", "point", None), P(), P(), P(), P()),
        check_vma=False,
    )
```

```python
import functools
import math

import jax
import jax.numpy as jnp
from jax import lax
from jax.experimental import pallas as pl
from jax.experimental.pallas import tpu as pltpu
from jax.sharding import PartitionSpec as P

F32 = jnp.float32
BF16 = jnp.bfloat16
GROUP = 4
EPS = 1e-05
EARLY = 0
LATE = 0
SIDE = 4
GELU_A = math.sqrt(2.0 / math.pi)
GELU_B = 0.044715
SMALL = 16 * 1024 * 1024
FRONT_LIMIT = 16 * 1024 * 1024


def split(value):
    high = value.astype(BF16)
    return high, (value - high.astype(F32)).astype(BF16)


def product(left, right, left_dim, right_dim):
    def one(a, b):
        return lax.dot_general(
            a, b, (((left_dim,), (right_dim,)), ((), ())), preferred_element_type=F32
        )

    if left[0].shape[left_dim] % 128 == 0 or left_dim == right_dim == 0:
        return one(
            jnp.concatenate([left[0], left[0], left[1]], axis=left_dim),
            jnp.concatenate([right[0], right[1], right[0]], axis=right_dim),
        )
    return one(left[0], right[0]) + (one(left[0], right[1]) + one(left[1], right[0]))


def rows_of(pair, start, size):
    return pair[0][start : start + size], pair[1][start : start + size]


def stacked(first, second, axis=0):
    return tuple(jnp.concatenate([a, b], axis=axis) for a, b in zip(first, second))


def column(row):
    wide = jnp.broadcast_to(row, (8, row.shape[1]))
    return wide.T[:, 0:1]


def head_mask(head_size, slices):
    shape = (GROUP * head_size, GROUP * slices)
    row = lax.broadcasted_iota(jnp.int32, shape, 0) // head_size
    lane = lax.broadcasted_iota(jnp.int32, shape, 1) // slices
    return row == lane


def spread_blocks(value, mask):
    return jnp.where(mask, jnp.concatenate([value] * GROUP, axis=0), 0.0)


def fold_blocks(value, mask, head_size):
    kept = jnp.where(mask, value, 0.0)
    total = kept[:head_size]
    for i in range(1, GROUP):
        total = total + kept[i * head_size : (i + 1) * head_size]
    return total


def standardise(columns):
    centre = columns - jnp.mean(columns, axis=0, keepdims=True)
    rstd = lax.rsqrt(jnp.mean(centre * centre, axis=0, keepdims=True) + EPS)
    return centre * rstd, rstd


def standardise_pull(grad, hat, rstd):
    first = jnp.mean(grad, axis=0, keepdims=True)
    second = jnp.mean(grad * hat, axis=0, keepdims=True)
    return rstd * (grad - first - hat * second)


def row_total(left, right):
    value = split(left * right)
    ones = jnp.ones((16, left.shape[1]), BF16)
    nt = (((1,), (1,)), ((), ()))
    total = lax.dot_general(ones, value[0], nt, preferred_element_type=F32)
    total = total + lax.dot_general(ones, value[1], nt, preferred_element_type=F32)
    return total[0:1]


def fetch(sources, targets, sems):
    copies = [
        pltpu.make_async_copy(source, target, sems.at[i])
        for i, (source, target) in enumerate(zip(sources, targets))
    ]
    for copy in copies:
        copy.start()
    return copies


def views(ref, *sizes):
    result, start = [], 0
    for size in sizes:
        result.append(ref.at[start : start + size])
        start += size
    return result


def front_kernel(
    x_hbm, gain_hbm, fx_hbm, xw_hbm, logit_hbm, temper_hbm,
    packed, wide_packed, sums,
    x, gain, fx_weight, x_weight, logit_weight, temper, sems,
):
    sources = (x_hbm, gain_hbm, fx_hbm, xw_hbm, logit_hbm, temper_hbm)
    targets = (x, gain, fx_weight, x_weight, logit_weight, temper)
    width, total = x.shape[2], packed.shape[1]
    weight_h, weight_l, fx_h, fx_l, assign_h, assign_l, hat_h, hat_l, both_h, both_l = views(
        packed, *[total] * 2, *[width] * 8
    )
    x_t, rstd_rows, temper_rows = views(wide_packed, width, 8, temper.shape[0])
    copies = fetch(sources, targets, sems)
    sums[sums.shape[0] - 8 :] = jnp.zeros((8, 128), F32)
    head_size, slices = logit_weight.shape
    heads = temper.shape[0]
    points = x.shape[1]
    width = x.shape[2]
    copies[0].wait()
    columns = x[0].T
    x_t[...] = columns
    hat, rstd = standardise(columns)
    rstd_rows[...] = jnp.broadcast_to(rstd, (8, points))
    hat = split(hat)
    hat_h[...], hat_l[...] = hat
    for copy in copies[1:]:
        copy.wait()
    both = jnp.concatenate([fx_weight[...], x_weight[...]], axis=1)
    both = split(both * column(gain[...]))
    both_h[...], both_l[...] = both
    projected = split(product(both, hat, 0, 0))
    fx = rows_of(projected, 0, width)
    assign = rows_of(projected, width, width)
    fx_h[...], fx_l[...] = fx
    assign_h[...], assign_l[...] = assign
    mask = head_mask(head_size, slices)
    wide = jnp.concatenate([logit_weight[...]] * GROUP, axis=1)
    logit_blocks = split(spread_blocks(wide, mask))
    ones = jnp.ones((16, points), BF16)
    blocks = total // 128
    for g in range(heads // GROUP):
        rows = GROUP * head_size
        logits = product(logit_blocks, rows_of(assign, g * rows, rows), 0, 0)
        parts = []
        for i in range(GROUP):
            head = g * GROUP + i
            scale = jnp.full((1, points), temper[head], F32)
            temper_rows[head : head + 1] = scale
            scaled = logits[i * slices : (i + 1) * slices] / scale
            scaled = scaled - jnp.max(scaled, axis=0, keepdims=True)
            grown = jnp.exp(scaled)
            parts.append(grown / jnp.sum(grown, axis=0, keepdims=True))
        weights = split(jnp.concatenate(parts, axis=0))
        span = slice(g * GROUP * slices, (g + 1) * GROUP * slices)
        weight_h[span], weight_l[span] = weights
        num = product(rows_of(fx, g * rows, rows), weights, 1, 1)
        num = fold_blocks(num, mask, head_size)
        nt = (((1,), (1,)), ((), ()))
        den = lax.dot_general(ones, weights[0], nt, preferred_element_type=F32)
        den = den + lax.dot_general(ones, weights[1], nt, preferred_element_type=F32)
        for i in range(num.shape[1] // 128):
            j = g * (num.shape[1] // 128) + i
            lanes = slice(i * 128, (i + 1) * 128)
            sums[j * head_size : (j + 1) * head_size] = num[:, lanes]
            row = blocks * head_size + j
            sums[row : row + 1] = den[0:1, lanes]


def map_views(packed, width, head_size, slices):
    views_of = views(
        packed, *[width] * 8, *[GROUP * head_size] * 2, *[3 * head_size] * 2, *[head_size] * 2
    )
    maps_t = [ref.at[:, 0:head_size] for ref in views_of[10:12]]
    maps = [ref.at[:, 0 : 3 * head_size] for ref in views_of[12:14]]
    logits = [ref.at[:, 0 : GROUP * slices] for ref in views_of[8:10]]
    return views_of[:8], logits, maps_t, maps


def ready_kernel(
    cotangent, out_weight, gain, expand_weight, down_weight, query, key, value, logit_weight,
    columns_packed, packed,
):
    width = cotangent.shape[2]
    head_size, slices = logit_weight.shape
    cot_t, hidden_grad = views(columns_packed, width, width)
    (out_h, out_l, out_t_h, out_t_l, expand_h, expand_l, expand_t_h, expand_t_l), logits, maps_t, maps = (
        map_views(packed, width, head_size, slices)
    )
    columns = cotangent[0].T
    cot_t[...] = columns
    hidden_grad[...] = product(split(down_weight[...]), split(columns), 1, 0)
    out_h[...], out_l[...] = split(out_weight[...])
    out_t_h[...], out_t_l[...] = split(out_weight[...].T)
    expand = expand_weight[...] * column(gain[...])
    expand_h[...], expand_l[...] = split(expand)
    expand_t_h[...], expand_t_l[...] = split(expand.T)
    both = jnp.concatenate([query[...], key[...], value[...]], axis=1)
    maps_t[0][...], maps_t[1][...] = split(both.T)
    maps[0][...], maps[1][...] = split(both)
    wide = jnp.concatenate([logit_weight[...]] * GROUP, axis=1)
    logits[0][...], logits[1][...] = split(spread_blocks(wide, head_mask(head_size, slices)))


def back_views(packed, wide_packed, width, head_size, slices):
    return views(packed, *[width] * 12) + views(
        wide_packed, width, 5 * head_size, SIDE * slices, 8
    )


def back_kernel(
    head_size, slices,
    sums, front, front_wide, columns_packed, map_packed,
    out_sum, packed, wide_packed,
):
    total = front.shape[1]
    heads = total // slices
    width = (wide_packed.shape[0] - 8) - 5 * head_size - SIDE * slices
    weight_h, weight_l = views(front, total, total)
    x_t = front_wide.at[0:width]
    cot_t, hidden_grad = views(columns_packed, width, width)
    (out_h, out_l, out_t_h, out_t_l, expand_h, expand_l, expand_t_h, expand_t_l), _, maps_t, _ = (
        map_views(map_packed, width, head_size, slices)
    )
    maps_h, maps_l = maps_t
    (spread_grad_h, spread_grad_l, spread_h, spread_l, hat_h, hat_l, before_grad_h, before_grad_l,
     hidden_h, hidden_l, grad_h, grad_l, mixed_grad, middle, attn, denom_rows) = back_views(
        packed, wide_packed, width, head_size, slices
    )
    rows, lanes = GROUP * head_size, GROUP * slices
    blocks = total // 128
    ends = [blocks * head_size + j for j in range(blocks)]
    denom = jnp.concatenate([sums[end : end + 1] for end in ends], axis=1) + EPS
    nums = [sums[j * head_size : (j + 1) * head_size] for j in range(blocks)]
    denom_rows[...] = jnp.broadcast_to(denom, (8, total))
    tokens = jnp.concatenate(nums, axis=1) / denom
    qkv = product((maps_h[...], maps_l[...]), split(tokens), 1, 0)
    qkv_pair = split(qkv)
    wide = SIDE * slices
    same = (lax.broadcasted_iota(jnp.int32, (wide, wide), 0) // slices) == (
        lax.broadcasted_iota(jnp.int32, (wide, wide), 1) // slices
    )
    results = []
    for pair in range(heads // SIDE):
        span = slice(pair * wide, (pair + 1) * wide)
        q = tuple(a[0:head_size, span] for a in qkv_pair)
        k = tuple(a[head_size : 2 * head_size, span] for a in qkv_pair)
        v = tuple(a[2 * head_size :, span] for a in qkv_pair)
        scores = product(k, q, 0, 0) * head_size ** (-0.5)
        scores = jnp.where(same, scores, -1e30)
        scores = scores - jnp.max(scores, axis=0, keepdims=True)
        grown = jnp.where(same, jnp.exp(scores), 0.0)
        probs = grown / jnp.sum(grown, axis=0, keepdims=True)
        attn[:, span] = probs
        results.append(product(v, split(probs), 1, 0))
    result = jnp.concatenate(results, axis=1)
    middle[0:head_size] = tokens
    middle[head_size : 4 * head_size] = qkv
    middle[4 * head_size : 5 * head_size] = result
    mask = head_mask(head_size, slices)
    spread = []
    for g in range(heads // GROUP):
        span = slice(g * lanes, (g + 1) * lanes)
        blocks = split(spread_blocks(result[:, span], mask))
        spread.append(product(blocks, (weight_h[span], weight_l[span]), 1, 0))
    spread = split(jnp.concatenate(spread, axis=0))
    spread_h[...], spread_l[...] = spread
    mixed = x_t[...] + product((out_t_h[...], out_t_l[...]), spread, 1, 0)
    hat, rstd = standardise(mixed)
    hat_pair = split(hat)
    hat_h[...], hat_l[...] = hat_pair
    before = product((expand_t_h[...], expand_t_l[...]), hat_pair, 1, 0)
    square = before * before
    bent = jnp.tanh(GELU_A * (before + GELU_B * before * square))
    half = 0.5 * (1.0 + bent)
    hidden_h[...], hidden_l[...] = split(before * half)
    slope = half + 0.5 * before * (1.0 - bent * bent) * (GELU_A * (1.0 + 3.0 * GELU_B * square))
    before_grad = split(hidden_grad[...] * slope)
    before_grad_h[...], before_grad_l[...] = before_grad
    hat_grad = product((expand_h[...], expand_l[...]), before_grad, 1, 0)
    grad = cot_t[...] + standardise_pull(hat_grad, hat, rstd)
    mixed_grad[...] = grad
    grad_pair = split(grad)
    grad_h[...], grad_l[...] = grad_pair
    spread_grad = split(product((out_h[...], out_l[...]), grad_pair, 1, 0))
    spread_grad_h[...], spread_grad_l[...] = spread_grad
    sums_out = []
    for g in range(heads // GROUP):
        span = slice(g * lanes, (g + 1) * lanes)
        full = product(
            rows_of(spread_grad, g * rows, rows), (weight_h[span], weight_l[span]), 1, 1
        )
        sums_out.append(fold_blocks(full, mask, head_size))
    out_sum[...] = jnp.concatenate(sums_out, axis=1)


def place(axes):
    d, p = lax.axis_index("dp"), lax.axis_index("point")
    halves = [lax.rem((p if axis else d) // bit, 2) for axis, bit in axes]
    first = lax.rem(d, 2) == 0
    return jnp.where(first, *halves), jnp.where(first, *halves[::-1])


def block(ref, index, size):
    return ref.at[pl.ds(pl.multiple_of(index * size, 8), size)]


def store_halves(value, mine, other):
    half = mine.shape[0]
    core = lax.rem(lax.axis_index("dp"), 2)
    mine[...] = block(value, core, half)[...]
    other[...] = block(value, 1 - core, half)[...]


def quarter():
    return 2 * lax.rem(lax.axis_index("point"), 2) + lax.rem(lax.axis_index("dp") // 2, 2)


def add_quarter_kernel(mine, received, *parts):
    size = parts[0].shape[0]
    for i, part in enumerate(parts):
        index = quarter() ^ i
        part[...] = block(mine, index, size)[...] + block(received, index, size)[...]


def arrange_quarters(own, partner, result):
    core = lax.rem(lax.axis_index("dp"), 2)
    size = own.shape[0] // 4
    for side, ref in ((core, own), (1 - core, partner)):
        for i in range(4):
            block(result, 4 * side + (quarter() ^ i), size)[...] = ref[i * size : (i + 1) * size]


def add_halve_kernel(axes, mine, received, kept, sent):
    half = kept.shape[0]
    upper, _ = place(axes)
    kept[...] = block(mine, upper, half)[...] + block(received, upper, half)[...]
    sent[...] = block(mine, 1 - upper, half)[...] + block(received, 1 - upper, half)[...]


def arrange(levels, own, partner, result):
    if not levels:
        return arrange_quarters(own, partner, result)
    core = lax.rem(lax.axis_index("dp"), 2)
    count = 1 << len(levels)
    size = own.shape[0] // count
    for side, ref in enumerate((own, partner)):
        uppers = [place(axes)[side] for axes in levels]
        for i in range(count):
            index = core if side == 0 else 1 - core
            for level, upper in enumerate(uppers):
                same = (i >> (len(levels) - 1 - level)) & 1 == 0
                index = 2 * index + (upper if same else 1 - upper)
            block(result, index, size)[...] = ref[i * size : (i + 1) * size]


def early_kernel(factor, columns_packed, packed, mine, other, early):
    width = early.shape[1]
    pieces = [ref[...] for ref in views(packed, *[width] * 12)[2:]]
    spread, hat, before_grad, hidden, grad = (pieces[i : i + 2] for i in range(0, 10, 2))
    early[0:width] = product(spread, grad, 1, 1) * factor
    early[width : 2 * width] = product(hat, before_grad, 1, 1) * factor
    early[2 * width :] = product(hidden, split(columns_packed[0:width]), 1, 1) * factor
    store_halves(early, mine, other)


def end_kernel(
    factor, middle_factor, head_size, slices,
    out_sum, front, front_wide, map_packed, back, back_wide,
    late_mine, late_other, packed,
    late,
):
    width = late.shape[1]
    points = front.shape[1]
    total = out_sum.shape[1]
    heads = total // slices
    weight_h, weight_l, fx_h, fx_l, assign_h, assign_l, hat_h, hat_l = views(
        front, *[total] * 2, *[width] * 6
    )
    temper_rows = front_wide.at[width + 8 : width + 8 + heads]
    both_grad_h, both_grad_l = views(packed, 2 * width, 2 * width)
    _, logit_maps, _, maps = map_views(map_packed, width, head_size, slices)
    spread_grad_h, spread_grad_l, *_, middle, attn, denom_rows = back_views(
        back, back_wide, width, head_size, slices
    )
    rows, lanes = GROUP * head_size, GROUP * slices
    tokens = middle[0:head_size]
    qkv_pair = split(middle[head_size : 4 * head_size])
    result = middle[4 * head_size : 5 * head_size]
    result_grad = split(out_sum[...])
    wide = SIDE * slices
    parts = []
    for pair in range(heads // SIDE):
        span = slice(pair * wide, (pair + 1) * wide)
        q = tuple(a[0:head_size, span] for a in qkv_pair)
        k = tuple(a[head_size : 2 * head_size, span] for a in qkv_pair)
        v = tuple(a[2 * head_size :, span] for a in qkv_pair)
        probs = attn[:, span]
        grad = tuple(a[:, span] for a in result_grad)
        value_grad = product(grad, split(probs), 1, 1)
        probs_grad = product(v, grad, 0, 0)
        weighted = probs * probs_grad
        total = jnp.sum(weighted, axis=0, keepdims=True)
        score_grad = split((weighted - probs * total) * head_size ** (-0.5))
        query_grad = product(k, score_grad, 1, 0)
        key_grad = product(q, score_grad, 1, 1)
        parts.append(jnp.concatenate([query_grad, key_grad, value_grad], axis=0))
    qkv_grad = split(jnp.concatenate(parts, axis=1))
    maps = (maps[0][...], maps[1][...])
    map_grad = product(split(tokens), qkv_grad, 1, 1)
    denom = denom_rows[0:1]
    num_grad = product(maps, qkv_grad, 1, 0) / denom
    den_grad = column(-jnp.sum(num_grad * tokens, axis=0, keepdims=True))
    mask = head_mask(head_size, slices)
    logit_blocks = (logit_maps[0][...], logit_maps[1][...])
    fx_grads, assign_grads = [], []
    logit_grad = jnp.zeros((head_size, lanes), F32)
    for g in range(heads // GROUP):
        span = slice(g * lanes, (g + 1) * lanes)
        piece = slice(g * rows, (g + 1) * rows)
        num_blocks = split(spread_blocks(num_grad[:, span], mask))
        result_blocks = split(spread_blocks(result[:, span], mask))
        weights = (weight_h[span], weight_l[span])
        fx_grads.append(product(num_blocks, weights, 1, 0))
        weight_grad = product(
            stacked(num_blocks, result_blocks),
            stacked(
                (fx_h[piece], fx_l[piece]), (spread_grad_h[piece], spread_grad_l[piece])
            ),
            0,
            0,
        )
        weight_grad = weight_grad + den_grad[span]
        grads = []
        for i in range(GROUP):
            block = slice(i * slices, (i + 1) * slices)
            head = g * GROUP + i
            scale = temper_rows[head : head + 1]
            w = weights[0][block].astype(F32) + weights[1][block].astype(F32)
            weighted = w * weight_grad[block]
            total = jnp.sum(weighted, axis=0, keepdims=True)
            grads.append((weighted - w * total) / scale)
        grads = split(jnp.concatenate(grads, axis=0))
        assign_grads.append(product(logit_blocks, grads, 1, 0))
        full = product((assign_h[piece], assign_l[piece]), grads, 1, 1)
        logit_grad = logit_grad + fold_blocks(full, mask, head_size)
    both_grad = split(jnp.concatenate(fx_grads + assign_grads, axis=0))
    both_grad_h[...], both_grad_l[...] = both_grad
    matrix = product((hat_h[...], hat_l[...]), both_grad, 1, 1) * factor
    late[0:width] = matrix[:, :width]
    late[width : 2 * width] = matrix[:, width:]
    logit_grad = logit_grad[:, : 2 * slices] + logit_grad[:, 2 * slices :]
    logit_grad = logit_grad[:, :slices] + logit_grad[:, slices:]
    base = 2 * width
    late[base:] = jnp.zeros((late.shape[0] - base, width), F32)
    late[base : base + head_size, 0 : 3 * head_size] = map_grad * middle_factor
    late[base : base + head_size, 128 : 128 + slices] = logit_grad * factor
    store_halves(late, late_mine, late_other)


def rows_kernel(front, front_wide, back_wide, end, x_grad):
    width = x_grad.shape[2]
    total = front.shape[1]
    _, hat_h, hat_l, both_h, both_l = views(front, 2 * total + 4 * width, *[width] * 4)
    rstd = front_wide[width : width + 1]
    grads = [ref[...] for ref in views(end, 2 * width, 2 * width)]
    hat_grad = product((both_h[...], both_l[...]), grads, 1, 0)
    hat = hat_h[...].astype(F32) + hat_l[...].astype(F32)
    x_grad[0] = (back_wide[0:width] + standardise_pull(hat_grad, hat, rstd)).T


def early_out_kernel(
    levels,
    own, partner, gain, expand_weight,
    matrices, gain_row,
    early, scaled, sems,
):
    arrange(levels, own, partner, early)
    width = gain.shape[1]
    copies = [
        pltpu.make_async_copy(early.at[0:width], matrices.at[2], sems.at[0]),
        pltpu.make_async_copy(early.at[2 * width : 3 * width], matrices.at[4], sems.at[1]),
        pltpu.make_async_copy(scaled, matrices.at[3], sems.at[2]),
    ]
    copies[0].start()
    copies[1].start()
    grad = early[width : 2 * width]
    scaled[...] = grad * column(gain[...])
    copies[2].start()
    gain_row[...] = row_total(grad, expand_weight[...])
    for copy in copies:
        copy.wait()


def late_out_kernel(
    levels,
    own, partner, gain, fx_weight, x_weight, gain_row, given,
    matrices, maps_out, logit_out, gains_out,
    late, scaled, maps, logit, gains, sems,
):
    arrange(levels, own, partner, late)
    width = gain.shape[1]
    head_size, slices = logit.shape
    base = 2 * width
    for i in range(3):
        maps[i] = late[base : base + head_size, i * head_size : (i + 1) * head_size]
    logit[...] = late[base : base + head_size, 128 : 128 + slices]
    copies = fetch((maps, logit), (maps_out, logit_out), sems)
    gain_column = column(gain[...])
    total = jnp.zeros((1, width), F32)
    for i, weight in enumerate((fx_weight, x_weight)):
        scaled[i] = late[i * width : (i + 1) * width] * gain_column
        copy = pltpu.make_async_copy(scaled.at[i], matrices.at[i], sems.at[2 + i])
        copy.start()
        copies.append(copy)
    for i, weight in enumerate((fx_weight, x_weight)):
        total = total + row_total(late[i * width : (i + 1) * width], weight[...])
    gains[...] = jnp.concatenate([total, gain_row[...]], axis=0)
    copies.append(pltpu.make_async_copy(gains, gains_out, sems.at[4]))
    copies[-1].start()
    for copy in copies:
        copy.wait()


VMEM = pl.BlockSpec(memory_space=pltpu.VMEM)
SMEM = pl.BlockSpec(memory_space=pltpu.SMEM)


HBM = pl.BlockSpec(memory_space=pltpu.HBM)


def call(body, name, in_specs, out_specs, out_shape, args, flops, limit=SMALL, scratch=(),
         aliases=None):
    return pl.pallas_call(
        body,
        name=name,
        in_specs=in_specs,
        out_specs=out_specs,
        out_shape=out_shape,
        scratch_shapes=scratch,
        input_output_aliases=aliases or {},
        compiler_params=pltpu.CompilerParams(vmem_limit_bytes=limit),
        cost_estimate=pl.CostEstimate(flops=flops, bytes_accessed=1 << 20, transcendentals=0),
    )(*args)


def swap(value, moves, sizes):
    dp, point = sizes
    pairs = []
    for d in range(dp):
        for p in range(point):
            other_d, other_p = moves(d, p)
            pairs.append((d * point + p, other_d * point + other_p))
    return lax.ppermute(value, ("dp", "point"), pairs)


def bits(count):
    return [1 << i for i in range(count.bit_length() - 1)]


def tie(*values):
    return lax.optimization_barrier(values)


def flips(axes):
    def moves(d, p):
        axis, bit = axes[d & 1]
        return (d, p ^ bit) if axis else (d ^ bit, p)

    return moves


CORES = ((0, 1), (0, 1))


def paired(axes):
    turned = list(axes)
    for i in range(0, len(axes) - 1, 2):
        turned[i], turned[i + 1] = axes[i + 1], axes[i]
    return list(zip(axes, turned))


def point_steps(sizes):
    masks = bits(sizes[1])
    groups = [[bit] for bit in masks[:-2]]
    groups.append([masks[-2], masks[-1], masks[-2] | masks[-1]] if len(masks) > 1 else masks)

    def step(group):
        def run(value):
            parts = [swap(value, flips(((1, mask),) * 2), sizes) for mask in group]
            if len(parts) == 1:
                return value + parts[0]
            return (value + parts[0]) + (parts[1] + parts[2])
        return run

    return [step(group) for group in groups]


def all_axes(sizes):
    return paired(
        [(1, 1)] + [(0, b) for b in bits(sizes[0])[1:]] + [(1, b) for b in bits(sizes[1])[1:]]
    )


def quarter_steps(sizes):
    group = [lambda d, p: (d ^ 2, p), lambda d, p: (d, p ^ 1), lambda d, p: (d ^ 2, p ^ 1)]
    others = paired([(0, b) for b in bits(sizes[0])[2:]] + [(1, b) for b in bits(sizes[1])[1:]])

    def cores(value):
        received = swap(value[1], flips(CORES), sizes)
        part = (value[0].shape[0] // 4, value[0].shape[1])
        return call(
            add_quarter_kernel, "add_quarter", [VMEM] * 2, [VMEM] * 4,
            [jax.ShapeDtypeStruct(part, F32)] * 4, (value[0], received), received.size,
        )

    def scatter(value):
        parts = [swap(part, moves, sizes) for part, moves in zip(value[1:], group)]
        return (value[0] + parts[0]) + (parts[1] + parts[2])

    def add(axes):
        return lambda value: value + swap(value, flips(axes), sizes)

    def gather(value):
        return jnp.concatenate([value] + [swap(value, moves, sizes) for moves in group], axis=0)

    def last(value):
        return value, swap(value, flips(CORES), sizes)

    return [cores, scatter] + [add(axes) for axes in others] + [gather, last]


def all_steps(sizes, scatters):
    if scatters == 0:
        return quarter_steps(sizes)
    steps_axes = all_axes(sizes)

    def add_halve(i, mine, received):
        half = (mine.shape[0] // 2, mine.shape[1])
        return call(
            functools.partial(add_halve_kernel, steps_axes[i]), "add_halve", [VMEM] * 2,
            [VMEM] * 2, [jax.ShapeDtypeStruct(half, F32)] * 2, (mine, received), mine.size,
        )

    def cores(value):
        return add_halve(0, value[0], swap(value[1], flips(CORES), sizes))

    def scatter(i):
        def step(value):
            received = swap(value[1], flips(steps_axes[i]), sizes)
            if i + 1 < scatters:
                return add_halve(i + 1, value[0], received)
            return value[0] + received
        return step

    def add(i):
        return lambda value: value + swap(value, flips(steps_axes[i]), sizes)

    def gather(i):
        return lambda value: jnp.concatenate(
            [value, swap(value, flips(steps_axes[i]), sizes)], axis=0
        )

    def last(value):
        return value, swap(value, flips(CORES), sizes)

    return (
        [cores] + [scatter(i) for i in range(scatters)]
        + [add(i) for i in range(scatters, len(steps_axes))]
        + [gather(i) for i in reversed(range(scatters))] + [last]
    )


def shards(
    sizes,
    inputs, cotangent, gain_one, fx_weight, x_weight, slice_logit_weight, temper,
    slice_query_matrix, slice_key_matrix, slice_value_matrix, out_weight, gain_two,
    expand_weight, down_weight,
):
    points, width = inputs.shape[1:]
    head_size, slices = slice_logit_weight.shape
    heads = temper.shape[0]
    total = heads * slices
    gain_one, gain_two = gain_one[None], gain_two[None]
    factor = 1.0 / math.sqrt(points * sizes[0] * sizes[1])
    axes = all_axes(sizes)

    def shape(*dims, dtype=F32):
        return jax.ShapeDtypeStruct(dims, dtype)

    def pair(*dims):
        return [shape(*dims, dtype=BF16)] * 2

    dense = 6 * points * width * width
    pinned = [
        pltpu.with_memory_space_constraint(array, pltpu.HBM)
        for array in (inputs, gain_one, fx_weight, x_weight, slice_logit_weight, temper)
    ]
    front, front_wide, sums = call(
        front_kernel, "front", [HBM] * 6, [VMEM] * 3,
        [shape(2 * total + 8 * width, points, dtype=BF16), shape(width + 8 + heads, points),
         shape(total // 128 * head_size + 8, 128)],
        pinned,
        4 * dense,
        FRONT_LIMIT,
        [
            pltpu.VMEM(inputs.shape, F32), pltpu.VMEM((1, width), F32),
            pltpu.VMEM((width, width), F32), pltpu.VMEM((width, width), F32),
            pltpu.VMEM((head_size, slices), F32), pltpu.SMEM((heads,), F32),
            pltpu.SemaphoreType.DMA((6,)),
        ],
    )
    sums, cotangent, out_weight, gain_two, expand_weight, down_weight = tie(
        sums, cotangent, out_weight, gain_two, expand_weight, down_weight
    )
    columns, maps = call(
        ready_kernel, "ready", [VMEM] * 9, [VMEM] * 2,
        [shape(2 * width, points),
         shape(8 * width + (2 * GROUP + 8) * head_size, width, dtype=BF16)],
        (cotangent, out_weight, gain_two, expand_weight, down_weight, slice_query_matrix,
         slice_key_matrix, slice_value_matrix, slice_logit_weight),
        2 * dense,
    )
    for step in point_steps(sizes):
        sums = step(sums)
    out_sum, back, back_wide = call(
        functools.partial(back_kernel, head_size, slices), "back", [VMEM] * 5, [VMEM] * 3,
        [shape(head_size, total), shape(12 * width, points, dtype=BF16),
         shape(width + 5 * head_size + SIDE * slices + 8, points)],
        (sums, front, front_wide, columns, maps),
        6 * dense,
    )
    early_value = call(
        functools.partial(early_kernel, factor), "early", [VMEM] * 2, [VMEM] * 2,
        [shape(3 * width // 2, width)] * 2, (columns, back), 3 * dense,
        scratch=[pltpu.VMEM((3 * width, width), F32)],
    )
    behind = [early_value]
    for step in all_steps(sizes, EARLY):
        behind.append(step(behind[-1]))
    order = [None, 2]
    for i, step in enumerate(reversed(point_steps(sizes))):
        out_sum = step(out_sum)
        if i < len(order) and order[i] is not None:
            out_sum, _ = tie(out_sum, behind[order[i]])
    rows = -(-(2 * width + head_size) // 64) * 64
    mine, other, end = call(
        functools.partial(end_kernel, factor, factor / sizes[1], head_size, slices), "end",
        [VMEM] * 6, [VMEM] * 3,
        [shape(rows // 2, width)] * 2 + [shape(4 * width, points, dtype=BF16)],
        (out_sum, front, front_wide, maps, back, back_wide),
        8 * dense,
        scratch=[pltpu.VMEM((rows, width), F32)],
    )
    late, _ = tie((mine, other), behind[2])
    input_grad = call(
        rows_kernel, "rows", [VMEM] * 4, VMEM, shape(1, points, width),
        (front, front_wide, back_wide, end), 2 * dense,
    )
    steps = all_steps(sizes, LATE)
    for i, step in enumerate(steps):
        late = step(late)
        if i == 0:
            late, input_grad = tie(late, input_grad)
    matrices, gain_row = call(
        functools.partial(early_out_kernel, tuple(axes[:EARLY])), "early_out", [VMEM] * 4, [HBM, VMEM],
        [shape(5, width, width), shape(1, width)],
        (*behind[-1], gain_two, expand_weight),
        dense // 8,
        scratch=[pltpu.VMEM((3 * width, width), F32), pltpu.VMEM((width, width), F32),
                 pltpu.SemaphoreType.DMA((3,))],
    )
    matrices, map_grads, logit_grad, gains = call(
        functools.partial(late_out_kernel, tuple(axes[:LATE])), "late_out", [VMEM] * 6 + [HBM],
        [HBM] * 4,
        [shape(5, width, width), shape(3, head_size, head_size), shape(head_size, slices),
         shape(2, width)],
        (*late, gain_one, fx_weight, x_weight, gain_row, matrices),
        dense // 8,
        scratch=[pltpu.VMEM((rows, width), F32), pltpu.VMEM((2, width, width), F32),
                 pltpu.VMEM((3, head_size, head_size), F32), pltpu.VMEM((head_size, slices), F32),
                 pltpu.VMEM((2, width), F32), pltpu.SemaphoreType.DMA((5,))],
        aliases={6: 0},
    )
    return input_grad, matrices, map_grads, logit_grad, gains


def solution(mesh):
    sizes = (mesh.shape["dp"], mesh.shape["point"])
    placed = (P("dp", "point", None),) * 2 + (P(),) * 12
    return jax.shard_map(
        functools.partial(shards, sizes),
        mesh=mesh,
        in_specs=placed,
        out_specs=(P("dp", "point", None), P(), P(), P(), P()),
        check_vma=False,
    )
```

```python
import functools
import math

import jax
import jax.numpy as jnp
from jax import lax
from jax.experimental import pallas as pl
from jax.experimental.pallas import tpu as pltpu
from jax.sharding import PartitionSpec as P

F32 = jnp.float32
BF16 = jnp.bfloat16
GROUP = 4
EPS = 1e-05
EARLY = 0
LATE = 0
SIDE = 4
GELU_A = math.sqrt(2.0 / math.pi)
GELU_B = 0.044715
SMALL = 16 * 1024 * 1024
FRONT_LIMIT = 16 * 1024 * 1024


def split(value):
    high = value.astype(BF16)
    return high, (value - high.astype(F32)).astype(BF16)


def product(left, right, left_dim, right_dim):
    def one(a, b):
        return lax.dot_general(
            a, b, (((left_dim,), (right_dim,)), ((), ())), preferred_element_type=F32
        )

    if left[0].shape[left_dim] % 128 == 0 or left_dim == right_dim == 0:
        return one(
            jnp.concatenate([left[0], left[0], left[1]], axis=left_dim),
            jnp.concatenate([right[0], right[1], right[0]], axis=right_dim),
        )
    return one(left[0], right[0]) + (one(left[0], right[1]) + one(left[1], right[0]))


def rows_of(pair, start, size):
    return pair[0][start : start + size], pair[1][start : start + size]


def stacked(first, second, axis=0):
    return tuple(jnp.concatenate([a, b], axis=axis) for a, b in zip(first, second))


def column(row):
    wide = jnp.broadcast_to(row, (8, row.shape[1]))
    return wide.T[:, 0:1]


def head_mask(head_size, slices):
    shape = (GROUP * head_size, GROUP * slices)
    row = lax.broadcasted_iota(jnp.int32, shape, 0) // head_size
    lane = lax.broadcasted_iota(jnp.int32, shape, 1) // slices
    return row == lane


def spread_blocks(value, mask):
    return jnp.where(mask, jnp.concatenate([value] * GROUP, axis=0), 0.0)


def fold_blocks(value, mask, head_size):
    kept = jnp.where(mask, value, 0.0)
    total = kept[:head_size]
    for i in range(1, GROUP):
        total = total + kept[i * head_size : (i + 1) * head_size]
    return total


def standardise(columns):
    centre = columns - jnp.mean(columns, axis=0, keepdims=True)
    rstd = lax.rsqrt(jnp.mean(centre * centre, axis=0, keepdims=True) + EPS)
    return centre * rstd, rstd


def standardise_pull(grad, hat, rstd):
    first = jnp.mean(grad, axis=0, keepdims=True)
    second = jnp.mean(grad * hat, axis=0, keepdims=True)
    return rstd * (grad - first - hat * second)


def row_total(left, right):
    value = split(left * right)
    ones = jnp.ones((16, left.shape[1]), BF16)
    nt = (((1,), (1,)), ((), ()))
    total = lax.dot_general(ones, value[0], nt, preferred_element_type=F32)
    total = total + lax.dot_general(ones, value[1], nt, preferred_element_type=F32)
    return total[0:1]


def fetch(sources, targets, sems):
    copies = [
        pltpu.make_async_copy(source, target, sems.at[i])
        for i, (source, target) in enumerate(zip(sources, targets))
    ]
    for copy in copies:
        copy.start()
    return copies


def views(ref, *sizes):
    result, start = [], 0
    for size in sizes:
        result.append(ref.at[start : start + size])
        start += size
    return result


def front_kernel(
    x_hbm, gain_hbm, fx_hbm, xw_hbm, logit_hbm, temper_hbm,
    packed, wide_packed, sums,
    x, gain, fx_weight, x_weight, logit_weight, temper, sems,
):
    sources = (x_hbm, gain_hbm, fx_hbm, xw_hbm, logit_hbm, temper_hbm)
    targets = (x, gain, fx_weight, x_weight, logit_weight, temper)
    width, total = x.shape[2], packed.shape[1]
    weight_h, weight_l, fx_h, fx_l, assign_h, assign_l, hat_h, hat_l, both_h, both_l = views(
        packed, *[total] * 2, *[width] * 8
    )
    x_t, rstd_rows, temper_rows = views(wide_packed, width, 8, temper.shape[0])
    copies = fetch(sources, targets, sems)
    sums[sums.shape[0] - 8 :] = jnp.zeros((8, 128), F32)
    head_size, slices = logit_weight.shape
    heads = temper.shape[0]
    points = x.shape[1]
    width = x.shape[2]
    copies[0].wait()
    columns = x[0].T
    x_t[...] = columns
    hat, rstd = standardise(columns)
    rstd_rows[...] = jnp.broadcast_to(rstd, (8, points))
    hat = split(hat)
    hat_h[...], hat_l[...] = hat
    for copy in copies[1:]:
        copy.wait()
    both = jnp.concatenate([fx_weight[...], x_weight[...]], axis=1)
    both = split(both * column(gain[...]))
    both_h[...], both_l[...] = both
    projected = split(product(both, hat, 0, 0))
    fx = rows_of(projected, 0, width)
    assign = rows_of(projected, width, width)
    fx_h[...], fx_l[...] = fx
    assign_h[...], assign_l[...] = assign
    mask = head_mask(head_size, slices)
    wide = jnp.concatenate([logit_weight[...]] * GROUP, axis=1)
    logit_blocks = split(spread_blocks(wide, mask))
    ones = jnp.ones((16, points), BF16)
    blocks = total // 128
    for g in range(heads // GROUP):
        rows = GROUP * head_size
        logits = product(logit_blocks, rows_of(assign, g * rows, rows), 0, 0)
        parts = []
        for i in range(GROUP):
            head = g * GROUP + i
            scale = jnp.full((1, points), temper[head], F32)
            temper_rows[head : head + 1] = scale
            scaled = logits[i * slices : (i + 1) * slices] / scale
            scaled = scaled - jnp.max(scaled, axis=0, keepdims=True)
            grown = jnp.exp(scaled)
            parts.append(grown / jnp.sum(grown, axis=0, keepdims=True))
        weights = split(jnp.concatenate(parts, axis=0))
        span = slice(g * GROUP * slices, (g + 1) * GROUP * slices)
        weight_h[span], weight_l[span] = weights
        num = product(rows_of(fx, g * rows, rows), weights, 1, 1)
        num = fold_blocks(num, mask, head_size)
        nt = (((1,), (1,)), ((), ()))
        den = lax.dot_general(ones, weights[0], nt, preferred_element_type=F32)
        den = den + lax.dot_general(ones, weights[1], nt, preferred_element_type=F32)
        for i in range(num.shape[1] // 128):
            j = g * (num.shape[1] // 128) + i
            lanes = slice(i * 128, (i + 1) * 128)
            sums[j * head_size : (j + 1) * head_size] = num[:, lanes]
            row = blocks * head_size + j
            sums[row : row + 1] = den[0:1, lanes]


def map_views(packed, width, head_size, slices):
    views_of = views(
        packed, *[width] * 8, *[GROUP * head_size] * 2, *[3 * head_size] * 2, *[head_size] * 2
    )
    maps_t = [ref.at[:, 0:head_size] for ref in views_of[10:12]]
    maps = [ref.at[:, 0 : 3 * head_size] for ref in views_of[12:14]]
    logits = [ref.at[:, 0 : GROUP * slices] for ref in views_of[8:10]]
    return views_of[:8], logits, maps_t, maps


def ready_kernel(
    cotangent, out_weight, gain, expand_weight, down_weight, query, key, value, logit_weight,
    columns_packed, packed,
):
    width = cotangent.shape[2]
    head_size, slices = logit_weight.shape
    cot_t, hidden_grad = views(columns_packed, width, width)
    (out_h, out_l, out_t_h, out_t_l, expand_h, expand_l, expand_t_h, expand_t_l), logits, maps_t, maps = (
        map_views(packed, width, head_size, slices)
    )
    columns = cotangent[0].T
    cot_t[...] = columns
    hidden_grad[...] = product(split(down_weight[...]), split(columns), 1, 0)
    out_h[...], out_l[...] = split(out_weight[...])
    out_t_h[...], out_t_l[...] = split(out_weight[...].T)
    expand = expand_weight[...] * column(gain[...])
    expand_h[...], expand_l[...] = split(expand)
    expand_t_h[...], expand_t_l[...] = split(expand.T)
    both = jnp.concatenate([query[...], key[...], value[...]], axis=1)
    maps_t[0][...], maps_t[1][...] = split(both.T)
    maps[0][...], maps[1][...] = split(both)
    wide = jnp.concatenate([logit_weight[...]] * GROUP, axis=1)
    logits[0][...], logits[1][...] = split(spread_blocks(wide, head_mask(head_size, slices)))


def back_views(packed, wide_packed, width, head_size, slices):
    return views(packed, *[width] * 12) + views(
        wide_packed, width, 5 * head_size, SIDE * slices, 8
    )


def back_kernel(
    head_size, slices,
    sums, front, front_wide, columns_packed, map_packed,
    out_sum, packed, wide_packed,
):
    total = front.shape[1]
    heads = total // slices
    width = (wide_packed.shape[0] - 8) - 5 * head_size - SIDE * slices
    weight_h, weight_l = views(front, total, total)
    x_t = front_wide.at[0:width]
    cot_t, hidden_grad = views(columns_packed, width, width)
    (out_h, out_l, out_t_h, out_t_l, expand_h, expand_l, expand_t_h, expand_t_l), _, maps_t, _ = (
        map_views(map_packed, width, head_size, slices)
    )
    maps_h, maps_l = maps_t
    (spread_grad_h, spread_grad_l, spread_h, spread_l, hat_h, hat_l, before_grad_h, before_grad_l,
     hidden_h, hidden_l, grad_h, grad_l, mixed_grad, middle, attn, denom_rows) = back_views(
        packed, wide_packed, width, head_size, slices
    )
    rows, lanes = GROUP * head_size, GROUP * slices
    blocks = total // 128
    ends = [blocks * head_size + j for j in range(blocks)]
    denom = jnp.concatenate([sums[end : end + 1] for end in ends], axis=1) + EPS
    nums = [sums[j * head_size : (j + 1) * head_size] for j in range(blocks)]
    denom_rows[...] = jnp.broadcast_to(denom, (8, total))
    tokens = jnp.concatenate(nums, axis=1) / denom
    qkv = product((maps_h[...], maps_l[...]), split(tokens), 1, 0)
    qkv_pair = split(qkv)
    wide = SIDE * slices
    same = (lax.broadcasted_iota(jnp.int32, (wide, wide), 0) // slices) == (
        lax.broadcasted_iota(jnp.int32, (wide, wide), 1) // slices
    )
    results = []
    for pair in range(heads // SIDE):
        span = slice(pair * wide, (pair + 1) * wide)
        q = tuple(a[0:head_size, span] for a in qkv_pair)
        k = tuple(a[head_size : 2 * head_size, span] for a in qkv_pair)
        v = tuple(a[2 * head_size :, span] for a in qkv_pair)
        scores = product(k, q, 0, 0) * head_size ** (-0.5)
        scores = jnp.where(same, scores, -1e30)
        scores = scores - jnp.max(scores, axis=0, keepdims=True)
        grown = jnp.where(same, jnp.exp(scores), 0.0)
        probs = grown / jnp.sum(grown, axis=0, keepdims=True)
        attn[:, span] = probs
        results.append(product(v, split(probs), 1, 0))
    result = jnp.concatenate(results, axis=1)
    middle[0:head_size] = tokens
    middle[head_size : 4 * head_size] = qkv
    middle[4 * head_size : 5 * head_size] = result
    mask = head_mask(head_size, slices)
    spread = []
    for g in range(heads // GROUP):
        span = slice(g * lanes, (g + 1) * lanes)
        blocks = split(spread_blocks(result[:, span], mask))
        spread.append(product(blocks, (weight_h[span], weight_l[span]), 1, 0))
    spread = split(jnp.concatenate(spread, axis=0))
    spread_h[...], spread_l[...] = spread
    mixed = x_t[...] + product((out_t_h[...], out_t_l[...]), spread, 1, 0)
    hat, rstd = standardise(mixed)
    hat_pair = split(hat)
    hat_h[...], hat_l[...] = hat_pair
    before = product((expand_t_h[...], expand_t_l[...]), hat_pair, 1, 0)
    square = before * before
    bent = jnp.tanh(GELU_A * (before + GELU_B * before * square))
    half = 0.5 * (1.0 + bent)
    hidden_h[...], hidden_l[...] = split(before * half)
    slope = half + 0.5 * before * (1.0 - bent * bent) * (GELU_A * (1.0 + 3.0 * GELU_B * square))
    before_grad = split(hidden_grad[...] * slope)
    before_grad_h[...], before_grad_l[...] = before_grad
    hat_grad = product((expand_h[...], expand_l[...]), before_grad, 1, 0)
    grad = cot_t[...] + standardise_pull(hat_grad, hat, rstd)
    mixed_grad[...] = grad
    grad_pair = split(grad)
    grad_h[...], grad_l[...] = grad_pair
    spread_grad = split(product((out_h[...], out_l[...]), grad_pair, 1, 0))
    spread_grad_h[...], spread_grad_l[...] = spread_grad
    sums_out = []
    for g in range(heads // GROUP):
        span = slice(g * lanes, (g + 1) * lanes)
        full = product(
            rows_of(spread_grad, g * rows, rows), (weight_h[span], weight_l[span]), 1, 1
        )
        sums_out.append(fold_blocks(full, mask, head_size))
    out_sum[...] = jnp.concatenate(sums_out, axis=1)


def place(axes):
    d, p = lax.axis_index("dp"), lax.axis_index("point")
    halves = [lax.rem((p if axis else d) // bit, 2) for axis, bit in axes]
    first = lax.rem(d, 2) == 0
    return jnp.where(first, *halves), jnp.where(first, *halves[::-1])


def block(ref, index, size):
    return ref.at[pl.ds(pl.multiple_of(index * size, 8), size)]


def store_halves(value, mine, other):
    half = mine.shape[0]
    core = lax.rem(lax.axis_index("dp"), 2)
    mine[...] = block(value, core, half)[...]
    other[...] = block(value, 1 - core, half)[...]


def quarter():
    return 2 * lax.rem(lax.axis_index("point"), 2) + lax.rem(lax.axis_index("dp") // 2, 2)


def add_quarter_kernel(mine, received, *parts):
    size = parts[0].shape[0]
    for i, part in enumerate(parts):
        index = quarter() ^ i
        part[...] = block(mine, index, size)[...] + block(received, index, size)[...]


def arrange_quarters(own, partner, result):
    core = lax.rem(lax.axis_index("dp"), 2)
    size = own.shape[0] // 4
    for side, ref in ((core, own), (1 - core, partner)):
        for i in range(4):
            block(result, 4 * side + (quarter() ^ i), size)[...] = ref[i * size : (i + 1) * size]


def add_halve_kernel(axes, mine, received, kept, sent):
    half = kept.shape[0]
    upper, _ = place(axes)
    kept[...] = block(mine, upper, half)[...] + block(received, upper, half)[...]
    sent[...] = block(mine, 1 - upper, half)[...] + block(received, 1 - upper, half)[...]


def arrange(levels, own, partner, result):
    if not levels:
        return arrange_quarters(own, partner, result)
    core = lax.rem(lax.axis_index("dp"), 2)
    count = 1 << len(levels)
    size = own.shape[0] // count
    for side, ref in enumerate((own, partner)):
        uppers = [place(axes)[side] for axes in levels]
        for i in range(count):
            index = core if side == 0 else 1 - core
            for level, upper in enumerate(uppers):
                same = (i >> (len(levels) - 1 - level)) & 1 == 0
                index = 2 * index + (upper if same else 1 - upper)
            block(result, index, size)[...] = ref[i * size : (i + 1) * size]


def early_kernel(factor, columns_packed, packed, mine, other, early):
    width = early.shape[1]
    pieces = [ref[...] for ref in views(packed, *[width] * 12)[2:]]
    spread, hat, before_grad, hidden, grad = (pieces[i : i + 2] for i in range(0, 10, 2))
    early[0:width] = product(spread, grad, 1, 1) * factor
    early[width : 2 * width] = product(hat, before_grad, 1, 1) * factor
    early[2 * width :] = product(hidden, split(columns_packed[0:width]), 1, 1) * factor
    store_halves(early, mine, other)


def end_kernel(
    factor, middle_factor, head_size, slices,
    out_sum, front, front_wide, map_packed, back, back_wide,
    late_mine, late_other, packed,
    late,
):
    width = late.shape[1]
    points = front.shape[1]
    total = out_sum.shape[1]
    heads = total // slices
    weight_h, weight_l, fx_h, fx_l, assign_h, assign_l, hat_h, hat_l = views(
        front, *[total] * 2, *[width] * 6
    )
    temper_rows = front_wide.at[width + 8 : width + 8 + heads]
    both_grad_h, both_grad_l = views(packed, 2 * width, 2 * width)
    _, logit_maps, _, maps = map_views(map_packed, width, head_size, slices)
    spread_grad_h, spread_grad_l, *_, middle, attn, denom_rows = back_views(
        back, back_wide, width, head_size, slices
    )
    rows, lanes = GROUP * head_size, GROUP * slices
    tokens = middle[0:head_size]
    qkv_pair = split(middle[head_size : 4 * head_size])
    result = middle[4 * head_size : 5 * head_size]
    result_grad = split(out_sum[...])
    wide = SIDE * slices
    parts = []
    for pair in range(heads // SIDE):
        span = slice(pair * wide, (pair + 1) * wide)
        q = tuple(a[0:head_size, span] for a in qkv_pair)
        k = tuple(a[head_size : 2 * head_size, span] for a in qkv_pair)
        v = tuple(a[2 * head_size :, span] for a in qkv_pair)
        probs = attn[:, span]
        grad = tuple(a[:, span] for a in result_grad)
        value_grad = product(grad, split(probs), 1, 1)
        probs_grad = product(v, grad, 0, 0)
        weighted = probs * probs_grad
        total = jnp.sum(weighted, axis=0, keepdims=True)
        score_grad = split((weighted - probs * total) * head_size ** (-0.5))
        query_grad = product(k, score_grad, 1, 0)
        key_grad = product(q, score_grad, 1, 1)
        parts.append(jnp.concatenate([query_grad, key_grad, value_grad], axis=0))
    qkv_grad = split(jnp.concatenate(parts, axis=1))
    maps = (maps[0][...], maps[1][...])
    map_grad = product(split(tokens), qkv_grad, 1, 1)
    denom = denom_rows[0:1]
    num_grad = product(maps, qkv_grad, 1, 0) / denom
    den_grad = column(-jnp.sum(num_grad * tokens, axis=0, keepdims=True))
    mask = head_mask(head_size, slices)
    logit_blocks = (logit_maps[0][...], logit_maps[1][...])
    fx_grads, assign_grads = [], []
    logit_grad = jnp.zeros((head_size, lanes), F32)
    for g in range(heads // GROUP):
        span = slice(g * lanes, (g + 1) * lanes)
        piece = slice(g * rows, (g + 1) * rows)
        num_blocks = split(spread_blocks(num_grad[:, span], mask))
        result_blocks = split(spread_blocks(result[:, span], mask))
        weights = (weight_h[span], weight_l[span])
        fx_grads.append(product(num_blocks, weights, 1, 0))
        weight_grad = product(
            stacked(num_blocks, result_blocks),
            stacked(
                (fx_h[piece], fx_l[piece]), (spread_grad_h[piece], spread_grad_l[piece])
            ),
            0,
            0,
        )
        weight_grad = weight_grad + den_grad[span]
        grads = []
        for i in range(GROUP):
            block = slice(i * slices, (i + 1) * slices)
            head = g * GROUP + i
            scale = temper_rows[head : head + 1]
            w = weights[0][block].astype(F32) + weights[1][block].astype(F32)
            weighted = w * weight_grad[block]
            total = jnp.sum(weighted, axis=0, keepdims=True)
            grads.append((weighted - w * total) / scale)
        grads = split(jnp.concatenate(grads, axis=0))
        assign_grads.append(product(logit_blocks, grads, 1, 0))
        full = product((assign_h[piece], assign_l[piece]), grads, 1, 1)
        logit_grad = logit_grad + fold_blocks(full, mask, head_size)
    both_grad = split(jnp.concatenate(fx_grads + assign_grads, axis=0))
    both_grad_h[...], both_grad_l[...] = both_grad
    matrix = product((hat_h[...], hat_l[...]), both_grad, 1, 1) * factor
    late[0:width] = matrix[:, :width]
    late[width : 2 * width] = matrix[:, width:]
    logit_grad = logit_grad[:, : 2 * slices] + logit_grad[:, 2 * slices :]
    logit_grad = logit_grad[:, :slices] + logit_grad[:, slices:]
    base = 2 * width
    late[base:] = jnp.zeros((late.shape[0] - base, width), F32)
    late[base : base + head_size, 0 : 3 * head_size] = map_grad * middle_factor
    late[base : base + head_size, 128 : 128 + slices] = logit_grad * factor
    store_halves(late, late_mine, late_other)


def rows_kernel(front, front_wide, back_wide, end, x_grad):
    width = x_grad.shape[2]
    total = front.shape[1]
    _, hat_h, hat_l, both_h, both_l = views(front, 2 * total + 4 * width, *[width] * 4)
    rstd = front_wide[width : width + 1]
    grads = [ref[...] for ref in views(end, 2 * width, 2 * width)]
    hat_grad = product((both_h[...], both_l[...]), grads, 1, 0)
    hat = hat_h[...].astype(F32) + hat_l[...].astype(F32)
    x_grad[0] = (back_wide[0:width] + standardise_pull(hat_grad, hat, rstd)).T


def early_out_kernel(
    levels,
    own, partner, gain, expand_weight,
    matrices, gain_row,
    early, scaled, sems,
):
    arrange(levels, own, partner, early)
    width = gain.shape[1]
    copies = [
        pltpu.make_async_copy(early.at[0:width], matrices.at[2], sems.at[0]),
        pltpu.make_async_copy(early.at[2 * width : 3 * width], matrices.at[4], sems.at[1]),
        pltpu.make_async_copy(scaled, matrices.at[3], sems.at[2]),
    ]
    copies[0].start()
    copies[1].start()
    grad = early[width : 2 * width]
    scaled[...] = grad * column(gain[...])
    copies[2].start()
    gain_row[...] = row_total(grad, expand_weight[...])
    for copy in copies:
        copy.wait()


def late_out_kernel(
    levels,
    own, partner, gain, fx_weight, x_weight, gain_row, given,
    matrices, maps_out, logit_out, gains_out,
    late, scaled, maps, logit, gains, sems,
):
    arrange(levels, own, partner, late)
    width = gain.shape[1]
    head_size, slices = logit.shape
    base = 2 * width
    for i in range(3):
        maps[i] = late[base : base + head_size, i * head_size : (i + 1) * head_size]
    logit[...] = late[base : base + head_size, 128 : 128 + slices]
    copies = fetch((maps, logit), (maps_out, logit_out), sems)
    gain_column = column(gain[...])
    total = jnp.zeros((1, width), F32)
    for i, weight in enumerate((fx_weight, x_weight)):
        scaled[i] = late[i * width : (i + 1) * width] * gain_column
        copy = pltpu.make_async_copy(scaled.at[i], matrices.at[i], sems.at[2 + i])
        copy.start()
        copies.append(copy)
    for i, weight in enumerate((fx_weight, x_weight)):
        total = total + row_total(late[i * width : (i + 1) * width], weight[...])
    gains[...] = jnp.concatenate([total, gain_row[...]], axis=0)
    copies.append(pltpu.make_async_copy(gains, gains_out, sems.at[4]))
    copies[-1].start()
    for copy in copies:
        copy.wait()


VMEM = pl.BlockSpec(memory_space=pltpu.VMEM)
SMEM = pl.BlockSpec(memory_space=pltpu.SMEM)


HBM = pl.BlockSpec(memory_space=pltpu.HBM)


def call(body, name, in_specs, out_specs, out_shape, args, flops, limit=SMALL, scratch=(),
         aliases=None):
    return pl.pallas_call(
        body,
        name=name,
        in_specs=in_specs,
        out_specs=out_specs,
        out_shape=out_shape,
        scratch_shapes=scratch,
        input_output_aliases=aliases or {},
        compiler_params=pltpu.CompilerParams(vmem_limit_bytes=limit),
        cost_estimate=pl.CostEstimate(flops=flops, bytes_accessed=1 << 20, transcendentals=0),
    )(*args)


def swap(value, moves, sizes):
    dp, point = sizes
    pairs = []
    for d in range(dp):
        for p in range(point):
            other_d, other_p = moves(d, p)
            pairs.append((d * point + p, other_d * point + other_p))
    return lax.ppermute(value, ("dp", "point"), pairs)


def bits(count):
    return [1 << i for i in range(count.bit_length() - 1)]


def tie(*values):
    return lax.optimization_barrier(values)


def flips(axes):
    def moves(d, p):
        axis, bit = axes[d & 1]
        return (d, p ^ bit) if axis else (d ^ bit, p)

    return moves


CORES = ((0, 1), (0, 1))


def paired(axes):
    turned = list(axes)
    for i in range(0, len(axes) - 1, 2):
        turned[i], turned[i + 1] = axes[i + 1], axes[i]
    return list(zip(axes, turned))


def direct_steps(masks, sizes):
    groups = [[mask] for mask in masks[:-2]]
    if len(masks) > 1:
        groups.append([masks[-2], masks[-1], masks[-2] | masks[-1]])
    elif masks:
        groups.append([masks[-1]])

    def step(group):
        def run(value):
            parts = [swap(value, flips(((1, mask),) * 2), sizes) for mask in group]
            if len(parts) == 1:
                return value + parts[0]
            return (value + parts[0]) + (parts[1] + parts[2])
        return run

    return [step(group) for group in groups]


def point_steps(sizes):
    return direct_steps(bits(sizes[1]), sizes)


def all_axes(sizes):
    return paired(
        [(1, 1)] + [(0, b) for b in bits(sizes[0])[1:]] + [(1, b) for b in bits(sizes[1])[1:]]
    )


def quarter_steps(sizes, direct):
    group = [lambda d, p: (d ^ 2, p), lambda d, p: (d, p ^ 1), lambda d, p: (d ^ 2, p ^ 1)]
    others = paired([(0, b) for b in bits(sizes[0])[2:]] + [(1, b) for b in bits(sizes[1])[1:]])

    def cores(value):
        received = swap(value[1], flips(CORES), sizes)
        part = (value[0].shape[0] // 4, value[0].shape[1])
        return call(
            add_quarter_kernel, "add_quarter", [VMEM] * 2, [VMEM] * 4,
            [jax.ShapeDtypeStruct(part, F32)] * 4, (value[0], received), received.size,
        )

    def scatter(value):
        parts = [swap(part, moves, sizes) for part, moves in zip(value[1:], group)]
        return (value[0] + parts[0]) + (parts[1] + parts[2])

    def add(axes):
        return lambda value: value + swap(value, flips(axes), sizes)

    def gather(value):
        return jnp.concatenate([value] + [swap(value, moves, sizes) for moves in group], axis=0)

    def last(value):
        return value, swap(value, flips(CORES), sizes)

    if direct:
        sums = [add(axes) for axes in paired([(0, b) for b in bits(sizes[0])[2:]])]
        sums += direct_steps(bits(sizes[1])[1:], sizes)
    else:
        sums = [add(axes) for axes in others]
    return [cores, scatter] + sums + [gather, last]


def all_steps(sizes, scatters, direct=False):
    if scatters == 0:
        return quarter_steps(sizes, direct)
    steps_axes = all_axes(sizes)

    def add_halve(i, mine, received):
        half = (mine.shape[0] // 2, mine.shape[1])
        return call(
            functools.partial(add_halve_kernel, steps_axes[i]), "add_halve", [VMEM] * 2,
            [VMEM] * 2, [jax.ShapeDtypeStruct(half, F32)] * 2, (mine, received), mine.size,
        )

    def cores(value):
        return add_halve(0, value[0], swap(value[1], flips(CORES), sizes))

    def scatter(i):
        def step(value):
            received = swap(value[1], flips(steps_axes[i]), sizes)
            if i + 1 < scatters:
                return add_halve(i + 1, value[0], received)
            return value[0] + received
        return step

    def add(i):
        return lambda value: value + swap(value, flips(steps_axes[i]), sizes)

    def gather(i):
        return lambda value: jnp.concatenate(
            [value, swap(value, flips(steps_axes[i]), sizes)], axis=0
        )

    def last(value):
        return value, swap(value, flips(CORES), sizes)

    return (
        [cores] + [scatter(i) for i in range(scatters)]
        + [add(i) for i in range(scatters, len(steps_axes))]
        + [gather(i) for i in reversed(range(scatters))] + [last]
    )


def shards(
    sizes,
    inputs, cotangent, gain_one, fx_weight, x_weight, slice_logit_weight, temper,
    slice_query_matrix, slice_key_matrix, slice_value_matrix, out_weight, gain_two,
    expand_weight, down_weight,
):
    points, width = inputs.shape[1:]
    head_size, slices = slice_logit_weight.shape
    heads = temper.shape[0]
    total = heads * slices
    gain_one, gain_two = gain_one[None], gain_two[None]
    factor = 1.0 / math.sqrt(points * sizes[0] * sizes[1])
    axes = all_axes(sizes)

    def shape(*dims, dtype=F32):
        return jax.ShapeDtypeStruct(dims, dtype)

    def pair(*dims):
        return [shape(*dims, dtype=BF16)] * 2

    dense = 6 * points * width * width
    pinned = [
        pltpu.with_memory_space_constraint(array, pltpu.HBM)
        for array in (inputs, gain_one, fx_weight, x_weight, slice_logit_weight, temper)
    ]
    front, front_wide, sums = call(
        front_kernel, "front", [HBM] * 6, [VMEM] * 3,
        [shape(2 * total + 8 * width, points, dtype=BF16), shape(width + 8 + heads, points),
         shape(total // 128 * head_size + 8, 128)],
        pinned,
        4 * dense,
        FRONT_LIMIT,
        [
            pltpu.VMEM(inputs.shape, F32), pltpu.VMEM((1, width), F32),
            pltpu.VMEM((width, width), F32), pltpu.VMEM((width, width), F32),
            pltpu.VMEM((head_size, slices), F32), pltpu.SMEM((heads,), F32),
            pltpu.SemaphoreType.DMA((6,)),
        ],
    )
    sums, cotangent, out_weight, gain_two, expand_weight, down_weight = tie(
        sums, cotangent, out_weight, gain_two, expand_weight, down_weight
    )
    columns, maps = call(
        ready_kernel, "ready", [VMEM] * 9, [VMEM] * 2,
        [shape(2 * width, points),
         shape(8 * width + (2 * GROUP + 8) * head_size, width, dtype=BF16)],
        (cotangent, out_weight, gain_two, expand_weight, down_weight, slice_query_matrix,
         slice_key_matrix, slice_value_matrix, slice_logit_weight),
        2 * dense,
    )
    for step in point_steps(sizes):
        sums = step(sums)
    out_sum, back, back_wide = call(
        functools.partial(back_kernel, head_size, slices), "back", [VMEM] * 5, [VMEM] * 3,
        [shape(head_size, total), shape(12 * width, points, dtype=BF16),
         shape(width + 5 * head_size + SIDE * slices + 8, points)],
        (sums, front, front_wide, columns, maps),
        6 * dense,
    )
    early_value = call(
        functools.partial(early_kernel, factor), "early", [VMEM] * 2, [VMEM] * 2,
        [shape(3 * width // 2, width)] * 2, (columns, back), 3 * dense,
        scratch=[pltpu.VMEM((3 * width, width), F32)],
    )
    behind = [early_value]
    for step in all_steps(sizes, EARLY):
        behind.append(step(behind[-1]))
    order = [None, 2]
    for i, step in enumerate(reversed(point_steps(sizes))):
        out_sum = step(out_sum)
        if i < len(order) and order[i] is not None:
            out_sum, _ = tie(out_sum, behind[order[i]])
    rows = -(-(2 * width + head_size) // 64) * 64
    mine, other, end = call(
        functools.partial(end_kernel, factor, factor / sizes[1], head_size, slices), "end",
        [VMEM] * 6, [VMEM] * 3,
        [shape(rows // 2, width)] * 2 + [shape(4 * width, points, dtype=BF16)],
        (out_sum, front, front_wide, maps, back, back_wide),
        8 * dense,
        scratch=[pltpu.VMEM((rows, width), F32)],
    )
    late, _ = tie((mine, other), behind[2])
    input_grad = call(
        rows_kernel, "rows", [VMEM] * 4, VMEM, shape(1, points, width),
        (front, front_wide, back_wide, end), 2 * dense,
    )
    steps = all_steps(sizes, LATE, True)
    for i, step in enumerate(steps):
        late = step(late)
        if i == 0:
            late, input_grad = tie(late, input_grad)
    matrices, gain_row = call(
        functools.partial(early_out_kernel, tuple(axes[:EARLY])), "early_out", [VMEM] * 4, [HBM, VMEM],
        [shape(5, width, width), shape(1, width)],
        (*behind[-1], gain_two, expand_weight),
        dense // 8,
        scratch=[pltpu.VMEM((3 * width, width), F32), pltpu.VMEM((width, width), F32),
                 pltpu.SemaphoreType.DMA((3,))],
    )
    matrices, map_grads, logit_grad, gains = call(
        functools.partial(late_out_kernel, tuple(axes[:LATE])), "late_out", [VMEM] * 6 + [HBM],
        [HBM] * 4,
        [shape(5, width, width), shape(3, head_size, head_size), shape(head_size, slices),
         shape(2, width)],
        (*late, gain_one, fx_weight, x_weight, gain_row, matrices),
        dense // 8,
        scratch=[pltpu.VMEM((rows, width), F32), pltpu.VMEM((2, width, width), F32),
                 pltpu.VMEM((3, head_size, head_size), F32), pltpu.VMEM((head_size, slices), F32),
                 pltpu.VMEM((2, width), F32), pltpu.SemaphoreType.DMA((5,))],
        aliases={6: 0},
    )
    return input_grad, matrices, map_grads, logit_grad, gains


def solution(mesh):
    sizes = (mesh.shape["dp"], mesh.shape["point"])
    placed = (P("dp", "point", None),) * 2 + (P(),) * 12
    return jax.shard_map(
        functools.partial(shards, sizes),
        mesh=mesh,
        in_specs=placed,
        out_specs=(P("dp", "point", None), P(), P(), P(), P()),
        check_vma=False,
    )
```

```python
import functools
import math

import jax
import jax.numpy as jnp
from jax import lax
from jax.experimental import pallas as pl
from jax.experimental.pallas import tpu as pltpu
from jax.sharding import PartitionSpec as P

F32 = jnp.float32
BF16 = jnp.bfloat16
GROUP = 4
EPS = 1e-05
EARLY = 0
LATE = 0
SIDE = 4
GELU_A = math.sqrt(2.0 / math.pi)
GELU_B = 0.044715
SMALL = 16 * 1024 * 1024
FRONT_LIMIT = 16 * 1024 * 1024


def split(value):
    high = value.astype(BF16)
    return high, (value - high.astype(F32)).astype(BF16)


def product(left, right, left_dim, right_dim):
    def one(a, b):
        return lax.dot_general(
            a, b, (((left_dim,), (right_dim,)), ((), ())), preferred_element_type=F32
        )

    if left[0].shape[left_dim] % 128 == 0 or left_dim == right_dim == 0:
        return one(
            jnp.concatenate([left[0], left[0], left[1]], axis=left_dim),
            jnp.concatenate([right[0], right[1], right[0]], axis=right_dim),
        )
    return one(left[0], right[0]) + (one(left[0], right[1]) + one(left[1], right[0]))


def rows_of(pair, start, size):
    return pair[0][start : start + size], pair[1][start : start + size]


def stacked(first, second, axis=0):
    return tuple(jnp.concatenate([a, b], axis=axis) for a, b in zip(first, second))


def column(row):
    wide = jnp.broadcast_to(row, (8, row.shape[1]))
    return wide.T[:, 0:1]


def head_mask(head_size, slices):
    shape = (GROUP * head_size, GROUP * slices)
    row = lax.broadcasted_iota(jnp.int32, shape, 0) // head_size
    lane = lax.broadcasted_iota(jnp.int32, shape, 1) // slices
    return row == lane


def spread_blocks(value, mask):
    return jnp.where(mask, jnp.concatenate([value] * GROUP, axis=0), 0.0)


def fold_blocks(value, mask, head_size):
    kept = jnp.where(mask, value, 0.0)
    total = kept[:head_size]
    for i in range(1, GROUP):
        total = total + kept[i * head_size : (i + 1) * head_size]
    return total


def standardise(columns):
    centre = columns - jnp.mean(columns, axis=0, keepdims=True)
    rstd = lax.rsqrt(jnp.mean(centre * centre, axis=0, keepdims=True) + EPS)
    return centre * rstd, rstd


def standardise_pull(grad, hat, rstd):
    first = jnp.mean(grad, axis=0, keepdims=True)
    second = jnp.mean(grad * hat, axis=0, keepdims=True)
    return rstd * (grad - first - hat * second)


def row_total(left, right):
    value = split(left * right)
    ones = jnp.ones((16, left.shape[1]), BF16)
    nt = (((1,), (1,)), ((), ()))
    total = lax.dot_general(ones, value[0], nt, preferred_element_type=F32)
    total = total + lax.dot_general(ones, value[1], nt, preferred_element_type=F32)
    return total[0:1]


def fetch(sources, targets, sems):
    copies = [
        pltpu.make_async_copy(source, target, sems.at[i])
        for i, (source, target) in enumerate(zip(sources, targets))
    ]
    for copy in copies:
        copy.start()
    return copies


def views(ref, *sizes):
    result, start = [], 0
    for size in sizes:
        result.append(ref.at[start : start + size])
        start += size
    return result


def front_kernel(
    x_hbm, gain_hbm, fx_hbm, xw_hbm, logit_hbm, temper_hbm,
    packed, wide_packed, sums,
    x, gain, fx_weight, x_weight, logit_weight, temper, sems,
):
    sources = (x_hbm, gain_hbm, fx_hbm, xw_hbm, logit_hbm, temper_hbm)
    targets = (x, gain, fx_weight, x_weight, logit_weight, temper)
    width, total = x.shape[2], packed.shape[1]
    weight_h, weight_l, fx_h, fx_l, assign_h, assign_l, hat_h, hat_l, both_h, both_l = views(
        packed, *[total] * 2, *[width] * 8
    )
    x_t, rstd_rows, temper_rows = views(wide_packed, width, 8, temper.shape[0])
    copies = fetch(sources, targets, sems)
    sums[sums.shape[0] - 8 :] = jnp.zeros((8, 128), F32)
    head_size, slices = logit_weight.shape
    heads = temper.shape[0]
    points = x.shape[1]
    width = x.shape[2]
    copies[0].wait()
    columns = x[0].T
    x_t[...] = columns
    hat, rstd = standardise(columns)
    rstd_rows[...] = jnp.broadcast_to(rstd, (8, points))
    hat = split(hat)
    hat_h[...], hat_l[...] = hat
    for copy in copies[1:]:
        copy.wait()
    both = jnp.concatenate([fx_weight[...], x_weight[...]], axis=1)
    both = split(both * column(gain[...]))
    both_h[...], both_l[...] = both
    projected = split(product(both, hat, 0, 0))
    fx = rows_of(projected, 0, width)
    assign = rows_of(projected, width, width)
    fx_h[...], fx_l[...] = fx
    assign_h[...], assign_l[...] = assign
    mask = head_mask(head_size, slices)
    wide = jnp.concatenate([logit_weight[...]] * GROUP, axis=1)
    logit_blocks = split(spread_blocks(wide, mask))
    ones = jnp.ones((16, points), BF16)
    blocks = total // 128
    for g in range(heads // GROUP):
        rows = GROUP * head_size
        logits = product(logit_blocks, rows_of(assign, g * rows, rows), 0, 0)
        parts = []
        for i in range(GROUP):
            head = g * GROUP + i
            scale = jnp.full((1, points), temper[head], F32)
            temper_rows[head : head + 1] = scale
            scaled = logits[i * slices : (i + 1) * slices] / scale
            scaled = scaled - jnp.max(scaled, axis=0, keepdims=True)
            grown = jnp.exp(scaled)
            parts.append(grown / jnp.sum(grown, axis=0, keepdims=True))
        weights = split(jnp.concatenate(parts, axis=0))
        span = slice(g * GROUP * slices, (g + 1) * GROUP * slices)
        weight_h[span], weight_l[span] = weights
        num = product(rows_of(fx, g * rows, rows), weights, 1, 1)
        num = fold_blocks(num, mask, head_size)
        nt = (((1,), (1,)), ((), ()))
        den = lax.dot_general(ones, weights[0], nt, preferred_element_type=F32)
        den = den + lax.dot_general(ones, weights[1], nt, preferred_element_type=F32)
        for i in range(num.shape[1] // 128):
            j = g * (num.shape[1] // 128) + i
            lanes = slice(i * 128, (i + 1) * 128)
            sums[j * head_size : (j + 1) * head_size] = num[:, lanes]
            row = blocks * head_size + j
            sums[row : row + 1] = den[0:1, lanes]


def map_views(packed, width, head_size, slices):
    views_of = views(
        packed, *[width] * 8, *[GROUP * head_size] * 2, *[3 * head_size] * 2, *[head_size] * 2
    )
    maps_t = [ref.at[:, 0:head_size] for ref in views_of[10:12]]
    maps = [ref.at[:, 0 : 3 * head_size] for ref in views_of[12:14]]
    logits = [ref.at[:, 0 : GROUP * slices] for ref in views_of[8:10]]
    return views_of[:8], logits, maps_t, maps


def ready_kernel(
    cotangent, out_weight, gain, expand_weight, down_weight, query, key, value, logit_weight,
    columns_packed, packed,
):
    width = cotangent.shape[2]
    head_size, slices = logit_weight.shape
    cot_t, hidden_grad = views(columns_packed, width, width)
    (out_h, out_l, out_t_h, out_t_l, expand_h, expand_l, expand_t_h, expand_t_l), logits, maps_t, maps = (
        map_views(packed, width, head_size, slices)
    )
    columns = cotangent[0].T
    cot_t[...] = columns
    hidden_grad[...] = product(split(down_weight[...]), split(columns), 1, 0)
    out_h[...], out_l[...] = split(out_weight[...])
    out_t_h[...], out_t_l[...] = split(out_weight[...].T)
    expand = expand_weight[...] * column(gain[...])
    expand_h[...], expand_l[...] = split(expand)
    expand_t_h[...], expand_t_l[...] = split(expand.T)
    both = jnp.concatenate([query[...], key[...], value[...]], axis=1)
    maps_t[0][...], maps_t[1][...] = split(both.T)
    maps[0][...], maps[1][...] = split(both)
    wide = jnp.concatenate([logit_weight[...]] * GROUP, axis=1)
    logits[0][...], logits[1][...] = split(spread_blocks(wide, head_mask(head_size, slices)))


def back_views(packed, wide_packed, width, head_size, slices):
    return views(packed, *[width] * 12) + views(
        wide_packed, width, 5 * head_size, SIDE * slices, 8
    )


def back_kernel(
    head_size, slices,
    sums, front, front_wide, columns_packed, map_packed,
    out_sum, packed, wide_packed,
):
    total = front.shape[1]
    heads = total // slices
    width = (wide_packed.shape[0] - 8) - 5 * head_size - SIDE * slices
    weight_h, weight_l = views(front, total, total)
    x_t = front_wide.at[0:width]
    cot_t, hidden_grad = views(columns_packed, width, width)
    (out_h, out_l, out_t_h, out_t_l, expand_h, expand_l, expand_t_h, expand_t_l), _, maps_t, _ = (
        map_views(map_packed, width, head_size, slices)
    )
    maps_h, maps_l = maps_t
    (spread_grad_h, spread_grad_l, spread_h, spread_l, hat_h, hat_l, before_grad_h, before_grad_l,
     hidden_h, hidden_l, grad_h, grad_l, mixed_grad, middle, attn, denom_rows) = back_views(
        packed, wide_packed, width, head_size, slices
    )
    rows, lanes = GROUP * head_size, GROUP * slices
    blocks = total // 128
    ends = [blocks * head_size + j for j in range(blocks)]
    denom = jnp.concatenate([sums[end : end + 1] for end in ends], axis=1) + EPS
    nums = [sums[j * head_size : (j + 1) * head_size] for j in range(blocks)]
    denom_rows[...] = jnp.broadcast_to(denom, (8, total))
    tokens = jnp.concatenate(nums, axis=1) / denom
    qkv = product((maps_h[...], maps_l[...]), split(tokens), 1, 0)
    qkv_pair = split(qkv)
    wide = SIDE * slices
    same = (lax.broadcasted_iota(jnp.int32, (wide, wide), 0) // slices) == (
        lax.broadcasted_iota(jnp.int32, (wide, wide), 1) // slices
    )
    results = []
    for pair in range(heads // SIDE):
        span = slice(pair * wide, (pair + 1) * wide)
        q = tuple(a[0:head_size, span] for a in qkv_pair)
        k = tuple(a[head_size : 2 * head_size, span] for a in qkv_pair)
        v = tuple(a[2 * head_size :, span] for a in qkv_pair)
        scores = product(k, q, 0, 0) * head_size ** (-0.5)
        scores = jnp.where(same, scores, -1e30)
        scores = scores - jnp.max(scores, axis=0, keepdims=True)
        grown = jnp.where(same, jnp.exp(scores), 0.0)
        probs = grown / jnp.sum(grown, axis=0, keepdims=True)
        attn[:, span] = probs
        results.append(product(v, split(probs), 1, 0))
    result = jnp.concatenate(results, axis=1)
    middle[0:head_size] = tokens
    middle[head_size : 4 * head_size] = qkv
    middle[4 * head_size : 5 * head_size] = result
    mask = head_mask(head_size, slices)
    spread = []
    for g in range(heads // GROUP):
        span = slice(g * lanes, (g + 1) * lanes)
        blocks = split(spread_blocks(result[:, span], mask))
        spread.append(product(blocks, (weight_h[span], weight_l[span]), 1, 0))
    spread = split(jnp.concatenate(spread, axis=0))
    spread_h[...], spread_l[...] = spread
    mixed = x_t[...] + product((out_t_h[...], out_t_l[...]), spread, 1, 0)
    hat, rstd = standardise(mixed)
    hat_pair = split(hat)
    hat_h[...], hat_l[...] = hat_pair
    before = product((expand_t_h[...], expand_t_l[...]), hat_pair, 1, 0)
    square = before * before
    bent = jnp.tanh(GELU_A * (before + GELU_B * before * square))
    half = 0.5 * (1.0 + bent)
    hidden_h[...], hidden_l[...] = split(before * half)
    slope = half + 0.5 * before * (1.0 - bent * bent) * (GELU_A * (1.0 + 3.0 * GELU_B * square))
    before_grad = split(hidden_grad[...] * slope)
    before_grad_h[...], before_grad_l[...] = before_grad
    hat_grad = product((expand_h[...], expand_l[...]), before_grad, 1, 0)
    grad = cot_t[...] + standardise_pull(hat_grad, hat, rstd)
    mixed_grad[...] = grad
    grad_pair = split(grad)
    grad_h[...], grad_l[...] = grad_pair
    spread_grad = split(product((out_h[...], out_l[...]), grad_pair, 1, 0))
    spread_grad_h[...], spread_grad_l[...] = spread_grad
    sums_out = []
    for g in range(heads // GROUP):
        span = slice(g * lanes, (g + 1) * lanes)
        full = product(
            rows_of(spread_grad, g * rows, rows), (weight_h[span], weight_l[span]), 1, 1
        )
        sums_out.append(fold_blocks(full, mask, head_size))
    out_sum[...] = jnp.concatenate(sums_out, axis=1)


def place(axes):
    d, p = lax.axis_index("dp"), lax.axis_index("point")
    halves = [lax.rem((p if axis else d) // bit, 2) for axis, bit in axes]
    first = lax.rem(d, 2) == 0
    return jnp.where(first, *halves), jnp.where(first, *halves[::-1])


def block(ref, index, size):
    return ref.at[pl.ds(pl.multiple_of(index * size, 8), size)]


def store_halves(value, mine, other):
    half = mine.shape[0]
    core = lax.rem(lax.axis_index("dp"), 2)
    mine[...] = block(value, core, half)[...]
    other[...] = block(value, 1 - core, half)[...]


def quarter():
    return 2 * lax.rem(lax.axis_index("point"), 2) + lax.rem(lax.axis_index("dp") // 2, 2)


def add_quarter_kernel(mine, received, *parts):
    size = parts[0].shape[0]
    for i, part in enumerate(parts):
        index = quarter() ^ i
        part[...] = block(mine, index, size)[...] + block(received, index, size)[...]


def arrange_quarters(own, partner, result):
    core = lax.rem(lax.axis_index("dp"), 2)
    size = own.shape[0] // 4
    for side, ref in ((core, own), (1 - core, partner)):
        for i in range(4):
            block(result, 4 * side + (quarter() ^ i), size)[...] = ref[i * size : (i + 1) * size]


def add_halve_kernel(axes, mine, received, kept, sent):
    half = kept.shape[0]
    upper, _ = place(axes)
    kept[...] = block(mine, upper, half)[...] + block(received, upper, half)[...]
    sent[...] = block(mine, 1 - upper, half)[...] + block(received, 1 - upper, half)[...]


def arrange(levels, own, partner, result):
    if not levels:
        return arrange_quarters(own, partner, result)
    core = lax.rem(lax.axis_index("dp"), 2)
    count = 1 << len(levels)
    size = own.shape[0] // count
    for side, ref in enumerate((own, partner)):
        uppers = [place(axes)[side] for axes in levels]
        for i in range(count):
            index = core if side == 0 else 1 - core
            for level, upper in enumerate(uppers):
                same = (i >> (len(levels) - 1 - level)) & 1 == 0
                index = 2 * index + (upper if same else 1 - upper)
            block(result, index, size)[...] = ref[i * size : (i + 1) * size]


def early_kernel(factor, columns_packed, packed, mine, other, early):
    width = early.shape[1]
    pieces = [ref[...] for ref in views(packed, *[width] * 12)[2:]]
    spread, hat, before_grad, hidden, grad = (pieces[i : i + 2] for i in range(0, 10, 2))
    early[0:width] = product(spread, grad, 1, 1) * factor
    early[width : 2 * width] = product(hat, before_grad, 1, 1) * factor
    early[2 * width :] = product(hidden, split(columns_packed[0:width]), 1, 1) * factor
    store_halves(early, mine, other)


def end_kernel(
    factor, middle_factor, head_size, slices,
    out_sum, front, front_wide, map_packed, back, back_wide,
    late_mine, late_other, packed,
    late,
):
    width = late.shape[1]
    points = front.shape[1]
    total = out_sum.shape[1]
    heads = total // slices
    weight_h, weight_l, fx_h, fx_l, assign_h, assign_l, hat_h, hat_l = views(
        front, *[total] * 2, *[width] * 6
    )
    temper_rows = front_wide.at[width + 8 : width + 8 + heads]
    both_grad_h, both_grad_l = views(packed, 2 * width, 2 * width)
    _, logit_maps, _, maps = map_views(map_packed, width, head_size, slices)
    spread_grad_h, spread_grad_l, *_, middle, attn, denom_rows = back_views(
        back, back_wide, width, head_size, slices
    )
    rows, lanes = GROUP * head_size, GROUP * slices
    tokens = middle[0:head_size]
    qkv_pair = split(middle[head_size : 4 * head_size])
    result = middle[4 * head_size : 5 * head_size]
    result_grad = split(out_sum[...])
    wide = SIDE * slices
    parts = []
    for pair in range(heads // SIDE):
        span = slice(pair * wide, (pair + 1) * wide)
        q = tuple(a[0:head_size, span] for a in qkv_pair)
        k = tuple(a[head_size : 2 * head_size, span] for a in qkv_pair)
        v = tuple(a[2 * head_size :, span] for a in qkv_pair)
        probs = attn[:, span]
        grad = tuple(a[:, span] for a in result_grad)
        value_grad = product(grad, split(probs), 1, 1)
        probs_grad = product(v, grad, 0, 0)
        weighted = probs * probs_grad
        total = jnp.sum(weighted, axis=0, keepdims=True)
        score_grad = split((weighted - probs * total) * head_size ** (-0.5))
        query_grad = product(k, score_grad, 1, 0)
        key_grad = product(q, score_grad, 1, 1)
        parts.append(jnp.concatenate([query_grad, key_grad, value_grad], axis=0))
    qkv_grad = split(jnp.concatenate(parts, axis=1))
    maps = (maps[0][...], maps[1][...])
    map_grad = product(split(tokens), qkv_grad, 1, 1)
    denom = denom_rows[0:1]
    num_grad = product(maps, qkv_grad, 1, 0) / denom
    den_grad = column(-jnp.sum(num_grad * tokens, axis=0, keepdims=True))
    mask = head_mask(head_size, slices)
    logit_blocks = (logit_maps[0][...], logit_maps[1][...])
    fx_grads, assign_grads = [], []
    logit_grad = jnp.zeros((head_size, lanes), F32)
    for g in range(heads // GROUP):
        span = slice(g * lanes, (g + 1) * lanes)
        piece = slice(g * rows, (g + 1) * rows)
        num_blocks = split(spread_blocks(num_grad[:, span], mask))
        result_blocks = split(spread_blocks(result[:, span], mask))
        weights = (weight_h[span], weight_l[span])
        fx_grads.append(product(num_blocks, weights, 1, 0))
        weight_grad = product(
            stacked(num_blocks, result_blocks),
            stacked(
                (fx_h[piece], fx_l[piece]), (spread_grad_h[piece], spread_grad_l[piece])
            ),
            0,
            0,
        )
        weight_grad = weight_grad + den_grad[span]
        grads = []
        for i in range(GROUP):
            block = slice(i * slices, (i + 1) * slices)
            head = g * GROUP + i
            scale = temper_rows[head : head + 1]
            w = weights[0][block].astype(F32) + weights[1][block].astype(F32)
            weighted = w * weight_grad[block]
            total = jnp.sum(weighted, axis=0, keepdims=True)
            grads.append((weighted - w * total) / scale)
        grads = split(jnp.concatenate(grads, axis=0))
        assign_grads.append(product(logit_blocks, grads, 1, 0))
        full = product((assign_h[piece], assign_l[piece]), grads, 1, 1)
        logit_grad = logit_grad + fold_blocks(full, mask, head_size)
    both_grad = split(jnp.concatenate(fx_grads + assign_grads, axis=0))
    both_grad_h[...], both_grad_l[...] = both_grad
    matrix = product((hat_h[...], hat_l[...]), both_grad, 1, 1) * factor
    late[0:width] = matrix[:, :width]
    late[width : 2 * width] = matrix[:, width:]
    logit_grad = logit_grad[:, : 2 * slices] + logit_grad[:, 2 * slices :]
    logit_grad = logit_grad[:, :slices] + logit_grad[:, slices:]
    base = 2 * width
    late[base:] = jnp.zeros((late.shape[0] - base, width), F32)
    late[base : base + head_size, 0 : 3 * head_size] = map_grad * middle_factor
    late[base : base + head_size, 128 : 128 + slices] = logit_grad * factor
    store_halves(late, late_mine, late_other)


def rows_kernel(front, front_wide, back_wide, end, x_grad):
    width = x_grad.shape[2]
    total = front.shape[1]
    _, hat_h, hat_l, both_h, both_l = views(front, 2 * total + 4 * width, *[width] * 4)
    rstd = front_wide[width : width + 1]
    grads = [ref[...] for ref in views(end, 2 * width, 2 * width)]
    hat_grad = product((both_h[...], both_l[...]), grads, 1, 0)
    hat = hat_h[...].astype(F32) + hat_l[...].astype(F32)
    x_grad[0] = (back_wide[0:width] + standardise_pull(hat_grad, hat, rstd)).T


def early_out_kernel(
    levels,
    own, partner, gain, expand_weight,
    matrices, gain_row,
    early, scaled, sems,
):
    arrange(levels, own, partner, early)
    width = gain.shape[1]
    copies = [
        pltpu.make_async_copy(early.at[0:width], matrices.at[2], sems.at[0]),
        pltpu.make_async_copy(early.at[2 * width : 3 * width], matrices.at[4], sems.at[1]),
        pltpu.make_async_copy(scaled, matrices.at[3], sems.at[2]),
    ]
    copies[0].start()
    copies[1].start()
    grad = early[width : 2 * width]
    scaled[...] = grad * column(gain[...])
    copies[2].start()
    gain_row[...] = row_total(grad, expand_weight[...])
    for copy in copies:
        copy.wait()


def late_out_kernel(
    levels,
    own, partner, gain, fx_weight, x_weight, gain_row, given,
    matrices, maps_out, logit_out, gains_out,
    late, scaled, maps, logit, gains, sems,
):
    arrange(levels, own, partner, late)
    width = gain.shape[1]
    head_size, slices = logit.shape
    base = 2 * width
    for i in range(3):
        maps[i] = late[base : base + head_size, i * head_size : (i + 1) * head_size]
    logit[...] = late[base : base + head_size, 128 : 128 + slices]
    copies = fetch((maps, logit), (maps_out, logit_out), sems)
    gain_column = column(gain[...])
    total = jnp.zeros((1, width), F32)
    for i, weight in enumerate((fx_weight, x_weight)):
        scaled[i] = late[i * width : (i + 1) * width] * gain_column
        copy = pltpu.make_async_copy(scaled.at[i], matrices.at[i], sems.at[2 + i])
        copy.start()
        copies.append(copy)
    for i, weight in enumerate((fx_weight, x_weight)):
        total = total + row_total(late[i * width : (i + 1) * width], weight[...])
    gains[...] = jnp.concatenate([total, gain_row[...]], axis=0)
    copies.append(pltpu.make_async_copy(gains, gains_out, sems.at[4]))
    copies[-1].start()
    for copy in copies:
        copy.wait()


VMEM = pl.BlockSpec(memory_space=pltpu.VMEM)
SMEM = pl.BlockSpec(memory_space=pltpu.SMEM)


HBM = pl.BlockSpec(memory_space=pltpu.HBM)


def call(body, name, in_specs, out_specs, out_shape, args, flops, limit=SMALL, scratch=(),
         aliases=None):
    return pl.pallas_call(
        body,
        name=name,
        in_specs=in_specs,
        out_specs=out_specs,
        out_shape=out_shape,
        scratch_shapes=scratch,
        input_output_aliases=aliases or {},
        compiler_params=pltpu.CompilerParams(vmem_limit_bytes=limit),
        cost_estimate=pl.CostEstimate(flops=flops, bytes_accessed=1 << 20, transcendentals=0),
    )(*args)


def swap(value, moves, sizes):
    dp, point = sizes
    pairs = []
    for d in range(dp):
        for p in range(point):
            other_d, other_p = moves(d, p)
            pairs.append((d * point + p, other_d * point + other_p))
    return lax.ppermute(value, ("dp", "point"), pairs)


def bits(count):
    return [1 << i for i in range(count.bit_length() - 1)]


def tie(*values):
    return lax.optimization_barrier(values)


def flips(axes):
    def moves(d, p):
        axis, bit = axes[d & 1]
        return (d, p ^ bit) if axis else (d ^ bit, p)

    return moves


CORES = ((0, 1), (0, 1))


def paired(axes):
    turned = list(axes)
    for i in range(0, len(axes) - 1, 2):
        turned[i], turned[i + 1] = axes[i + 1], axes[i]
    return list(zip(axes, turned))


def direct_steps(masks, sizes):
    groups = [[mask] for mask in masks[:-2]]
    if len(masks) > 1:
        groups.append([masks[-2], masks[-1], masks[-2] | masks[-1]])
    elif masks:
        groups.append([masks[-1]])

    def step(group):
        def run(value):
            parts = [swap(value, flips(((1, mask),) * 2), sizes) for mask in group]
            if len(parts) == 1:
                return value + parts[0]
            return (value + parts[0]) + (parts[1] + parts[2])
        return run

    return [step(group) for group in groups]


def point_steps(sizes):
    return direct_steps(bits(sizes[1]), sizes)


def all_axes(sizes):
    return paired(
        [(1, 1)] + [(0, b) for b in bits(sizes[0])[1:]] + [(1, b) for b in bits(sizes[1])[1:]]
    )


def quarter_steps(sizes, direct):
    group = [lambda d, p: (d ^ 2, p), lambda d, p: (d, p ^ 1), lambda d, p: (d ^ 2, p ^ 1)]
    others = paired(([(0, b) for b in bits(sizes[0])[2:]] + [(1, b) for b in bits(sizes[1])[1:]])[::-1])

    def cores(value):
        received = swap(value[1], flips(CORES), sizes)
        part = (value[0].shape[0] // 4, value[0].shape[1])
        return call(
            add_quarter_kernel, "add_quarter", [VMEM] * 2, [VMEM] * 4,
            [jax.ShapeDtypeStruct(part, F32)] * 4, (value[0], received), received.size,
        )

    def scatter(value):
        parts = [swap(part, moves, sizes) for part, moves in zip(value[1:], group)]
        return (value[0] + parts[0]) + (parts[1] + parts[2])

    def add(axes):
        return lambda value: value + swap(value, flips(axes), sizes)

    def gather(value):
        return jnp.concatenate([value] + [swap(value, moves, sizes) for moves in group], axis=0)

    def last(value):
        return value, swap(value, flips(CORES), sizes)

    if direct:
        sums = [add(axes) for axes in paired([(0, b) for b in bits(sizes[0])[2:]])]
        sums += direct_steps(bits(sizes[1])[1:], sizes)
    else:
        sums = [add(axes) for axes in others]
    return [cores, scatter] + sums + [gather, last]


def all_steps(sizes, scatters, direct=False):
    if scatters == 0:
        return quarter_steps(sizes, direct)
    steps_axes = all_axes(sizes)

    def add_halve(i, mine, received):
        half = (mine.shape[0] // 2, mine.shape[1])
        return call(
            functools.partial(add_halve_kernel, steps_axes[i]), "add_halve", [VMEM] * 2,
            [VMEM] * 2, [jax.ShapeDtypeStruct(half, F32)] * 2, (mine, received), mine.size,
        )

    def cores(value):
        return add_halve(0, value[0], swap(value[1], flips(CORES), sizes))

    def scatter(i):
        def step(value):
            received = swap(value[1], flips(steps_axes[i]), sizes)
            if i + 1 < scatters:
                return add_halve(i + 1, value[0], received)
            return value[0] + received
        return step

    def add(i):
        return lambda value: value + swap(value, flips(steps_axes[i]), sizes)

    def gather(i):
        return lambda value: jnp.concatenate(
            [value, swap(value, flips(steps_axes[i]), sizes)], axis=0
        )

    def last(value):
        return value, swap(value, flips(CORES), sizes)

    return (
        [cores] + [scatter(i) for i in range(scatters)]
        + [add(i) for i in range(scatters, len(steps_axes))]
        + [gather(i) for i in reversed(range(scatters))] + [last]
    )


def shards(
    sizes,
    inputs, cotangent, gain_one, fx_weight, x_weight, slice_logit_weight, temper,
    slice_query_matrix, slice_key_matrix, slice_value_matrix, out_weight, gain_two,
    expand_weight, down_weight,
):
    points, width = inputs.shape[1:]
    head_size, slices = slice_logit_weight.shape
    heads = temper.shape[0]
    total = heads * slices
    gain_one, gain_two = gain_one[None], gain_two[None]
    factor = 1.0 / math.sqrt(points * sizes[0] * sizes[1])
    axes = all_axes(sizes)

    def shape(*dims, dtype=F32):
        return jax.ShapeDtypeStruct(dims, dtype)

    def pair(*dims):
        return [shape(*dims, dtype=BF16)] * 2

    dense = 6 * points * width * width
    pinned = [
        pltpu.with_memory_space_constraint(array, pltpu.HBM)
        for array in (inputs, gain_one, fx_weight, x_weight, slice_logit_weight, temper)
    ]
    front, front_wide, sums = call(
        front_kernel, "front", [HBM] * 6, [VMEM] * 3,
        [shape(2 * total + 8 * width, points, dtype=BF16), shape(width + 8 + heads, points),
         shape(total // 128 * head_size + 8, 128)],
        pinned,
        4 * dense,
        FRONT_LIMIT,
        [
            pltpu.VMEM(inputs.shape, F32), pltpu.VMEM((1, width), F32),
            pltpu.VMEM((width, width), F32), pltpu.VMEM((width, width), F32),
            pltpu.VMEM((head_size, slices), F32), pltpu.SMEM((heads,), F32),
            pltpu.SemaphoreType.DMA((6,)),
        ],
    )
    sums, cotangent, out_weight, gain_two, expand_weight, down_weight = tie(
        sums, cotangent, out_weight, gain_two, expand_weight, down_weight
    )
    columns, maps = call(
        ready_kernel, "ready", [VMEM] * 9, [VMEM] * 2,
        [shape(2 * width, points),
         shape(8 * width + (2 * GROUP + 8) * head_size, width, dtype=BF16)],
        (cotangent, out_weight, gain_two, expand_weight, down_weight, slice_query_matrix,
         slice_key_matrix, slice_value_matrix, slice_logit_weight),
        2 * dense,
    )
    for step in point_steps(sizes):
        sums = step(sums)
    out_sum, back, back_wide = call(
        functools.partial(back_kernel, head_size, slices), "back", [VMEM] * 5, [VMEM] * 3,
        [shape(head_size, total), shape(12 * width, points, dtype=BF16),
         shape(width + 5 * head_size + SIDE * slices + 8, points)],
        (sums, front, front_wide, columns, maps),
        6 * dense,
    )
    early_value = call(
        functools.partial(early_kernel, factor), "early", [VMEM] * 2, [VMEM] * 2,
        [shape(3 * width // 2, width)] * 2, (columns, back), 3 * dense,
        scratch=[pltpu.VMEM((3 * width, width), F32)],
    )
    behind = [early_value]
    for step in all_steps(sizes, EARLY):
        behind.append(step(behind[-1]))
    order = [None, 2]
    for i, step in enumerate(reversed(point_steps(sizes))):
        out_sum = step(out_sum)
        if i < len(order) and order[i] is not None:
            out_sum, _ = tie(out_sum, behind[order[i]])
    rows = -(-(2 * width + head_size) // 64) * 64
    mine, other, end = call(
        functools.partial(end_kernel, factor, factor / sizes[1], head_size, slices), "end",
        [VMEM] * 6, [VMEM] * 3,
        [shape(rows // 2, width)] * 2 + [shape(4 * width, points, dtype=BF16)],
        (out_sum, front, front_wide, maps, back, back_wide),
        8 * dense,
        scratch=[pltpu.VMEM((rows, width), F32)],
    )
    late, _ = tie((mine, other), behind[2])
    input_grad = call(
        rows_kernel, "rows", [VMEM] * 4, VMEM, shape(1, points, width),
        (front, front_wide, back_wide, end), 2 * dense,
    )
    steps = all_steps(sizes, LATE, True)
    for i, step in enumerate(steps):
        late = step(late)
        if i == 0:
            late, input_grad = tie(late, input_grad)
    matrices, gain_row = call(
        functools.partial(early_out_kernel, tuple(axes[:EARLY])), "early_out", [VMEM] * 4, [HBM, VMEM],
        [shape(5, width, width), shape(1, width)],
        (*behind[-1], gain_two, expand_weight),
        dense // 8,
        scratch=[pltpu.VMEM((3 * width, width), F32), pltpu.VMEM((width, width), F32),
                 pltpu.SemaphoreType.DMA((3,))],
    )
    matrices, map_grads, logit_grad, gains = call(
        functools.partial(late_out_kernel, tuple(axes[:LATE])), "late_out", [VMEM] * 6 + [HBM],
        [HBM] * 4,
        [shape(5, width, width), shape(3, head_size, head_size), shape(head_size, slices),
         shape(2, width)],
        (*late, gain_one, fx_weight, x_weight, gain_row, matrices),
        dense // 8,
        scratch=[pltpu.VMEM((rows, width), F32), pltpu.VMEM((2, width, width), F32),
                 pltpu.VMEM((3, head_size, head_size), F32), pltpu.VMEM((head_size, slices), F32),
                 pltpu.VMEM((2, width), F32), pltpu.SemaphoreType.DMA((5,))],
        aliases={6: 0},
    )
    return input_grad, matrices, map_grads, logit_grad, gains


def solution(mesh):
    sizes = (mesh.shape["dp"], mesh.shape["point"])
    placed = (P("dp", "point", None),) * 2 + (P(),) * 12
    return jax.shard_map(
        functools.partial(shards, sizes),
        mesh=mesh,
        in_specs=placed,
        out_specs=(P("dp", "point", None), P(), P(), P(), P()),
        check_vma=False,
    )
```

```python
import functools
import math

import jax
import jax.numpy as jnp
from jax import lax
from jax.experimental import pallas as pl
from jax.experimental.pallas import tpu as pltpu
from jax.sharding import PartitionSpec as P

F32 = jnp.float32
BF16 = jnp.bfloat16
GROUP = 4
EPS = 1e-05
EARLY = 0
LATE = 0
SIDE = 4
GELU_A = math.sqrt(2.0 / math.pi)
GELU_B = 0.044715
SMALL = 16 * 1024 * 1024
FRONT_LIMIT = 16 * 1024 * 1024


def split(value):
    high = value.astype(BF16)
    return high, (value - high.astype(F32)).astype(BF16)


def product(left, right, left_dim, right_dim):
    def one(a, b):
        return lax.dot_general(
            a, b, (((left_dim,), (right_dim,)), ((), ())), preferred_element_type=F32
        )

    if left[0].shape[left_dim] % 128 == 0 or left_dim == right_dim == 0:
        return one(
            jnp.concatenate([left[0], left[0], left[1]], axis=left_dim),
            jnp.concatenate([right[0], right[1], right[0]], axis=right_dim),
        )
    return one(left[0], right[0]) + (one(left[0], right[1]) + one(left[1], right[0]))


def rows_of(pair, start, size):
    return pair[0][start : start + size], pair[1][start : start + size]


def stacked(first, second, axis=0):
    return tuple(jnp.concatenate([a, b], axis=axis) for a, b in zip(first, second))


def column(row):
    wide = jnp.broadcast_to(row, (8, row.shape[1]))
    return wide.T[:, 0:1]


def head_mask(head_size, slices):
    shape = (GROUP * head_size, GROUP * slices)
    row = lax.broadcasted_iota(jnp.int32, shape, 0) // head_size
    lane = lax.broadcasted_iota(jnp.int32, shape, 1) // slices
    return row == lane


def spread_blocks(value, mask):
    return jnp.where(mask, jnp.concatenate([value] * GROUP, axis=0), 0.0)


def fold_blocks(value, mask, head_size):
    kept = jnp.where(mask, value, 0.0)
    total = kept[:head_size]
    for i in range(1, GROUP):
        total = total + kept[i * head_size : (i + 1) * head_size]
    return total


def standardise(columns):
    centre = columns - jnp.mean(columns, axis=0, keepdims=True)
    rstd = lax.rsqrt(jnp.mean(centre * centre, axis=0, keepdims=True) + EPS)
    return centre * rstd, rstd


def standardise_pull(grad, hat, rstd):
    first = jnp.mean(grad, axis=0, keepdims=True)
    second = jnp.mean(grad * hat, axis=0, keepdims=True)
    return rstd * (grad - first - hat * second)


def row_total(left, right):
    value = split(left * right)
    ones = jnp.ones((16, left.shape[1]), BF16)
    nt = (((1,), (1,)), ((), ()))
    total = lax.dot_general(ones, value[0], nt, preferred_element_type=F32)
    total = total + lax.dot_general(ones, value[1], nt, preferred_element_type=F32)
    return total[0:1]


def fetch(sources, targets, sems):
    copies = [
        pltpu.make_async_copy(source, target, sems.at[i])
        for i, (source, target) in enumerate(zip(sources, targets))
    ]
    for copy in copies:
        copy.start()
    return copies


def views(ref, *sizes):
    result, start = [], 0
    for size in sizes:
        result.append(ref.at[start : start + size])
        start += size
    return result


def front_kernel(
    x_hbm, gain_hbm, fx_hbm, xw_hbm, logit_hbm, temper_hbm,
    packed, wide_packed, sums,
    x, gain, fx_weight, x_weight, logit_weight, temper, sems,
):
    sources = (x_hbm, gain_hbm, fx_hbm, xw_hbm, logit_hbm, temper_hbm)
    targets = (x, gain, fx_weight, x_weight, logit_weight, temper)
    width, total = x.shape[2], packed.shape[1]
    weight_h, weight_l, fx_h, fx_l, assign_h, assign_l, hat_h, hat_l, both_h, both_l = views(
        packed, *[total] * 2, *[width] * 8
    )
    x_t, rstd_rows, temper_rows = views(wide_packed, width, 8, temper.shape[0])
    copies = fetch(sources, targets, sems)
    sums[sums.shape[0] - 8 :] = jnp.zeros((8, 128), F32)
    head_size, slices = logit_weight.shape
    heads = temper.shape[0]
    points = x.shape[1]
    width = x.shape[2]
    copies[0].wait()
    columns = x[0].T
    x_t[...] = columns
    hat, rstd = standardise(columns)
    rstd_rows[...] = jnp.broadcast_to(rstd, (8, points))
    hat = split(hat)
    hat_h[...], hat_l[...] = hat
    for copy in copies[1:]:
        copy.wait()
    both = jnp.concatenate([fx_weight[...], x_weight[...]], axis=1)
    both = split(both * column(gain[...]))
    both_h[...], both_l[...] = both
    projected = split(product(both, hat, 0, 0))
    fx = rows_of(projected, 0, width)
    assign = rows_of(projected, width, width)
    fx_h[...], fx_l[...] = fx
    assign_h[...], assign_l[...] = assign
    mask = head_mask(head_size, slices)
    wide = jnp.concatenate([logit_weight[...]] * GROUP, axis=1)
    logit_blocks = split(spread_blocks(wide, mask))
    ones = jnp.ones((16, points), BF16)
    blocks = total // 128
    for g in range(heads // GROUP):
        rows = GROUP * head_size
        logits = product(logit_blocks, rows_of(assign, g * rows, rows), 0, 0)
        parts = []
        for i in range(GROUP):
            head = g * GROUP + i
            scale = jnp.full((1, points), temper[head], F32)
            temper_rows[head : head + 1] = scale
            scaled = logits[i * slices : (i + 1) * slices] * (1.0 / scale)
            scaled = scaled - jnp.max(scaled, axis=0, keepdims=True)
            grown = jnp.exp(scaled)
            parts.append(grown * (1.0 / jnp.sum(grown, axis=0, keepdims=True)))
        weights = split(jnp.concatenate(parts, axis=0))
        span = slice(g * GROUP * slices, (g + 1) * GROUP * slices)
        weight_h[span], weight_l[span] = weights
        num = product(rows_of(fx, g * rows, rows), weights, 1, 1)
        num = fold_blocks(num, mask, head_size)
        nt = (((1,), (1,)), ((), ()))
        den = lax.dot_general(ones, weights[0], nt, preferred_element_type=F32)
        den = den + lax.dot_general(ones, weights[1], nt, preferred_element_type=F32)
        for i in range(num.shape[1] // 128):
            j = g * (num.shape[1] // 128) + i
            lanes = slice(i * 128, (i + 1) * 128)
            sums[j * head_size : (j + 1) * head_size] = num[:, lanes]
            row = blocks * head_size + j
            sums[row : row + 1] = den[0:1, lanes]


def map_views(packed, width, head_size, slices):
    views_of = views(
        packed, *[width] * 8, *[GROUP * head_size] * 2, *[3 * head_size] * 2, *[head_size] * 2
    )
    maps_t = [ref.at[:, 0:head_size] for ref in views_of[10:12]]
    maps = [ref.at[:, 0 : 3 * head_size] for ref in views_of[12:14]]
    logits = [ref.at[:, 0 : GROUP * slices] for ref in views_of[8:10]]
    return views_of[:8], logits, maps_t, maps


def ready_kernel(
    cotangent, out_weight, gain, expand_weight, down_weight, query, key, value, logit_weight,
    columns_packed, packed,
):
    width = cotangent.shape[2]
    head_size, slices = logit_weight.shape
    cot_t, hidden_grad = views(columns_packed, width, width)
    (out_h, out_l, out_t_h, out_t_l, expand_h, expand_l, expand_t_h, expand_t_l), logits, maps_t, maps = (
        map_views(packed, width, head_size, slices)
    )
    columns = cotangent[0].T
    cot_t[...] = columns
    hidden_grad[...] = product(split(down_weight[...]), split(columns), 1, 0)
    out_h[...], out_l[...] = split(out_weight[...])
    out_t_h[...], out_t_l[...] = split(out_weight[...].T)
    expand = expand_weight[...] * column(gain[...])
    expand_h[...], expand_l[...] = split(expand)
    expand_t_h[...], expand_t_l[...] = split(expand.T)
    both = jnp.concatenate([query[...], key[...], value[...]], axis=1)
    maps_t[0][...], maps_t[1][...] = split(both.T)
    maps[0][...], maps[1][...] = split(both)
    wide = jnp.concatenate([logit_weight[...]] * GROUP, axis=1)
    logits[0][...], logits[1][...] = split(spread_blocks(wide, head_mask(head_size, slices)))


def back_views(packed, wide_packed, width, head_size, slices):
    return views(packed, *[width] * 12) + views(
        wide_packed, width, 5 * head_size, SIDE * slices, 8
    )


def back_kernel(
    head_size, slices,
    sums, front, front_wide, columns_packed, map_packed,
    out_sum, packed, wide_packed,
):
    total = front.shape[1]
    heads = total // slices
    width = (wide_packed.shape[0] - 8) - 5 * head_size - SIDE * slices
    weight_h, weight_l = views(front, total, total)
    x_t = front_wide.at[0:width]
    cot_t, hidden_grad = views(columns_packed, width, width)
    (out_h, out_l, out_t_h, out_t_l, expand_h, expand_l, expand_t_h, expand_t_l), _, maps_t, _ = (
        map_views(map_packed, width, head_size, slices)
    )
    maps_h, maps_l = maps_t
    (spread_grad_h, spread_grad_l, spread_h, spread_l, hat_h, hat_l, before_grad_h, before_grad_l,
     hidden_h, hidden_l, grad_h, grad_l, mixed_grad, middle, attn, denom_rows) = back_views(
        packed, wide_packed, width, head_size, slices
    )
    rows, lanes = GROUP * head_size, GROUP * slices
    blocks = total // 128
    ends = [blocks * head_size + j for j in range(blocks)]
    denom = jnp.concatenate([sums[end : end + 1] for end in ends], axis=1) + EPS
    nums = [sums[j * head_size : (j + 1) * head_size] for j in range(blocks)]
    denom_rows[...] = jnp.broadcast_to(denom, (8, total))
    tokens = jnp.concatenate(nums, axis=1) / denom
    qkv = product((maps_h[...], maps_l[...]), split(tokens), 1, 0)
    qkv_pair = split(qkv)
    wide = SIDE * slices
    same = (lax.broadcasted_iota(jnp.int32, (wide, wide), 0) // slices) == (
        lax.broadcasted_iota(jnp.int32, (wide, wide), 1) // slices
    )
    results = []
    for pair in range(heads // SIDE):
        span = slice(pair * wide, (pair + 1) * wide)
        q = tuple(a[0:head_size, span] for a in qkv_pair)
        k = tuple(a[head_size : 2 * head_size, span] for a in qkv_pair)
        v = tuple(a[2 * head_size :, span] for a in qkv_pair)
        scores = product(k, q, 0, 0) * head_size ** (-0.5)
        scores = jnp.where(same, scores, -1e30)
        scores = scores - jnp.max(scores, axis=0, keepdims=True)
        grown = jnp.where(same, jnp.exp(scores), 0.0)
        probs = grown * (1.0 / jnp.sum(grown, axis=0, keepdims=True))
        attn[:, span] = probs
        results.append(product(v, split(probs), 1, 0))
    result = jnp.concatenate(results, axis=1)
    middle[0:head_size] = tokens
    middle[head_size : 4 * head_size] = qkv
    middle[4 * head_size : 5 * head_size] = result
    mask = head_mask(head_size, slices)
    spread = []
    for g in range(heads // GROUP):
        span = slice(g * lanes, (g + 1) * lanes)
        blocks = split(spread_blocks(result[:, span], mask))
        spread.append(product(blocks, (weight_h[span], weight_l[span]), 1, 0))
    spread = split(jnp.concatenate(spread, axis=0))
    spread_h[...], spread_l[...] = spread
    mixed = x_t[...] + product((out_t_h[...], out_t_l[...]), spread, 1, 0)
    hat, rstd = standardise(mixed)
    hat_pair = split(hat)
    hat_h[...], hat_l[...] = hat_pair
    before = product((expand_t_h[...], expand_t_l[...]), hat_pair, 1, 0)
    square = before * before
    bent = jnp.tanh(GELU_A * (before + GELU_B * before * square))
    half = 0.5 * (1.0 + bent)
    hidden_h[...], hidden_l[...] = split(before * half)
    slope = half + 0.5 * before * (1.0 - bent * bent) * (GELU_A * (1.0 + 3.0 * GELU_B * square))
    before_grad = split(hidden_grad[...] * slope)
    before_grad_h[...], before_grad_l[...] = before_grad
    hat_grad = product((expand_h[...], expand_l[...]), before_grad, 1, 0)
    grad = cot_t[...] + standardise_pull(hat_grad, hat, rstd)
    mixed_grad[...] = grad
    grad_pair = split(grad)
    grad_h[...], grad_l[...] = grad_pair
    spread_grad = split(product((out_h[...], out_l[...]), grad_pair, 1, 0))
    spread_grad_h[...], spread_grad_l[...] = spread_grad
    sums_out = []
    for g in range(heads // GROUP):
        span = slice(g * lanes, (g + 1) * lanes)
        full = product(
            rows_of(spread_grad, g * rows, rows), (weight_h[span], weight_l[span]), 1, 1
        )
        sums_out.append(fold_blocks(full, mask, head_size))
    out_sum[...] = jnp.concatenate(sums_out, axis=1)


def place(axes):
    d, p = lax.axis_index("dp"), lax.axis_index("point")
    halves = [lax.rem((p if axis else d) // bit, 2) for axis, bit in axes]
    first = lax.rem(d, 2) == 0
    return jnp.where(first, *halves), jnp.where(first, *halves[::-1])


def block(ref, index, size):
    return ref.at[pl.ds(pl.multiple_of(index * size, 8), size)]


def store_halves(value, mine, other):
    half = mine.shape[0]
    core = lax.rem(lax.axis_index("dp"), 2)
    mine[...] = block(value, core, half)[...]
    other[...] = block(value, 1 - core, half)[...]


def quarter():
    return 2 * lax.rem(lax.axis_index("point"), 2) + lax.rem(lax.axis_index("dp") // 2, 2)


def add_quarter_kernel(mine, received, *parts):
    size = parts[0].shape[0]
    for i, part in enumerate(parts):
        index = quarter() ^ i
        part[...] = block(mine, index, size)[...] + block(received, index, size)[...]


def arrange_quarters(own, partner, result):
    core = lax.rem(lax.axis_index("dp"), 2)
    size = own.shape[0] // 4
    for side, ref in ((core, own), (1 - core, partner)):
        for i in range(4):
            block(result, 4 * side + (quarter() ^ i), size)[...] = ref[i * size : (i + 1) * size]


def add_halve_kernel(axes, mine, received, kept, sent):
    half = kept.shape[0]
    upper, _ = place(axes)
    kept[...] = block(mine, upper, half)[...] + block(received, upper, half)[...]
    sent[...] = block(mine, 1 - upper, half)[...] + block(received, 1 - upper, half)[...]


def arrange(levels, own, partner, result):
    if not levels:
        return arrange_quarters(own, partner, result)
    core = lax.rem(lax.axis_index("dp"), 2)
    count = 1 << len(levels)
    size = own.shape[0] // count
    for side, ref in enumerate((own, partner)):
        uppers = [place(axes)[side] for axes in levels]
        for i in range(count):
            index = core if side == 0 else 1 - core
            for level, upper in enumerate(uppers):
                same = (i >> (len(levels) - 1 - level)) & 1 == 0
                index = 2 * index + (upper if same else 1 - upper)
            block(result, index, size)[...] = ref[i * size : (i + 1) * size]


def early_kernel(factor, columns_packed, packed, mine, other, early):
    width = early.shape[1]
    pieces = [ref[...] for ref in views(packed, *[width] * 12)[2:]]
    spread, hat, before_grad, hidden, grad = (pieces[i : i + 2] for i in range(0, 10, 2))
    early[0:width] = product(spread, grad, 1, 1) * factor
    early[width : 2 * width] = product(hat, before_grad, 1, 1) * factor
    early[2 * width :] = product(hidden, split(columns_packed[0:width]), 1, 1) * factor
    store_halves(early, mine, other)


def end_kernel(
    factor, middle_factor, head_size, slices,
    out_sum, front, front_wide, map_packed, back, back_wide,
    late_mine, late_other, packed,
    late,
):
    width = late.shape[1]
    points = front.shape[1]
    total = out_sum.shape[1]
    heads = total // slices
    weight_h, weight_l, fx_h, fx_l, assign_h, assign_l, hat_h, hat_l = views(
        front, *[total] * 2, *[width] * 6
    )
    temper_rows = front_wide.at[width + 8 : width + 8 + heads]
    both_grad_h, both_grad_l = views(packed, 2 * width, 2 * width)
    _, logit_maps, _, maps = map_views(map_packed, width, head_size, slices)
    spread_grad_h, spread_grad_l, *_, middle, attn, denom_rows = back_views(
        back, back_wide, width, head_size, slices
    )
    rows, lanes = GROUP * head_size, GROUP * slices
    tokens = middle[0:head_size]
    qkv_pair = split(middle[head_size : 4 * head_size])
    result = middle[4 * head_size : 5 * head_size]
    result_grad = split(out_sum[...])
    wide = SIDE * slices
    parts = []
    for pair in range(heads // SIDE):
        span = slice(pair * wide, (pair + 1) * wide)
        q = tuple(a[0:head_size, span] for a in qkv_pair)
        k = tuple(a[head_size : 2 * head_size, span] for a in qkv_pair)
        v = tuple(a[2 * head_size :, span] for a in qkv_pair)
        probs = attn[:, span]
        grad = tuple(a[:, span] for a in result_grad)
        value_grad = product(grad, split(probs), 1, 1)
        probs_grad = product(v, grad, 0, 0)
        weighted = probs * probs_grad
        total = jnp.sum(weighted, axis=0, keepdims=True)
        score_grad = split((weighted - probs * total) * head_size ** (-0.5))
        query_grad = product(k, score_grad, 1, 0)
        key_grad = product(q, score_grad, 1, 1)
        parts.append(jnp.concatenate([query_grad, key_grad, value_grad], axis=0))
    qkv_grad = split(jnp.concatenate(parts, axis=1))
    maps = (maps[0][...], maps[1][...])
    map_grad = product(split(tokens), qkv_grad, 1, 1)
    denom = denom_rows[0:1]
    num_grad = product(maps, qkv_grad, 1, 0) / denom
    den_grad = column(-jnp.sum(num_grad * tokens, axis=0, keepdims=True))
    mask = head_mask(head_size, slices)
    logit_blocks = (logit_maps[0][...], logit_maps[1][...])
    fx_grads, assign_grads = [], []
    logit_grad = jnp.zeros((head_size, lanes), F32)
    for g in range(heads // GROUP):
        span = slice(g * lanes, (g + 1) * lanes)
        piece = slice(g * rows, (g + 1) * rows)
        num_blocks = split(spread_blocks(num_grad[:, span], mask))
        result_blocks = split(spread_blocks(result[:, span], mask))
        weights = (weight_h[span], weight_l[span])
        fx_grads.append(product(num_blocks, weights, 1, 0))
        weight_grad = product(
            stacked(num_blocks, result_blocks),
            stacked(
                (fx_h[piece], fx_l[piece]), (spread_grad_h[piece], spread_grad_l[piece])
            ),
            0,
            0,
        )
        weight_grad = weight_grad + den_grad[span]
        grads = []
        for i in range(GROUP):
            block = slice(i * slices, (i + 1) * slices)
            head = g * GROUP + i
            scale = temper_rows[head : head + 1]
            w = weights[0][block].astype(F32) + weights[1][block].astype(F32)
            weighted = w * weight_grad[block]
            total = jnp.sum(weighted, axis=0, keepdims=True)
            grads.append((weighted - w * total) * (1.0 / scale))
        grads = split(jnp.concatenate(grads, axis=0))
        assign_grads.append(product(logit_blocks, grads, 1, 0))
        full = product((assign_h[piece], assign_l[piece]), grads, 1, 1)
        logit_grad = logit_grad + fold_blocks(full, mask, head_size)
    both_grad = split(jnp.concatenate(fx_grads + assign_grads, axis=0))
    both_grad_h[...], both_grad_l[...] = both_grad
    matrix = product((hat_h[...], hat_l[...]), both_grad, 1, 1) * factor
    late[0:width] = matrix[:, :width]
    late[width : 2 * width] = matrix[:, width:]
    logit_grad = logit_grad[:, : 2 * slices] + logit_grad[:, 2 * slices :]
    logit_grad = logit_grad[:, :slices] + logit_grad[:, slices:]
    base = 2 * width
    late[base:] = jnp.zeros((late.shape[0] - base, width), F32)
    late[base : base + head_size, 0 : 3 * head_size] = map_grad * middle_factor
    late[base : base + head_size, 128 : 128 + slices] = logit_grad * factor
    store_halves(late, late_mine, late_other)


def rows_kernel(front, front_wide, back_wide, end, x_grad):
    width = x_grad.shape[2]
    total = front.shape[1]
    _, hat_h, hat_l, both_h, both_l = views(front, 2 * total + 4 * width, *[width] * 4)
    rstd = front_wide[width : width + 1]
    grads = [ref[...] for ref in views(end, 2 * width, 2 * width)]
    hat_grad = product((both_h[...], both_l[...]), grads, 1, 0)
    hat = hat_h[...].astype(F32) + hat_l[...].astype(F32)
    x_grad[0] = (back_wide[0:width] + standardise_pull(hat_grad, hat, rstd)).T


def early_out_kernel(
    levels,
    own, partner, gain, expand_weight,
    matrices, gain_row,
    early, scaled, sems,
):
    arrange(levels, own, partner, early)
    width = gain.shape[1]
    copies = [
        pltpu.make_async_copy(early.at[0:width], matrices.at[2], sems.at[0]),
        pltpu.make_async_copy(early.at[2 * width : 3 * width], matrices.at[4], sems.at[1]),
        pltpu.make_async_copy(scaled, matrices.at[3], sems.at[2]),
    ]
    copies[0].start()
    copies[1].start()
    grad = early[width : 2 * width]
    scaled[...] = grad * column(gain[...])
    copies[2].start()
    gain_row[...] = row_total(grad, expand_weight[...])
    for copy in copies:
        copy.wait()


def late_out_kernel(
    levels,
    own, partner, gain, fx_weight, x_weight, gain_row, given,
    matrices, maps_out, logit_out, gains_out,
    late, scaled, maps, logit, gains, sems,
):
    arrange(levels, own, partner, late)
    width = gain.shape[1]
    head_size, slices = logit.shape
    base = 2 * width
    copies = []
    gain_column = column(gain[...])
    total = jnp.zeros((1, width), F32)
    for i, weight in enumerate((fx_weight, x_weight)):
        scaled[i] = late[i * width : (i + 1) * width] * gain_column
        copy = pltpu.make_async_copy(scaled.at[i], matrices.at[i], sems.at[2 + i])
        copy.start()
        copies.append(copy)
    for i in range(3):
        maps[i] = late[base : base + head_size, i * head_size : (i + 1) * head_size]
    logit[...] = late[base : base + head_size, 128 : 128 + slices]
    copies += fetch((maps, logit), (maps_out, logit_out), sems)
    for i, weight in enumerate((fx_weight, x_weight)):
        total = total + row_total(late[i * width : (i + 1) * width], weight[...])
    gains[...] = jnp.concatenate([total, gain_row[...]], axis=0)
    copies.append(pltpu.make_async_copy(gains, gains_out, sems.at[4]))
    copies[-1].start()
    for copy in copies:
        copy.wait()


VMEM = pl.BlockSpec(memory_space=pltpu.VMEM)
SMEM = pl.BlockSpec(memory_space=pltpu.SMEM)


HBM = pl.BlockSpec(memory_space=pltpu.HBM)


def call(body, name, in_specs, out_specs, out_shape, args, flops, limit=SMALL, scratch=(),
         aliases=None):
    return pl.pallas_call(
        body,
        name=name,
        in_specs=in_specs,
        out_specs=out_specs,
        out_shape=out_shape,
        scratch_shapes=scratch,
        input_output_aliases=aliases or {},
        compiler_params=pltpu.CompilerParams(vmem_limit_bytes=limit),
        cost_estimate=pl.CostEstimate(flops=flops, bytes_accessed=1 << 20, transcendentals=0),
    )(*args)


def swap(value, moves, sizes):
    dp, point = sizes
    pairs = []
    for d in range(dp):
        for p in range(point):
            other_d, other_p = moves(d, p)
            pairs.append((d * point + p, other_d * point + other_p))
    return lax.ppermute(value, ("dp", "point"), pairs)


def bits(count):
    return [1 << i for i in range(count.bit_length() - 1)]


def tie(*values):
    return lax.optimization_barrier(values)


def flips(axes):
    def moves(d, p):
        axis, bit = axes[d & 1]
        return (d, p ^ bit) if axis else (d ^ bit, p)

    return moves


CORES = ((0, 1), (0, 1))


def paired(axes):
    turned = list(axes)
    for i in range(0, len(axes) - 1, 2):
        turned[i], turned[i + 1] = axes[i + 1], axes[i]
    return list(zip(axes, turned))


def direct_steps(masks, sizes):
    groups = [[mask] for mask in masks[:-2]]
    if len(masks) > 1:
        groups.append([masks[-2], masks[-1], masks[-2] | masks[-1]])
    elif masks:
        groups.append([masks[-1]])

    def step(group):
        def run(value):
            parts = [swap(value, flips(((1, mask),) * 2), sizes) for mask in group]
            if len(parts) == 1:
                return value + parts[0]
            return (value + parts[0]) + (parts[1] + parts[2])
        return run

    return [step(group) for group in groups]


def point_steps(sizes):
    return direct_steps(bits(sizes[1]), sizes)


def all_axes(sizes):
    return paired(
        [(1, 1)] + [(0, b) for b in bits(sizes[0])[1:]] + [(1, b) for b in bits(sizes[1])[1:]]
    )


def quarter_steps(sizes, direct):
    group = [lambda d, p: (d ^ 2, p), lambda d, p: (d, p ^ 1), lambda d, p: (d ^ 2, p ^ 1)]
    others = paired(([(0, b) for b in bits(sizes[0])[2:]] + [(1, b) for b in bits(sizes[1])[1:]])[::-1])

    def cores(value):
        received = swap(value[1], flips(CORES), sizes)
        part = (value[0].shape[0] // 4, value[0].shape[1])
        return call(
            add_quarter_kernel, "add_quarter", [VMEM] * 2, [VMEM] * 4,
            [jax.ShapeDtypeStruct(part, F32)] * 4, (value[0], received), received.size,
        )

    def scatter(value):
        parts = [swap(part, moves, sizes) for part, moves in zip(value[1:], group)]
        return (value[0] + parts[0]) + (parts[1] + parts[2])

    def add(axes):
        return lambda value: value + swap(value, flips(axes), sizes)

    def gather(value):
        return jnp.concatenate([value] + [swap(value, moves, sizes) for moves in group], axis=0)

    def last(value):
        return value, swap(value, flips(CORES), sizes)

    if direct:
        sums = [add(axes) for axes in paired([(0, b) for b in bits(sizes[0])[2:]])]
        sums += direct_steps(bits(sizes[1])[1:], sizes)
    else:
        sums = [add(axes) for axes in others]
    return [cores, scatter] + sums + [gather, last]


def all_steps(sizes, scatters, direct=False):
    if scatters == 0:
        return quarter_steps(sizes, direct)
    steps_axes = all_axes(sizes)

    def add_halve(i, mine, received):
        half = (mine.shape[0] // 2, mine.shape[1])
        return call(
            functools.partial(add_halve_kernel, steps_axes[i]), "add_halve", [VMEM] * 2,
            [VMEM] * 2, [jax.ShapeDtypeStruct(half, F32)] * 2, (mine, received), mine.size,
        )

    def cores(value):
        return add_halve(0, value[0], swap(value[1], flips(CORES), sizes))

    def scatter(i):
        def step(value):
            received = swap(value[1], flips(steps_axes[i]), sizes)
            if i + 1 < scatters:
                return add_halve(i + 1, value[0], received)
            return value[0] + received
        return step

    def add(i):
        return lambda value: value + swap(value, flips(steps_axes[i]), sizes)

    def gather(i):
        return lambda value: jnp.concatenate(
            [value, swap(value, flips(steps_axes[i]), sizes)], axis=0
        )

    def last(value):
        return value, swap(value, flips(CORES), sizes)

    return (
        [cores] + [scatter(i) for i in range(scatters)]
        + [add(i) for i in range(scatters, len(steps_axes))]
        + [gather(i) for i in reversed(range(scatters))] + [last]
    )


def shards(
    sizes,
    inputs, cotangent, gain_one, fx_weight, x_weight, slice_logit_weight, temper,
    slice_query_matrix, slice_key_matrix, slice_value_matrix, out_weight, gain_two,
    expand_weight, down_weight,
):
    points, width = inputs.shape[1:]
    head_size, slices = slice_logit_weight.shape
    heads = temper.shape[0]
    total = heads * slices
    gain_one, gain_two = gain_one[None], gain_two[None]
    factor = 1.0 / math.sqrt(points * sizes[0] * sizes[1])
    axes = all_axes(sizes)

    def shape(*dims, dtype=F32):
        return jax.ShapeDtypeStruct(dims, dtype)

    def pair(*dims):
        return [shape(*dims, dtype=BF16)] * 2

    dense = 6 * points * width * width
    pinned = [
        pltpu.with_memory_space_constraint(array, pltpu.HBM)
        for array in (inputs, gain_one, fx_weight, x_weight, slice_logit_weight, temper)
    ]
    front, front_wide, sums = call(
        front_kernel, "front", [HBM] * 6, [VMEM] * 3,
        [shape(2 * total + 8 * width, points, dtype=BF16), shape(width + 8 + heads, points),
         shape(total // 128 * head_size + 8, 128)],
        pinned,
        4 * dense,
        FRONT_LIMIT,
        [
            pltpu.VMEM(inputs.shape, F32), pltpu.VMEM((1, width), F32),
            pltpu.VMEM((width, width), F32), pltpu.VMEM((width, width), F32),
            pltpu.VMEM((head_size, slices), F32), pltpu.SMEM((heads,), F32),
            pltpu.SemaphoreType.DMA((6,)),
        ],
    )
    sums, cotangent, out_weight, gain_two, expand_weight, down_weight = tie(
        sums, cotangent, out_weight, gain_two, expand_weight, down_weight
    )
    columns, maps = call(
        ready_kernel, "ready", [VMEM] * 9, [VMEM] * 2,
        [shape(2 * width, points),
         shape(8 * width + (2 * GROUP + 8) * head_size, width, dtype=BF16)],
        (cotangent, out_weight, gain_two, expand_weight, down_weight, slice_query_matrix,
         slice_key_matrix, slice_value_matrix, slice_logit_weight),
        2 * dense,
    )
    for step in point_steps(sizes):
        sums = step(sums)
    out_sum, back, back_wide = call(
        functools.partial(back_kernel, head_size, slices), "back", [VMEM] * 5, [VMEM] * 3,
        [shape(head_size, total), shape(12 * width, points, dtype=BF16),
         shape(width + 5 * head_size + SIDE * slices + 8, points)],
        (sums, front, front_wide, columns, maps),
        6 * dense,
    )
    early_value = call(
        functools.partial(early_kernel, factor), "early", [VMEM] * 2, [VMEM] * 2,
        [shape(3 * width // 2, width)] * 2, (columns, back), 3 * dense,
        scratch=[pltpu.VMEM((3 * width, width), F32)],
    )
    behind = [early_value]
    for step in all_steps(sizes, EARLY):
        behind.append(step(behind[-1]))
    order = [None, 2]
    for i, step in enumerate(reversed(point_steps(sizes))):
        out_sum = step(out_sum)
        if i < len(order) and order[i] is not None:
            out_sum, _ = tie(out_sum, behind[order[i]])
    rows = -(-(2 * width + head_size) // 64) * 64
    mine, other, end = call(
        functools.partial(end_kernel, factor, factor / sizes[1], head_size, slices), "end",
        [VMEM] * 6, [VMEM] * 3,
        [shape(rows // 2, width)] * 2 + [shape(4 * width, points, dtype=BF16)],
        (out_sum, front, front_wide, maps, back, back_wide),
        8 * dense,
        scratch=[pltpu.VMEM((rows, width), F32)],
    )
    late, _ = tie((mine, other), behind[2])
    input_grad = call(
        rows_kernel, "rows", [VMEM] * 4, VMEM, shape(1, points, width),
        (front, front_wide, back_wide, end), 2 * dense,
    )
    steps = all_steps(sizes, LATE, True)
    for i, step in enumerate(steps):
        late = step(late)
        if i == 0:
            late, input_grad = tie(late, input_grad)
    matrices, gain_row = call(
        functools.partial(early_out_kernel, tuple(axes[:EARLY])), "early_out", [VMEM] * 4, [HBM, VMEM],
        [shape(5, width, width), shape(1, width)],
        (*behind[-1], gain_two, expand_weight),
        dense // 8,
        scratch=[pltpu.VMEM((3 * width, width), F32), pltpu.VMEM((width, width), F32),
                 pltpu.SemaphoreType.DMA((3,))],
    )
    matrices, map_grads, logit_grad, gains = call(
        functools.partial(late_out_kernel, tuple(axes[:LATE])), "late_out", [VMEM] * 6 + [HBM],
        [HBM] * 4,
        [shape(5, width, width), shape(3, head_size, head_size), shape(head_size, slices),
         shape(2, width)],
        (*late, gain_one, fx_weight, x_weight, gain_row, matrices),
        dense // 8,
        scratch=[pltpu.VMEM((rows, width), F32), pltpu.VMEM((2, width, width), F32),
                 pltpu.VMEM((3, head_size, head_size), F32), pltpu.VMEM((head_size, slices), F32),
                 pltpu.VMEM((2, width), F32), pltpu.SemaphoreType.DMA((5,))],
        aliases={6: 0},
    )
    return input_grad, matrices, map_grads, logit_grad, gains


def solution(mesh):
    sizes = (mesh.shape["dp"], mesh.shape["point"])
    placed = (P("dp", "point", None),) * 2 + (P(),) * 12
    return jax.shard_map(
        functools.partial(shards, sizes),
        mesh=mesh,
        in_specs=placed,
        out_specs=(P("dp", "point", None), P(), P(), P(), P()),
        check_vma=False,
    )
```
